256 devices in a mesh: pairs: 32 (over x, y, core), tm: 8 (over z).
Axes of the slice: x: 4, y: 4, z: 8, core: 2. Of those that a mesh axis runs over, the one named last changes fastest.
Arguments:
- spectra: bfloat16 [2, 8, 1024, 4096], P(None, 'tm', 'pairs')
- pair_blocks: int32 [32, 4, 2], replicated, may hold values from 0 to 31, as said below
- block_count: int32 [32], replicated, may hold values from 1 to 4, as said below
Outputs:
- stacked: float32 [128, 128, 2048], P('pairs', None, 'tm')
The draws below stay inside these ranges and needn't reach their ends.
Inputs may be any that keep to these rules, and one draw needn't show every extreme that they name: pair_blocks[p, k] names two different channel blocks; block j holds channels j * 128 to (j + 1) * 128 - 1. Owner p's pair blocks are its slots 0 to block_count[p] - 1; its later slots are empty and their rows of stacked are zero.
All inputs are finite; a program needn't handle non-finite values.
Results may differ from the reference program's by a relative error of at most 0.006.
Values may be sent and summed in bfloat16 or wider, within the bound.
No kernel may reach another device: no remote copies, remote signals or barrier semaphores. Data moves between devices by JAX's collectives and lax.ppermute only.
A program may use at most 128 MiB of HBM per device.

```python
import math
import jax
import jax.numpy as jnp
from jax import lax

C = 4096
CB = 128
NF = 1024
FIRST_BIN = 16
FFT_LEN = 8192
LAGS = 2048
SMOOTH = 32
MAXB = 4
NBLK = 32
HOURS = 8
OWNERS = 32


def draw_spectra(key, part):
    key = jax.random.fold_in(key, 11)
    key_noise, key_common, key_channel, key_colour = jax.random.split(key, 4)
    full_shape = (2, HOURS, NF, C)
    noise_part = jax.random.normal(key_noise, full_shape)
    common_part = jax.random.normal(key_common, (2, 1, NF, C))
    channel_scale = jnp.exp(jax.random.uniform(key_channel, (C,)) * math.log(10.0))
    band_colour = jnp.exp(jax.random.uniform(key_colour, (NF,), minval=-0.7, maxval=0.7))
    values = (noise_part + common_part) * band_colour[:, None] * channel_scale
    return values.astype(jnp.bfloat16)


def draw_pair_blocks(key, part):
    key = jax.random.fold_in(key, 12)
    key_first, key_step = jax.random.split(key, 2)
    left_ids = jax.random.randint(key_first, (OWNERS, MAXB), 0, NBLK)
    step_ids = jax.random.randint(key_step, (OWNERS, MAXB), 1, NBLK)
    right_ids = (left_ids + step_ids) % NBLK
    left_ids = left_ids.at[0, 0].set(NBLK - 1)
    right_ids = right_ids.at[0, 0].set(0)
    return jnp.stack([left_ids, right_ids], axis=-1).astype(jnp.int32)


def draw_block_count(key, part):
    key = jax.random.fold_in(key, 13)
    key_one, key_two, key_busy, key_light = jax.random.split(key, 4)
    first_draw = jax.random.randint(key_one, (OWNERS,), 1, MAXB + 1)
    second_draw = jax.random.randint(key_two, (OWNERS,), 1, MAXB + 1)
    counts = jnp.maximum(1, first_draw * second_draw // MAXB)
    busy_owner = jax.random.randint(key_busy, (), 0, OWNERS)
    light_owner = (busy_owner + 1 + jax.random.randint(key_light, (), 0, OWNERS - 1)) % OWNERS
    counts = counts.at[busy_owner].set(MAXB).at[light_owner].set(1)
    return counts.astype(jnp.int32)


def setup_inputs(seed: int = 0) -> dict:
    streams_of = jax.random.split(jax.random.key(seed), 4)
    spectra = draw_spectra(jax.random.fold_in(streams_of[3], 71), 0)
    pair_blocks = draw_pair_blocks(jax.random.fold_in(streams_of[3], 71), 0)
    block_count = draw_block_count(jax.random.fold_in(streams_of[3], 71), 0)
    return dict(spectra=spectra, pair_blocks=pair_blocks, block_count=block_count)


amp_floor = 0.2

def whiten(raw_spectra, pad_band):
    components = raw_spectra.astype(jnp.float32)
    magnitude = jnp.sqrt(components[0] * components[0] + components[1] * components[1])
    rank_total = magnitude.ndim
    window = (1, 2 * SMOOTH + 1) + (1,) * (rank_total - 2)
    if pad_band:
        padding = ((0, 0), (SMOOTH, SMOOTH)) + ((0, 0),) * (rank_total - 2)
        inner_part = components
    else:
        padding = ((0, 0),) * rank_total
        inner_part = components[:, :, SMOOTH:components.shape[2] - SMOOTH]
    window_sum = lax.reduce_window(magnitude, jnp.zeros((), magnitude.dtype), lax.add, window, (1,) * rank_total, padding)
    smoothed = window_sum / (2 * SMOOTH + 1)
    return (inner_part / (smoothed[None] + 1e-05)).astype(jnp.bfloat16)

def lag_table(offset, span_width, bin_total):
    bin_index = lax.iota(jnp.int32, bin_total)[:, None] + FIRST_BIN
    lag_index = lax.iota(jnp.int32, span_width)[None, :] + offset + (FFT_LEN - LAGS // 2)
    phase_step = bin_index * lag_index % FFT_LEN
    phase_angle = phase_step.astype(jnp.float32) * (2.0 * math.pi / FFT_LEN)
    scale_factor = 1.0 / math.sqrt(bin_total)
    cosine = jnp.cos(phase_angle) * scale_factor
    sine_part = jnp.sin(phase_angle) * scale_factor
    real_rows = jnp.stack([cosine, sine_part], axis=1)
    imag_rows = jnp.stack([-sine_part, cosine], axis=1)
    return jnp.stack([real_rows, imag_rows], axis=0).astype(jnp.bfloat16)

def phase_stack(lagged):
    correlation = lagged[:, :, :, 0]
    quadrature = lagged[:, :, :, 1]
    linear = lax.optimization_barrier(jnp.mean(correlation, axis=0))
    magnitude = jnp.sqrt(correlation * correlation + quadrature * quadrature)
    inverse = 1.0 / jnp.maximum(magnitude, amp_floor)
    mean_real = lax.optimization_barrier(jnp.mean(correlation * inverse, axis=0))
    mean_imag = lax.optimization_barrier(jnp.mean(quadrature * inverse, axis=0))
    return linear * (mean_real * mean_real + mean_imag * mean_imag)

def reference(spectra, pair_blocks, block_count):
    whitened = whiten(spectra, True)
    blocked = whitened.reshape(2, HOURS, NF, C // CB, CB)
    inverse_table = lag_table(0, LAGS, NF).astype(jnp.float32)

    def one_owner(owner_index):
        own_blocks = pair_blocks[owner_index].reshape(2 * MAXB)
        chosen = jnp.take(blocked, own_blocks, axis=3).astype(jnp.float32)
        left_block = chosen[:, :, :, 0::2]
        right_block = chosen[:, :, :, 1::2]
        cross_real = left_block[0] * right_block[0] + left_block[1] * right_block[1]
        cross_imag = left_block[1] * right_block[0] - left_block[0] * right_block[1]
        cross_spectra = lax.optimization_barrier(jnp.stack([cross_real, cross_imag]).astype(jnp.bfloat16))
        cross_spectra = cross_spectra.astype(jnp.float32)
        lagged = jnp.einsum('chfkb,cfgl->hkbgl', cross_spectra, inverse_table)
        live_mask = (lax.iota(jnp.int32, MAXB) < block_count[owner_index]).astype(jnp.float32)
        lagged = lagged * live_mask[None, :, None, None, None]
        lagged = lax.optimization_barrier(lagged.astype(jnp.bfloat16)).astype(jnp.float32)
        return phase_stack(lagged)
    stacked = lax.map(one_owner, lax.iota(jnp.int32, OWNERS))
    return stacked.reshape(OWNERS * MAXB, CB, LAGS)
```

```python
import functools
import math

import jax
import jax.numpy as jnp
import ml_dtypes
import numpy as np
from jax import lax
from jax.experimental import pallas as pl
from jax.experimental.pallas import tpu as pltpu
from jax.sharding import PartitionSpec as P

C = 4096
CB = 128
NF = 1024
FIRST_BIN = 16
FFT_LEN = 8192
LAGS = 2048
SMOOTH = 32
MAXB = 4
HOURS = 8
OWNERS = 32
amp_floor = 0.2

CHIPS = OWNERS // 2
BINS = NF // OWNERS
CHIP_BINS = 2 * BINS
LAG_PART = LAGS // HOURS
RANK_CHIP = 28
RANK_PART = 48
ROWS_CHIP = 2 * RANK_CHIP
ROWS_PART = 2 * RANK_PART
STEP = 2.0 * math.pi / FFT_LEN


def slepian(points, half_width, count):
    n = np.arange(points, dtype=np.float64)
    tri = np.diag(((points - 1) / 2.0 - n) ** 2 * math.cos(2.0 * math.pi * half_width))
    off = n[1:] * (points - n[1:]) / 2.0
    tri = tri + np.diag(off, 1) + np.diag(off, -1)
    vectors = np.linalg.eigh(tri)[1][:, ::-1][:, :count]
    return vectors * np.where(vectors[points // 2] < 0, -1.0, 1.0)


def split_rounded(table):
    high = table.astype(ml_dtypes.bfloat16)
    low = (table - high.astype(np.float64)).astype(ml_dtypes.bfloat16)
    return high, low


def real_form(table):
    return np.block([[table.real, -table.imag], [table.imag, table.real]])


@functools.cache
def tables():
    chip_basis = slepian(CHIP_BINS, LAGS / 2 / FFT_LEN, RANK_CHIP)
    part_basis = slepian(NF, LAG_PART / 2 / FFT_LEN, RANK_PART)
    bins = np.arange(NF) - (NF - 1) / 2.0
    lags = np.arange(LAG_PART) - (LAG_PART - 1) / 2.0
    mid_bin = FIRST_BIN + (NF - 1) / 2.0
    compress = np.kron(np.eye(2), chip_basis.T)
    parts = []
    for part in range(HOURS):
        mid_lag = LAG_PART * part - LAGS // 2 + (LAG_PART - 1) / 2.0
        turned = np.exp(1j * STEP * (bins + mid_bin) * mid_lag)[:, None] * part_basis
        turned = turned.reshape(CHIPS, CHIP_BINS, RANK_PART)
        blocks = [real_form((chip_basis.T @ turned[chip]).T) for chip in range(CHIPS)]
        parts.append(np.concatenate(blocks, axis=1))
    combine = np.concatenate(parts, axis=0)
    waves = np.exp(1j * STEP * np.outer(lags, bins)) @ part_basis
    waves = waves * np.exp(1j * STEP * mid_bin * lags)[:, None] / math.sqrt(NF)
    expand = real_form(waves)
    row = np.arange(CHIP_BINS)[:, None] + SMOOTH
    column = np.arange(CHIP_BINS + 2 * SMOOTH)[None, :]
    window = (np.abs(row - column) <= SMOOTH).astype(ml_dtypes.bfloat16)
    compress = np.concatenate(split_rounded(compress), axis=1)
    expand = np.concatenate(split_rounded(expand), axis=1)
    return window, compress, split_rounded(combine), expand


def magnitude_of(real, imag):
    return jnp.sqrt(real * real + imag * imag)


def cross_kernel(
    blocks, core_ref, own, twin, near, far, window, compress, out, magnitudes, white, columns
):
    core = core_ref[0]
    own_row = pl.multiple_of(core * BINS, BINS)
    twin_row = pl.multiple_of((1 - core) * BINS, BINS)
    near_row = pl.multiple_of(core * (CHIP_BINS + SMOOTH), BINS)
    far_row = pl.multiple_of((1 - core) * (CHIP_BINS + SMOOTH), BINS)
    chunk = 512

    def whiten(step, carry):
        lanes = pl.ds(pl.multiple_of(step * chunk, chunk), chunk)
        magnitudes[pl.ds(near_row, SMOOTH), :] = near[:, lanes]
        magnitudes[pl.ds(far_row, SMOOTH), :] = far[:, lanes]
        parts = []
        for source, first in ((own, own_row), (twin, twin_row)):
            real = source[0, :, lanes].astype(jnp.float32)
            imag = source[1, :, lanes].astype(jnp.float32)
            size = magnitude_of(real, imag).astype(jnp.bfloat16)
            magnitudes[pl.ds(pl.multiple_of(first + SMOOTH, BINS), BINS), :] = size
            parts.append((real, imag, first))
        sums = jnp.dot(window[...], magnitudes[...], preferred_element_type=jnp.float32)
        smoothed = sums * (1.0 / (2 * SMOOTH + 1))
        columns[:, :chunk] = 1.0 / (smoothed + 1e-05)
        for real, imag, first in parts:
            inverse = columns[pl.ds(first, BINS), :chunk]
            white[0, pl.ds(first, BINS), lanes] = (real * inverse).astype(jnp.bfloat16)
            white[1, pl.ds(first, BINS), lanes] = (imag * inverse).astype(jnp.bfloat16)
        return carry

    lax.fori_loop(0, C // chunk, whiten, 0)

    def one_owner(chip, carry):
        base = (2 * chip + core) * (2 * MAXB)
        crossed = []
        for slot in range(MAXB):
            left = pl.ds(pl.multiple_of(blocks[base + 2 * slot] * CB, CB), CB)
            right = pl.ds(pl.multiple_of(blocks[base + 2 * slot + 1] * CB, CB), CB)
            left_re = white[0, :, left].astype(jnp.float32)
            left_im = white[1, :, left].astype(jnp.float32)
            right_re = white[0, :, right].astype(jnp.float32)
            right_im = white[1, :, right].astype(jnp.float32)
            real = left_re * right_re + left_im * right_im
            imag = left_im * right_re - left_re * right_im
            crossed.append(jnp.concatenate([real, imag], axis=0).astype(jnp.bfloat16))
        cross = jnp.concatenate(crossed, axis=1)
        cross = jnp.concatenate([cross, cross], axis=0)
        packed = jnp.dot(compress[...], cross, preferred_element_type=jnp.float32)
        out[chip] = packed.astype(jnp.bfloat16)
        return carry

    lax.fori_loop(0, CHIPS, one_owner, 0)


def combine_kernel(high, low, packed, out):
    value = packed[...]
    total = jnp.dot(high[...], value, preferred_element_type=jnp.float32)
    total = total + jnp.dot(low[...], value, preferred_element_type=jnp.float32)
    out[...] = total.astype(jnp.bfloat16)


def stack_kernel(live_ref, expand, parts, out):
    step = pl.program_id(0)
    linear = mean_real = mean_imag = None
    for hour in range(HOURS):
        part = parts[hour]
        part = jnp.concatenate([part, part], axis=0)
        lagged = jnp.dot(expand[...], part, preferred_element_type=jnp.float32)
        correlation = lagged[:LAG_PART]
        quadrature = lagged[LAG_PART:]
        power = correlation * correlation + quadrature * quadrature
        inverse = jnp.minimum(lax.rsqrt(power), 1.0 / amp_floor)
        unit_real = correlation * inverse
        unit_imag = quadrature * inverse
        if hour == 0:
            linear, mean_real, mean_imag = correlation, unit_real, unit_imag
        else:
            linear = linear + correlation
            mean_real = mean_real + unit_real
            mean_imag = mean_imag + unit_imag
    stacked = linear * (mean_real * mean_real + mean_imag * mean_imag) * (1.0 / HOURS**3)
    turned = stacked.T
    slots = out.shape[0]
    for slot in range(slots):
        live = step * slots + slot < live_ref[0]
        piece = turned[slot * CB : (slot + 1) * CB]
        out[slot] = jnp.where(live, piece, jnp.zeros_like(piece))


def on_device(spectra, pair_blocks, block_count):
    owner = lax.axis_index("pairs")
    core = owner % 2
    window, compress, (high, low), expand = tables()
    spectra = spectra[:, 0]
    wide = spectra.astype(jnp.float32)
    magnitude = magnitude_of(wide[0], wide[1]).astype(jnp.bfloat16)
    twin = lax.ppermute(spectra, "pairs", [(i, i ^ 1) for i in range(OWNERS)])
    last = OWNERS - 1
    near_pairs = [(i, i + 1) for i in range(1, last, 2)] + [(i, i - 1) for i in range(2, last, 2)]
    far_pairs = [(i, i + 2) for i in range(1, last - 1, 2)] + [(i, i - 2) for i in range(2, last, 2)]
    near = lax.ppermute(magnitude, "pairs", near_pairs)
    far = lax.ppermute(magnitude, "pairs", far_pairs)
    vmem = pl.BlockSpec(memory_space=pltpu.VMEM)
    smem = pl.BlockSpec(memory_space=pltpu.SMEM)
    packed = pl.pallas_call(
        cross_kernel,
        out_shape=jax.ShapeDtypeStruct((CHIPS, ROWS_CHIP, MAXB * CB), jnp.bfloat16),
        in_specs=[smem, smem] + [vmem] * 6,
        out_specs=vmem,
        scratch_shapes=[
            pltpu.VMEM((CHIP_BINS + 2 * SMOOTH, 512), jnp.bfloat16),
            pltpu.VMEM((2, CHIP_BINS, C), jnp.bfloat16),
            pltpu.VMEM((CHIP_BINS, 512), jnp.float32),
        ],
        compiler_params=pltpu.CompilerParams(vmem_limit_bytes=32 * 2**20),
        name="cross",
    )(pair_blocks.reshape(-1), core[None], spectra, twin, near, far, window, compress)
    groups = [list(range(0, OWNERS, 2)), list(range(1, OWNERS, 2))]
    packed = lax.all_to_all(packed, "pairs", 0, 0, axis_index_groups=groups, tiled=True)
    packed = packed.reshape(CHIPS * ROWS_CHIP, MAXB * CB)
    parts = pl.pallas_call(
        combine_kernel,
        out_shape=jax.ShapeDtypeStruct((HOURS * ROWS_PART, MAXB * CB), jnp.bfloat16),
        in_specs=[vmem] * 3,
        out_specs=vmem,
        compiler_params=pltpu.CompilerParams(vmem_limit_bytes=32 * 2**20),
        name="combine",
    )(high, low, packed)
    parts = parts.reshape(HOURS, ROWS_PART, MAXB * CB)
    parts = lax.all_to_all(parts, "tm", 0, 0, tiled=True)
    live = lax.dynamic_index_in_dim(block_count, owner, 0, keepdims=True)
    slots = 2
    return pl.pallas_call(
        stack_kernel,
        grid=(MAXB // slots,),
        out_shape=jax.ShapeDtypeStruct((MAXB, CB, LAG_PART), jnp.float32),
        in_specs=[
            smem,
            pl.BlockSpec((2 * LAG_PART, 2 * ROWS_PART), lambda i: (0, 0)),
            pl.BlockSpec((HOURS, ROWS_PART, slots * CB), lambda i: (0, 0, i)),
        ],
        out_specs=pl.BlockSpec((slots, CB, LAG_PART), lambda i: (i, 0, 0)),
        compiler_params=pltpu.CompilerParams(vmem_limit_bytes=32 * 2**20),
        name="stack",
    )(live, expand, parts)


def solution(mesh):
    return jax.shard_map(
        on_device,
        mesh=mesh,
        in_specs=(P(None, "tm", "pairs", None), P(), P()),
        out_specs=P("pairs", None, "tm"),
        check_vma=False,
    )
```

```python
import functools
import math

import jax
import jax.numpy as jnp
import ml_dtypes
import numpy as np
from jax import lax
from jax.experimental import pallas as pl
from jax.experimental.pallas import tpu as pltpu
from jax.sharding import PartitionSpec as P

C = 4096
CB = 128
NF = 1024
FIRST_BIN = 16
FFT_LEN = 8192
LAGS = 2048
SMOOTH = 32
MAXB = 4
HOURS = 8
OWNERS = 32
amp_floor = 0.2

CHIPS = OWNERS // 2
BINS = NF // OWNERS
CHIP_BINS = 2 * BINS
LAG_PART = LAGS // HOURS
RANK_CHIP = 28
RANK_PART = 48
ROWS_CHIP = 2 * RANK_CHIP
ROWS_PART = 2 * RANK_PART
STEP = 2.0 * math.pi / FFT_LEN


def slepian(points, half_width, count):
    n = np.arange(points, dtype=np.float64)
    tri = np.diag(((points - 1) / 2.0 - n) ** 2 * math.cos(2.0 * math.pi * half_width))
    off = n[1:] * (points - n[1:]) / 2.0
    tri = tri + np.diag(off, 1) + np.diag(off, -1)
    vectors = np.linalg.eigh(tri)[1][:, ::-1][:, :count]
    return vectors * np.where(vectors[points // 2] < 0, -1.0, 1.0)


def split_rounded(table):
    high = table.astype(ml_dtypes.bfloat16)
    low = (table - high.astype(np.float64)).astype(ml_dtypes.bfloat16)
    return high, low


def real_form(table):
    return np.block([[table.real, -table.imag], [table.imag, table.real]])


@functools.cache
def tables():
    chip_basis = slepian(CHIP_BINS, LAGS / 2 / FFT_LEN, RANK_CHIP)
    part_basis = slepian(NF, LAG_PART / 2 / FFT_LEN, RANK_PART)
    bins = np.arange(NF) - (NF - 1) / 2.0
    lags = np.arange(LAG_PART) - (LAG_PART - 1) / 2.0
    mid_bin = FIRST_BIN + (NF - 1) / 2.0
    compress = np.kron(np.eye(2), chip_basis.T)
    parts = []
    for part in range(HOURS):
        mid_lag = LAG_PART * part - LAGS // 2 + (LAG_PART - 1) / 2.0
        turned = np.exp(1j * STEP * (bins + mid_bin) * mid_lag)[:, None] * part_basis
        turned = turned.reshape(CHIPS, CHIP_BINS, RANK_PART)
        blocks = [real_form((chip_basis.T @ turned[chip]).T) for chip in range(CHIPS)]
        parts.append(np.concatenate(blocks, axis=1))
    combine = np.concatenate(parts, axis=0)
    waves = np.exp(1j * STEP * np.outer(lags, bins)) @ part_basis
    waves = waves * np.exp(1j * STEP * mid_bin * lags)[:, None] / math.sqrt(NF)
    expand = real_form(waves)
    row = np.arange(CHIP_BINS)[:, None] + SMOOTH
    column = np.arange(CHIP_BINS + 2 * SMOOTH)[None, :]
    window = (np.abs(row - column) <= SMOOTH).astype(ml_dtypes.bfloat16)
    compress = np.concatenate(split_rounded(compress), axis=1)
    expand = np.ascontiguousarray(np.concatenate(split_rounded(expand), axis=1).T)
    return window, compress, split_rounded(combine), expand


def magnitude_of(real, imag):
    return jnp.sqrt(real * real + imag * imag)


def cross_kernel(
    blocks, core_ref, own, twin, near, far, window, compress, out, magnitudes, white, columns
):
    core = core_ref[0]
    own_row = pl.multiple_of(core * BINS, BINS)
    twin_row = pl.multiple_of((1 - core) * BINS, BINS)
    near_row = pl.multiple_of(core * (CHIP_BINS + SMOOTH), BINS)
    far_row = pl.multiple_of((1 - core) * (CHIP_BINS + SMOOTH), BINS)
    chunk = 512

    def whiten(step, carry):
        lanes = pl.ds(pl.multiple_of(step * chunk, chunk), chunk)
        magnitudes[pl.ds(near_row, SMOOTH), :] = near[:, lanes]
        magnitudes[pl.ds(far_row, SMOOTH), :] = far[:, lanes]
        parts = []
        for source, first in ((own, own_row), (twin, twin_row)):
            real = source[0, :, lanes].astype(jnp.float32)
            imag = source[1, :, lanes].astype(jnp.float32)
            size = magnitude_of(real, imag).astype(jnp.bfloat16)
            magnitudes[pl.ds(pl.multiple_of(first + SMOOTH, BINS), BINS), :] = size
            parts.append((real, imag, first))
        sums = jnp.dot(window[...], magnitudes[...], preferred_element_type=jnp.float32)
        smoothed = sums * (1.0 / (2 * SMOOTH + 1))
        columns[:, :chunk] = 1.0 / (smoothed + 1e-05)
        for real, imag, first in parts:
            inverse = columns[pl.ds(first, BINS), :chunk]
            white[0, pl.ds(first, BINS), lanes] = (real * inverse).astype(jnp.bfloat16)
            white[1, pl.ds(first, BINS), lanes] = (imag * inverse).astype(jnp.bfloat16)
        return carry

    lax.fori_loop(0, C // chunk, whiten, 0, unroll=True)

    def one_owner(chip, carry):
        base = (2 * chip + core) * (2 * MAXB)
        crossed = []
        for slot in range(MAXB):
            left = pl.ds(pl.multiple_of(blocks[base + 2 * slot] * CB, CB), CB)
            right = pl.ds(pl.multiple_of(blocks[base + 2 * slot + 1] * CB, CB), CB)
            left_re = white[0, :, left].astype(jnp.float32)
            left_im = white[1, :, left].astype(jnp.float32)
            right_re = white[0, :, right].astype(jnp.float32)
            right_im = white[1, :, right].astype(jnp.float32)
            real = left_re * right_re + left_im * right_im
            imag = left_im * right_re - left_re * right_im
            crossed.append(jnp.concatenate([real, imag], axis=0).astype(jnp.bfloat16))
        cross = jnp.concatenate(crossed, axis=1)
        cross = jnp.concatenate([cross, cross], axis=0)
        packed = jnp.dot(compress[...], cross, preferred_element_type=jnp.float32)
        out[chip] = packed.astype(jnp.bfloat16)
        return carry

    lax.fori_loop(0, CHIPS, one_owner, 0, unroll=True)


def combine_kernel(high, low, packed, out):
    value = packed[...]
    total = jnp.dot(high[...], value, preferred_element_type=jnp.float32)
    total = total + jnp.dot(low[...], value, preferred_element_type=jnp.float32)
    out[...] = total.astype(jnp.bfloat16)


def stack_kernel(live_ref, expand, parts, out):
    step = pl.program_id(0)
    for slot in range(out.shape[0]):
        lanes = slice(slot * CB, (slot + 1) * CB)
        linear = mean_real = mean_imag = None
        for hour in range(HOURS):
            part = parts[hour, :, lanes]
            part = jnp.concatenate([part, part], axis=0)
            lagged = lax.dot_general(
                part, expand[...], (((0,), (0,)), ((), ())), preferred_element_type=jnp.float32
            )
            correlation = lagged[:, :LAG_PART]
            quadrature = lagged[:, LAG_PART:]
            power = correlation * correlation + quadrature * quadrature
            inverse = jnp.minimum(lax.rsqrt(power), 1.0 / amp_floor)
            unit_real = correlation * inverse
            unit_imag = quadrature * inverse
            if hour == 0:
                linear, mean_real, mean_imag = correlation, unit_real, unit_imag
            else:
                linear = linear + correlation
                mean_real = mean_real + unit_real
                mean_imag = mean_imag + unit_imag
        stacked = linear * (mean_real * mean_real + mean_imag * mean_imag) * (1.0 / HOURS**3)
        live = step * out.shape[0] + slot < live_ref[0]
        out[slot] = jnp.where(live, stacked, jnp.zeros_like(stacked))


def on_device(spectra, pair_blocks, block_count):
    owner = lax.axis_index("pairs")
    core = owner % 2
    window, compress, (high, low), expand = tables()
    spectra = spectra[:, 0]
    wide = spectra.astype(jnp.float32)
    magnitude = magnitude_of(wide[0], wide[1]).astype(jnp.bfloat16)
    twins = [(i, i ^ 1) for i in range(OWNERS)]
    twin = lax.ppermute(spectra, "pairs", twins)
    last = OWNERS - 1
    near_pairs = [(i, i + 1) for i in range(1, last, 2)] + [(i, i - 1) for i in range(2, last, 2)]
    near = lax.ppermute(magnitude, "pairs", near_pairs)
    far = lax.ppermute(near, "pairs", twins)
    vmem = pl.BlockSpec(memory_space=pltpu.VMEM)
    smem = pl.BlockSpec(memory_space=pltpu.SMEM)
    packed = pl.pallas_call(
        cross_kernel,
        out_shape=jax.ShapeDtypeStruct((CHIPS, ROWS_CHIP, MAXB * CB), jnp.bfloat16),
        in_specs=[smem, smem] + [vmem] * 6,
        out_specs=vmem,
        scratch_shapes=[
            pltpu.VMEM((CHIP_BINS + 2 * SMOOTH, 512), jnp.bfloat16),
            pltpu.VMEM((2, CHIP_BINS, C), jnp.bfloat16),
            pltpu.VMEM((CHIP_BINS, 512), jnp.float32),
        ],
        compiler_params=pltpu.CompilerParams(vmem_limit_bytes=32 * 2**20),
        name="cross",
    )(pair_blocks.reshape(-1), core[None], spectra, twin, near, far, window, compress)
    groups = [list(range(0, OWNERS, 2)), list(range(1, OWNERS, 2))]
    packed = lax.all_to_all(packed, "pairs", 0, 0, axis_index_groups=groups, tiled=True)
    packed = packed.reshape(CHIPS * ROWS_CHIP, MAXB * CB)
    parts = pl.pallas_call(
        combine_kernel,
        out_shape=jax.ShapeDtypeStruct((HOURS * ROWS_PART, MAXB * CB), jnp.bfloat16),
        in_specs=[vmem] * 3,
        out_specs=vmem,
        compiler_params=pltpu.CompilerParams(vmem_limit_bytes=32 * 2**20),
        name="combine",
    )(high, low, packed)
    parts = parts.reshape(HOURS, ROWS_PART, MAXB * CB)
    parts = lax.all_to_all(parts, "tm", 0, 0, tiled=True)
    live = lax.dynamic_index_in_dim(block_count, owner, 0, keepdims=True)
    slots = 2
    return pl.pallas_call(
        stack_kernel,
        grid=(MAXB // slots,),
        out_shape=jax.ShapeDtypeStruct((MAXB, CB, LAG_PART), jnp.float32),
        in_specs=[
            smem,
            pl.BlockSpec((2 * ROWS_PART, 2 * LAG_PART), lambda i: (0, 0)),
            pl.BlockSpec((HOURS, ROWS_PART, slots * CB), lambda i: (0, 0, i)),
        ],
        out_specs=pl.BlockSpec((slots, CB, LAG_PART), lambda i: (i, 0, 0)),
        compiler_params=pltpu.CompilerParams(vmem_limit_bytes=32 * 2**20),
        name="stack",
    )(live, expand, parts)


def solution(mesh):
    return jax.shard_map(
        on_device,
        mesh=mesh,
        in_specs=(P(None, "tm", "pairs", None), P(), P()),
        out_specs=P("pairs", None, "tm"),
        check_vma=False,
    )
```

```python
import functools
import math

import jax
import jax.numpy as jnp
import ml_dtypes
import numpy as np
from jax import lax
from jax.experimental import pallas as pl
from jax.experimental.pallas import tpu as pltpu
from jax.sharding import PartitionSpec as P

C = 4096
CB = 128
NF = 1024
FIRST_BIN = 16
FFT_LEN = 8192
LAGS = 2048
SMOOTH = 32
MAXB = 4
HOURS = 8
OWNERS = 32
amp_floor = 0.2

CHIPS = OWNERS // 2
BINS = NF // OWNERS
CHIP_BINS = 2 * BINS
LAG_PART = LAGS // HOURS
RANK_CHIP = 28
RANK_PART = 48
ROWS_CHIP = 2 * RANK_CHIP
ROWS_PART = 2 * RANK_PART
STEP = 2.0 * math.pi / FFT_LEN


def slepian(points, half_width, count):
    n = np.arange(points, dtype=np.float64)
    tri = np.diag(((points - 1) / 2.0 - n) ** 2 * math.cos(2.0 * math.pi * half_width))
    off = n[1:] * (points - n[1:]) / 2.0
    tri = tri + np.diag(off, 1) + np.diag(off, -1)
    vectors = np.linalg.eigh(tri)[1][:, ::-1][:, :count]
    return vectors * np.where(vectors[points // 2] < 0, -1.0, 1.0)


def split_rounded(table):
    high = table.astype(ml_dtypes.bfloat16)
    low = (table - high.astype(np.float64)).astype(ml_dtypes.bfloat16)
    return high, low


def real_form(table):
    return np.block([[table.real, -table.imag], [table.imag, table.real]])


@functools.cache
def tables():
    chip_basis = slepian(CHIP_BINS, LAGS / 2 / FFT_LEN, RANK_CHIP)
    part_basis = slepian(NF, LAG_PART / 2 / FFT_LEN, RANK_PART)
    bins = np.arange(NF) - (NF - 1) / 2.0
    lags = np.arange(LAG_PART) - LAG_PART // 2
    mid_bin = FIRST_BIN + (NF - 1) / 2.0
    compress = np.kron(np.eye(2), chip_basis.T)
    parts = []
    for part in range(HOURS // 2):
        mid_lag = LAG_PART * part - (LAGS - LAG_PART) // 2
        turned = np.exp(1j * STEP * (bins + mid_bin) * mid_lag)[:, None] * part_basis
        turned = turned.reshape(CHIPS, CHIP_BINS, RANK_PART)
        blocks = [(chip_basis.T @ turned[chip]).T for chip in range(CHIPS)]
        parts.append(np.concatenate(blocks, axis=1))
    combine = np.concatenate(parts, axis=0)
    combine = np.concatenate([combine.real, combine.imag], axis=0)
    waves = np.exp(1j * STEP * np.outer(lags, bins)) @ part_basis
    waves = waves * np.exp(1j * STEP * mid_bin * lags)[:, None] / math.sqrt(NF)
    expand = real_form(waves)
    row = np.arange(BINS)[:, None] + SMOOTH
    column = np.arange(BINS + 2 * SMOOTH)[None, :]
    window = (np.abs(row - column) <= SMOOTH).astype(ml_dtypes.bfloat16)
    turned = [window[:, -SMOOTH:], window[:, SMOOTH:-SMOOTH], window[:, :SMOOTH]]
    window = np.stack([window, np.concatenate(turned, axis=1)])
    halves = np.split(compress, 2 * CHIP_BINS // BINS, axis=1)
    by_core = []
    for core in range(2):
        own, twin = core, 1 - core
        ordered = [halves[own], halves[2 + own], halves[twin], halves[2 + twin]]
        by_core.append(np.concatenate(split_rounded(np.concatenate(ordered, axis=1)), axis=1))
    compress = np.stack(by_core)
    expand = np.ascontiguousarray(np.concatenate(split_rounded(expand), axis=1).T)
    return window, compress, split_rounded(combine), expand


def magnitude_of(real, imag):
    real, imag = real.astype(jnp.float32), imag.astype(jnp.float32)
    return jnp.sqrt(real * real + imag * imag).astype(jnp.bfloat16)


def whiten(core, window, source, first, centre, second, white):
    chunk = 512
    weights = window[core]
    for start in range(0, C, chunk):
        lanes = slice(start, start + chunk)
        sizes = jnp.concatenate([first[:, lanes], centre[:, lanes], second[:, lanes]], axis=0)
        sums = jnp.dot(weights, sizes, preferred_element_type=jnp.float32)
        inverse = 1.0 / (sums * (1.0 / (2 * SMOOTH + 1)) + 1e-05)
        for part in range(2):
            value = source[part, :, lanes].astype(jnp.float32) * inverse
            white[part, :, lanes] = value.astype(jnp.bfloat16)


def cross_of(blocks, base, white):
    crossed = []
    for slot in range(MAXB):
        left = pl.ds(pl.multiple_of(blocks[base + 2 * slot] * CB, CB), CB)
        right = pl.ds(pl.multiple_of(blocks[base + 2 * slot + 1] * CB, CB), CB)
        left_re = white[0, :, left].astype(jnp.float32)
        left_im = white[1, :, left].astype(jnp.float32)
        right_re = white[0, :, right].astype(jnp.float32)
        right_im = white[1, :, right].astype(jnp.float32)
        real = left_re * right_re + left_im * right_im
        imag = left_im * right_re - left_re * right_im
        crossed.append(jnp.concatenate([real, imag], axis=0).astype(jnp.bfloat16))
    return jnp.concatenate(crossed, axis=1)


def own_kernel(blocks, core_ref, window, own, near, own_size, twin_size, out, white):
    core = core_ref[0]
    whiten(core, window, own, near, own_size, twin_size, white)
    for chip in range(CHIPS):
        out[chip] = cross_of(blocks, (2 * chip + core) * (2 * MAXB), white)


def twin_kernel(
    blocks, core_ref, window, compress, twin, own_size, twin_size, far, own_cross, out, white
):
    core = core_ref[0]
    whiten(core, window, twin, own_size, twin_size, far, white)
    weights = compress[core]
    for chip in range(CHIPS):
        twin_cross = cross_of(blocks, (2 * chip + core) * (2 * MAXB), white)
        cross = jnp.concatenate([own_cross[chip], twin_cross] * 2, axis=0)
        packed = jnp.dot(weights, cross, preferred_element_type=jnp.float32)
        out[chip] = packed.astype(jnp.bfloat16)


def combine_kernel(high, low, packed, out):
    real = jnp.concatenate([packed[chip, :RANK_CHIP] for chip in range(CHIPS)], axis=0)
    imag = jnp.concatenate([packed[chip, RANK_CHIP:] for chip in range(CHIPS)], axis=0)
    value = jnp.concatenate([real, imag], axis=1)
    total = jnp.dot(high[...], value, preferred_element_type=jnp.float32)
    total = total + jnp.dot(low[...], value, preferred_element_type=jnp.float32)
    half = HOURS // 2 * RANK_PART
    wide = MAXB * CB
    for part in range(HOURS // 2):
        rows = slice(part * RANK_PART, (part + 1) * RANK_PART)
        turned = slice(half + part * RANK_PART, half + (part + 1) * RANK_PART)
        real_real, real_imag = total[rows, :wide], total[rows, wide:]
        imag_real, imag_imag = total[turned, :wide], total[turned, wide:]
        for where, sign in ((part, 1.0), (HOURS - 1 - part, -1.0)):
            out[where, :RANK_PART] = (real_real - sign * imag_imag).astype(jnp.bfloat16)
            out[where, RANK_PART:] = (real_imag + sign * imag_real).astype(jnp.bfloat16)


def stack_kernel(live_ref, expand, parts, out):
    step = pl.program_id(0)
    for slot in range(out.shape[0]):
        lanes = slice(slot * CB, (slot + 1) * CB)
        linear = mean_real = mean_imag = None
        for hour in range(HOURS):
            part = parts[hour, :, lanes]
            part = jnp.concatenate([part, part], axis=0)
            lagged = lax.dot_general(
                part, expand[...], (((0,), (0,)), ((), ())), preferred_element_type=jnp.float32
            )
            correlation = lagged[:, :LAG_PART]
            quadrature = lagged[:, LAG_PART:]
            power = correlation * correlation + quadrature * quadrature
            inverse = jnp.minimum(lax.rsqrt(power), 1.0 / amp_floor)
            unit_real = correlation * inverse
            unit_imag = quadrature * inverse
            if hour == 0:
                linear, mean_real, mean_imag = correlation, unit_real, unit_imag
            else:
                linear = linear + correlation
                mean_real = mean_real + unit_real
                mean_imag = mean_imag + unit_imag
        stacked = linear * (mean_real * mean_real + mean_imag * mean_imag) * (1.0 / HOURS**3)
        live = step * out.shape[0] + slot < live_ref[0]
        out[slot] = jnp.where(live, stacked, jnp.zeros_like(stacked))


def on_device(spectra, pair_blocks, block_count):
    owner = lax.axis_index("pairs")
    core = owner % 2
    window, compress, (high, low), expand = tables()
    spectra = spectra[:, 0]
    twins = [(i, i ^ 1) for i in range(OWNERS)]
    twin = lax.ppermute(spectra, "pairs", twins)
    own_size = magnitude_of(spectra[0], spectra[1])
    last = OWNERS - 1
    near_pairs = [(i, i + 1) for i in range(1, last, 2)] + [(i, i - 1) for i in range(2, last, 2)]
    near = lax.ppermute(own_size, "pairs", near_pairs)
    far = lax.ppermute(near, "pairs", twins)
    twin_size = magnitude_of(twin[0], twin[1])
    vmem = pl.BlockSpec(memory_space=pltpu.VMEM)
    smem = pl.BlockSpec(memory_space=pltpu.SMEM)
    limit = pltpu.CompilerParams(vmem_limit_bytes=32 * 2**20)
    slots = pair_blocks.reshape(-1)
    white = pltpu.VMEM((2, BINS, C), jnp.bfloat16)
    own_cross = pl.pallas_call(
        own_kernel,
        out_shape=jax.ShapeDtypeStruct((CHIPS, 2 * BINS, MAXB * CB), jnp.bfloat16),
        in_specs=[smem, smem] + [vmem] * 5,
        out_specs=vmem,
        scratch_shapes=[white],
        compiler_params=limit,
        name="own_cross",
    )(slots, core[None], window, spectra, near, own_size, twin_size)
    packed = pl.pallas_call(
        twin_kernel,
        out_shape=jax.ShapeDtypeStruct((CHIPS, ROWS_CHIP, MAXB * CB), jnp.bfloat16),
        in_specs=[smem, smem] + [vmem] * 7,
        out_specs=vmem,
        scratch_shapes=[white],
        compiler_params=limit,
        name="twin_cross",
    )(slots, core[None], window, compress, twin, own_size, twin_size, far, own_cross)
    groups = [list(range(0, OWNERS, 2)), list(range(1, OWNERS, 2))]
    packed = lax.all_to_all(packed, "pairs", 0, 0, axis_index_groups=groups, tiled=True)
    parts = pl.pallas_call(
        combine_kernel,
        out_shape=jax.ShapeDtypeStruct((HOURS, ROWS_PART, MAXB * CB), jnp.bfloat16),
        in_specs=[vmem] * 3,
        out_specs=vmem,
        compiler_params=pltpu.CompilerParams(vmem_limit_bytes=32 * 2**20),
        name="combine",
    )(high, low, packed)
    parts = lax.all_to_all(parts, "tm", 0, 0, tiled=True)
    live = lax.dynamic_index_in_dim(block_count, owner, 0, keepdims=True)
    slots = 2
    return pl.pallas_call(
        stack_kernel,
        grid=(MAXB // slots,),
        out_shape=jax.ShapeDtypeStruct((MAXB, CB, LAG_PART), jnp.float32),
        in_specs=[
            smem,
            pl.BlockSpec((2 * ROWS_PART, 2 * LAG_PART), lambda i: (0, 0)),
            pl.BlockSpec((HOURS, ROWS_PART, slots * CB), lambda i: (0, 0, i)),
        ],
        out_specs=pl.BlockSpec((slots, CB, LAG_PART), lambda i: (i, 0, 0)),
        compiler_params=pltpu.CompilerParams(vmem_limit_bytes=32 * 2**20),
        name="stack",
    )(live, expand, parts)


def solution(mesh):
    return jax.shard_map(
        on_device,
        mesh=mesh,
        in_specs=(P(None, "tm", "pairs", None), P(), P()),
        out_specs=P("pairs", None, "tm"),
        check_vma=False,
    )
```

```python
import functools
import math

import jax
import jax.numpy as jnp
import ml_dtypes
import numpy as np
from jax import lax
from jax.experimental import pallas as pl
from jax.experimental.pallas import tpu as pltpu
from jax.sharding import PartitionSpec as P

C = 4096
CB = 128
NF = 1024
FIRST_BIN = 16
FFT_LEN = 8192
LAGS = 2048
SMOOTH = 32
MAXB = 4
HOURS = 8
OWNERS = 32
amp_floor = 0.2

CHIPS = OWNERS // 2
BINS = NF // OWNERS
CHIP_BINS = 2 * BINS
LAG_PART = LAGS // HOURS
RANK_CHIP = 28
RANK_PART = 48
ROWS_CHIP = 2 * RANK_CHIP
ROWS_PART = 2 * RANK_PART
STEP = 2.0 * math.pi / FFT_LEN


def slepian(points, half_width, count):
    n = np.arange(points, dtype=np.float64)
    tri = np.diag(((points - 1) / 2.0 - n) ** 2 * math.cos(2.0 * math.pi * half_width))
    off = n[1:] * (points - n[1:]) / 2.0
    tri = tri + np.diag(off, 1) + np.diag(off, -1)
    vectors = np.linalg.eigh(tri)[1][:, ::-1][:, :count]
    return vectors * np.where(vectors[points // 2] < 0, -1.0, 1.0)


def split_rounded(table):
    high = table.astype(ml_dtypes.bfloat16)
    low = (table - high.astype(np.float64)).astype(ml_dtypes.bfloat16)
    return high, low


def real_form(table):
    return np.block([[table.real, -table.imag], [table.imag, table.real]])


@functools.cache
def tables():
    chip_basis = slepian(CHIP_BINS, LAGS / 2 / FFT_LEN, RANK_CHIP)
    part_basis = slepian(NF, LAG_PART / 2 / FFT_LEN, RANK_PART)
    bins = np.arange(NF) - (NF - 1) / 2.0
    lags = np.arange(LAG_PART) - LAG_PART // 2
    mid_bin = FIRST_BIN + (NF - 1) / 2.0
    compress = np.kron(np.eye(2), chip_basis.T)
    parts = []
    for part in range(HOURS // 2):
        mid_lag = LAG_PART * part - (LAGS - LAG_PART) // 2
        turned = np.exp(1j * STEP * (bins + mid_bin) * mid_lag)[:, None] * part_basis
        turned = turned.reshape(CHIPS, CHIP_BINS, RANK_PART)
        blocks = [(chip_basis.T @ turned[chip]).T for chip in range(CHIPS)]
        parts.append(np.concatenate(blocks, axis=1))
    combine = np.concatenate([half for part in parts for half in (part.real, part.imag)], axis=0)
    waves = np.exp(1j * STEP * np.outer(lags, bins)) @ part_basis
    waves = waves * np.exp(1j * STEP * mid_bin * lags)[:, None] / math.sqrt(NF)
    expand = real_form(waves)
    row = np.arange(BINS)[:, None] + SMOOTH
    column = np.arange(BINS + 2 * SMOOTH)[None, :]
    window = (np.abs(row - column) <= SMOOTH).astype(ml_dtypes.bfloat16)
    turned = [window[:, -SMOOTH:], window[:, SMOOTH:-SMOOTH], window[:, :SMOOTH]]
    window = np.stack([window, np.concatenate(turned, axis=1)])
    halves = np.split(compress, 2 * CHIP_BINS // BINS, axis=1)
    by_core = []
    for core in range(2):
        own, twin = core, 1 - core
        ordered = [halves[own], halves[2 + own], halves[twin], halves[2 + twin]]
        by_core.append(np.concatenate(split_rounded(np.concatenate(ordered, axis=1)), axis=1))
    compress = np.stack(by_core)
    padded = np.zeros((2 * CB, 2 * LAG_PART), ml_dtypes.bfloat16)
    for index, half in enumerate(split_rounded(expand)):
        padded[index * CB : index * CB + ROWS_PART] = half.T
    expand = padded
    return window, compress, split_rounded(combine), expand


def magnitude_of(real, imag):
    real, imag = real.astype(jnp.float32), imag.astype(jnp.float32)
    return jnp.sqrt(real * real + imag * imag).astype(jnp.bfloat16)


def whiten(core, window, source, first, centre, second, white):
    chunk = 512
    weights = window[core]
    for start in range(0, C, chunk):
        lanes = slice(start, start + chunk)
        sizes = jnp.concatenate([first[:, lanes], centre[:, lanes], second[:, lanes]], axis=0)
        sums = jnp.dot(weights, sizes, preferred_element_type=jnp.float32)
        inverse = 1.0 / (sums * (1.0 / (2 * SMOOTH + 1)) + 1e-05)
        for part in range(2):
            value = source[part, :, lanes].astype(jnp.float32) * inverse
            white[part, :, lanes] = value.astype(jnp.bfloat16)


def cross_of(blocks, base, white):
    crossed = []
    for slot in range(MAXB):
        left = pl.ds(pl.multiple_of(blocks[base + 2 * slot] * CB, CB), CB)
        right = pl.ds(pl.multiple_of(blocks[base + 2 * slot + 1] * CB, CB), CB)
        left_re = white[0, :, left].astype(jnp.float32)
        left_im = white[1, :, left].astype(jnp.float32)
        right_re = white[0, :, right].astype(jnp.float32)
        right_im = white[1, :, right].astype(jnp.float32)
        real = left_re * right_re + left_im * right_im
        imag = left_im * right_re - left_re * right_im
        crossed.append(jnp.concatenate([real, imag], axis=0).astype(jnp.bfloat16))
    return jnp.concatenate(crossed, axis=1)


def own_kernel(blocks, window, own, near, own_size, twin_size, out, white):
    core = blocks[CHIPS * 2 * MAXB]
    whiten(core, window, own, near, own_size, twin_size, white)
    for chip in range(CHIPS):
        out[chip] = cross_of(blocks, chip * 2 * MAXB, white)


def twin_kernel(
    blocks, window, compress, twin, own_size, twin_size, far, own_cross, out, white
):
    core = blocks[CHIPS * 2 * MAXB]
    whiten(core, window, twin, own_size, twin_size, far, white)
    weights = compress[core]
    for chip in range(CHIPS):
        twin_cross = cross_of(blocks, chip * 2 * MAXB, white)
        cross = jnp.concatenate([own_cross[chip], twin_cross] * 2, axis=0)
        packed = jnp.dot(weights, cross, preferred_element_type=jnp.float32)
        out[chip] = packed.astype(jnp.bfloat16)


def combine_kernel(high, low, packed, out, parts, sems):
    real = jnp.concatenate([packed[chip, :RANK_CHIP] for chip in range(CHIPS)], axis=0)
    imag = jnp.concatenate([packed[chip, RANK_CHIP:] for chip in range(CHIPS)], axis=0)
    value = jnp.concatenate([real, imag], axis=1)
    wide = MAXB * CB
    copies = []
    for part in range(HOURS // 2):
        rows = slice(part * ROWS_PART, (part + 1) * ROWS_PART)
        total = jnp.dot(high[rows], value, preferred_element_type=jnp.float32)
        total = total + jnp.dot(low[rows], value, preferred_element_type=jnp.float32)
        real_real, real_imag = total[:RANK_PART, :wide], total[:RANK_PART, wide:]
        imag_real, imag_imag = total[RANK_PART:, :wide], total[RANK_PART:, wide:]
        for where, sign in ((part, 1.0), (HOURS - 1 - part, -1.0)):
            both = [real_real - sign * imag_imag, real_imag + sign * imag_real]
            parts[where] = jnp.concatenate(both, axis=0).astype(jnp.bfloat16)
            copy = pltpu.make_async_copy(parts.at[where], out.at[where], sems.at[where])
            copy.start()
            copies.append(copy)
    for copy in copies:
        copy.wait()


def stack_kernel(live, expand, parts, out, result, sems):
    blank = jnp.zeros((CB - ROWS_PART, CB), jnp.bfloat16)
    copies = []
    for slot in range(MAXB):
        lanes = slice(slot * CB, (slot + 1) * CB)
        rows = []
        for hour in range(HOURS):
            part = jnp.concatenate([parts[hour, :, lanes], blank], axis=0).T
            rows.append(jnp.concatenate([part, part], axis=1))
        lagged = jnp.dot(
            jnp.concatenate(rows, axis=0), expand[...], preferred_element_type=jnp.float32
        )
        linear = mean_real = mean_imag = None
        for hour in range(HOURS):
            correlation = lagged[hour * CB : (hour + 1) * CB, :LAG_PART]
            quadrature = lagged[hour * CB : (hour + 1) * CB, LAG_PART:]
            power = correlation * correlation + quadrature * quadrature
            inverse = jnp.minimum(lax.rsqrt(power), 1.0 / amp_floor)
            unit_real = correlation * inverse
            unit_imag = quadrature * inverse
            if hour == 0:
                linear, mean_real, mean_imag = correlation, unit_real, unit_imag
            else:
                linear = linear + correlation
                mean_real = mean_real + unit_real
                mean_imag = mean_imag + unit_imag
        stacked = linear * (mean_real * mean_real + mean_imag * mean_imag) * (1.0 / HOURS**3)
        result[slot] = jnp.where(live[slot] > 0, stacked, jnp.zeros_like(stacked))
        copy = pltpu.make_async_copy(result.at[slot], out.at[slot], sems.at[slot])
        copy.start()
        copies.append(copy)
    for copy in copies:
        copy.wait()


def on_device(spectra, pair_blocks, block_count):
    owner = lax.axis_index("pairs")
    core = owner % 2
    window, compress, (high, low), expand = tables()
    spectra = spectra[:, 0]
    twins = [(i, i ^ 1) for i in range(OWNERS)]
    twin = lax.ppermute(spectra, "pairs", twins)
    own_size = magnitude_of(spectra[0], spectra[1])
    last = OWNERS - 1
    near_pairs = [(i, i + 1) for i in range(1, last, 2)] + [(i, i - 1) for i in range(2, last, 2)]
    near = lax.ppermute(own_size, "pairs", near_pairs)
    far = lax.ppermute(near, "pairs", twins)
    twin_size = magnitude_of(twin[0], twin[1])
    vmem = pl.BlockSpec(memory_space=pltpu.VMEM)
    smem = pl.BlockSpec(memory_space=pltpu.SMEM)
    limit = pltpu.CompilerParams(vmem_limit_bytes=32 * 2**20)
    slots = lax.dynamic_index_in_dim(
        pair_blocks.reshape(CHIPS, 2, 2 * MAXB), core, 1, keepdims=False
    )
    slots = jnp.concatenate([slots.reshape(-1), core[None]])
    white = pltpu.VMEM((2, BINS, C), jnp.bfloat16)
    own_cross = pl.pallas_call(
        own_kernel,
        out_shape=jax.ShapeDtypeStruct((CHIPS, 2 * BINS, MAXB * CB), jnp.bfloat16),
        in_specs=[smem] + [vmem] * 5,
        out_specs=vmem,
        scratch_shapes=[white],
        compiler_params=limit,
        name="own_cross",
    )(slots, window, spectra, near, own_size, twin_size)
    packed = pl.pallas_call(
        twin_kernel,
        out_shape=jax.ShapeDtypeStruct((CHIPS, ROWS_CHIP, MAXB * CB), jnp.bfloat16),
        in_specs=[smem] + [vmem] * 7,
        out_specs=vmem,
        scratch_shapes=[white],
        compiler_params=limit,
        name="twin_cross",
    )(slots, window, compress, twin, own_size, twin_size, far, own_cross)
    groups = [list(range(0, OWNERS, 2)), list(range(1, OWNERS, 2))]
    packed = lax.all_to_all(packed, "pairs", 0, 0, axis_index_groups=groups, tiled=True)
    parts = pl.pallas_call(
        combine_kernel,
        out_shape=jax.ShapeDtypeStruct((HOURS, ROWS_PART, MAXB * CB), jnp.bfloat16),
        in_specs=[vmem] * 3,
        out_specs=pl.BlockSpec(memory_space=pl.ANY),
        scratch_shapes=[
            pltpu.VMEM((HOURS, ROWS_PART, MAXB * CB), jnp.bfloat16),
            pltpu.SemaphoreType.DMA((HOURS,)),
        ],
        compiler_params=limit,
        name="combine",
    )(high, low, packed)
    parts = lax.all_to_all(parts, "tm", 0, 0, tiled=True)
    count = lax.dynamic_index_in_dim(block_count, owner, 0, keepdims=False)
    live = (lax.broadcasted_iota(jnp.int32, (MAXB, 1, LAG_PART), 0) < count).astype(jnp.float32)
    return pl.pallas_call(
        stack_kernel,
        out_shape=jax.ShapeDtypeStruct((MAXB, CB, LAG_PART), jnp.float32),
        in_specs=[vmem] * 3,
        out_specs=pl.BlockSpec(memory_space=pl.ANY),
        scratch_shapes=[
            pltpu.VMEM((MAXB, CB, LAG_PART), jnp.float32),
            pltpu.SemaphoreType.DMA((MAXB,)),
        ],
        compiler_params=limit,
        name="stack",
    )(live, expand, parts)


def solution(mesh):
    return jax.shard_map(
        on_device,
        mesh=mesh,
        in_specs=(P(None, "tm", "pairs", None), P(), P()),
        out_specs=P("pairs", None, "tm"),
        check_vma=False,
    )
```

```python
import functools
import math

import jax
import jax.numpy as jnp
import ml_dtypes
import numpy as np
from jax import lax
from jax.experimental import pallas as pl
from jax.experimental.pallas import tpu as pltpu
from jax.sharding import PartitionSpec as P

C = 4096
CB = 128
NF = 1024
FIRST_BIN = 16
FFT_LEN = 8192
LAGS = 2048
SMOOTH = 32
MAXB = 4
HOURS = 8
OWNERS = 32
amp_floor = 0.2

CHIPS = OWNERS // 2
BINS = NF // OWNERS
CHIP_BINS = 2 * BINS
LAG_PART = LAGS // HOURS
RANK_CHIP = 28
RANK_PART = 48
ROWS_CHIP = 2 * RANK_CHIP
ROWS_PART = 2 * RANK_PART
STEP = 2.0 * math.pi / FFT_LEN


def slepian(points, half_width, count):
    n = np.arange(points, dtype=np.float64)
    tri = np.diag(((points - 1) / 2.0 - n) ** 2 * math.cos(2.0 * math.pi * half_width))
    off = n[1:] * (points - n[1:]) / 2.0
    tri = tri + np.diag(off, 1) + np.diag(off, -1)
    vectors = np.linalg.eigh(tri)[1][:, ::-1][:, :count]
    return vectors * np.where(vectors[points // 2] < 0, -1.0, 1.0)


def split_rounded(table):
    high = table.astype(ml_dtypes.bfloat16)
    low = (table - high.astype(np.float64)).astype(ml_dtypes.bfloat16)
    return high, low


def real_form(table):
    return np.block([[table.real, -table.imag], [table.imag, table.real]])


@functools.cache
def tables():
    chip_basis = slepian(CHIP_BINS, LAGS / 2 / FFT_LEN, RANK_CHIP)
    part_basis = slepian(NF, LAG_PART / 2 / FFT_LEN, RANK_PART)
    bins = np.arange(NF) - (NF - 1) / 2.0
    lags = np.arange(LAG_PART) - LAG_PART // 2
    mid_bin = FIRST_BIN + (NF - 1) / 2.0
    compress = np.kron(np.eye(2), chip_basis.T)
    parts = []
    for part in range(HOURS // 2):
        mid_lag = LAG_PART * part - (LAGS - LAG_PART) // 2
        turned = np.exp(1j * STEP * (bins + mid_bin) * mid_lag)[:, None] * part_basis
        turned = turned.reshape(CHIPS, CHIP_BINS, RANK_PART)
        blocks = [(chip_basis.T @ turned[chip]).T for chip in range(CHIPS)]
        parts.append(np.concatenate(blocks, axis=1))
    combine = np.concatenate([half for part in parts for half in (part.real, part.imag)], axis=0)
    waves = np.exp(1j * STEP * np.outer(lags, bins)) @ part_basis
    waves = waves * np.exp(1j * STEP * mid_bin * lags)[:, None] / math.sqrt(NF)
    expand = real_form(waves)
    row = np.arange(BINS)[:, None] + SMOOTH
    column = np.arange(BINS + 2 * SMOOTH)[None, :]
    window = (np.abs(row - column) <= SMOOTH).astype(ml_dtypes.bfloat16)
    turned = [window[:, -SMOOTH:], window[:, SMOOTH:-SMOOTH], window[:, :SMOOTH]]
    window = np.stack([window, np.concatenate(turned, axis=1)])
    halves = np.split(compress, 2 * CHIP_BINS // BINS, axis=1)
    by_core = []
    for core in range(2):
        own, twin = core, 1 - core
        ordered = [halves[own], halves[2 + own], halves[twin], halves[2 + twin]]
        by_core.append(np.concatenate(split_rounded(np.concatenate(ordered, axis=1)), axis=1))
    compress = np.stack(by_core)
    padded = np.zeros((2 * CB, 2 * LAG_PART), ml_dtypes.bfloat16)
    for index, half in enumerate(split_rounded(expand)):
        padded[index * CB : index * CB + ROWS_PART] = half.T
    expand = padded
    return window, compress, split_rounded(combine), expand


def magnitude_of(real, imag):
    real, imag = real.astype(jnp.float32), imag.astype(jnp.float32)
    return jnp.sqrt(real * real + imag * imag).astype(jnp.bfloat16)


def whiten(core, window, source, first, centre, second, white):
    chunk = 512
    weights = window[core]
    for start in range(0, C, chunk):
        lanes = slice(start, start + chunk)
        sizes = jnp.concatenate([first[:, lanes], centre[:, lanes], second[:, lanes]], axis=0)
        sums = jnp.dot(weights, sizes, preferred_element_type=jnp.float32)
        inverse = 1.0 / (sums * (1.0 / (2 * SMOOTH + 1)) + 1e-05)
        for part in range(2):
            value = source[part, :, lanes].astype(jnp.float32) * inverse
            white[part, :, lanes] = value.astype(jnp.bfloat16)


def cross_of(blocks, base, white):
    crossed = []
    for slot in range(MAXB):
        left = pl.ds(pl.multiple_of(blocks[base + 2 * slot] * CB, CB), CB)
        right = pl.ds(pl.multiple_of(blocks[base + 2 * slot + 1] * CB, CB), CB)
        left_re = white[0, :, left].astype(jnp.float32)
        left_im = white[1, :, left].astype(jnp.float32)
        right_re = white[0, :, right].astype(jnp.float32)
        right_im = white[1, :, right].astype(jnp.float32)
        real = left_re * right_re + left_im * right_im
        imag = left_im * right_re - left_re * right_im
        crossed.append(jnp.concatenate([real, imag], axis=0).astype(jnp.bfloat16))
    return jnp.concatenate(crossed, axis=1)


def own_kernel(blocks, window, own, near, own_size, twin_size, out, white):
    core = blocks[CHIPS * 2 * MAXB]
    whiten(core, window, own, near, own_size, twin_size, white)
    for chip in range(CHIPS):
        out[chip] = cross_of(blocks, chip * 2 * MAXB, white)


def twin_kernel(
    blocks, window, compress, twin, own_size, twin_size, far, own_cross, out, white
):
    core = blocks[CHIPS * 2 * MAXB]
    whiten(core, window, twin, own_size, twin_size, far, white)
    weights = compress[core]
    for chip in range(CHIPS):
        twin_cross = cross_of(blocks, chip * 2 * MAXB, white)
        cross = jnp.concatenate([own_cross[chip], twin_cross] * 2, axis=0)
        packed = jnp.dot(weights, cross, preferred_element_type=jnp.float32)
        out[chip] = packed.astype(jnp.bfloat16)


def combine_kernel(high, low, packed, out):
    wide = out.shape[2]
    real = [packed[chip, :RANK_CHIP, :wide] for chip in range(CHIPS)]
    imag = [packed[chip, RANK_CHIP:, :wide] for chip in range(CHIPS)]
    value = jnp.concatenate([jnp.concatenate(real, axis=0), jnp.concatenate(imag, axis=0)], axis=1)
    total = jnp.dot(high[...], value, preferred_element_type=jnp.float32)
    total = total + jnp.dot(low[...], value, preferred_element_type=jnp.float32)
    for part in range(HOURS // 2):
        base = part * ROWS_PART
        real_rows = slice(base, base + RANK_PART)
        imag_rows = slice(base + RANK_PART, base + ROWS_PART)
        real_real, real_imag = total[real_rows, :wide], total[real_rows, wide:]
        imag_real, imag_imag = total[imag_rows, :wide], total[imag_rows, wide:]
        for where, sign in ((part, 1.0), (HOURS - 1 - part, -1.0)):
            both = [real_real - sign * imag_imag, real_imag + sign * imag_real]
            out[where] = jnp.concatenate(both, axis=0).astype(jnp.bfloat16)


def stack_kernel(expand, parts, out, result, sems):
    blank = jnp.zeros((CB - ROWS_PART, CB), jnp.bfloat16)
    live = parts.shape[2] // CB
    copies = []
    for slot in range(live, MAXB):
        result[slot] = jnp.zeros((CB, LAG_PART), jnp.float32)
    if live < MAXB:
        copy = pltpu.make_async_copy(result.at[live:], out.at[live:], sems.at[live])
        copy.start()
        copies.append(copy)
    for slot in range(live):
        lanes = slice(slot * CB, (slot + 1) * CB)
        rows = []
        for hour in range(HOURS):
            part = jnp.concatenate([parts[hour, :, lanes], blank], axis=0).T
            rows.append(jnp.concatenate([part, part], axis=1))
        lagged = jnp.dot(
            jnp.concatenate(rows, axis=0), expand[...], preferred_element_type=jnp.float32
        )
        linear = mean_real = mean_imag = None
        for hour in range(HOURS):
            correlation = lagged[hour * CB : (hour + 1) * CB, :LAG_PART]
            quadrature = lagged[hour * CB : (hour + 1) * CB, LAG_PART:]
            power = correlation * correlation + quadrature * quadrature
            inverse = jnp.minimum(lax.rsqrt(power), 1.0 / amp_floor)
            unit_real = correlation * inverse
            unit_imag = quadrature * inverse
            if hour == 0:
                linear, mean_real, mean_imag = correlation, unit_real, unit_imag
            else:
                linear = linear + correlation
                mean_real = mean_real + unit_real
                mean_imag = mean_imag + unit_imag
        stacked = linear * (mean_real * mean_real + mean_imag * mean_imag) * (1.0 / HOURS**3)
        result[slot] = stacked
        copy = pltpu.make_async_copy(result.at[slot], out.at[slot], sems.at[slot])
        copy.start()
        copies.append(copy)
    for copy in copies:
        copy.wait()


def on_device(spectra, pair_blocks, block_count):
    owner = lax.axis_index("pairs")
    core = owner % 2
    window, compress, (high, low), expand = tables()
    spectra = spectra[:, 0]
    twins = [(i, i ^ 1) for i in range(OWNERS)]
    twin = lax.ppermute(spectra, "pairs", twins)
    own_size = magnitude_of(spectra[0], spectra[1])
    last = OWNERS - 1
    near_pairs = [(i, i + 1) for i in range(1, last, 2)] + [(i, i - 1) for i in range(2, last, 2)]
    near = lax.ppermute(own_size, "pairs", near_pairs)
    far = lax.ppermute(near, "pairs", twins)
    twin_size = magnitude_of(twin[0], twin[1])
    vmem = pl.BlockSpec(memory_space=pltpu.VMEM)
    smem = pl.BlockSpec(memory_space=pltpu.SMEM)
    limit = pltpu.CompilerParams(vmem_limit_bytes=32 * 2**20)
    slots = lax.dynamic_index_in_dim(
        pair_blocks.reshape(CHIPS, 2, 2 * MAXB), core, 1, keepdims=False
    )
    slots = jnp.concatenate([slots.reshape(-1), core[None]])
    white = pltpu.VMEM((2, BINS, C), jnp.bfloat16)
    own_cross = pl.pallas_call(
        own_kernel,
        out_shape=jax.ShapeDtypeStruct((CHIPS, 2 * BINS, MAXB * CB), jnp.bfloat16),
        in_specs=[smem] + [vmem] * 5,
        out_specs=vmem,
        scratch_shapes=[white],
        compiler_params=limit,
        name="own_cross",
    )(slots, window, spectra, near, own_size, twin_size)
    packed = pl.pallas_call(
        twin_kernel,
        out_shape=jax.ShapeDtypeStruct((CHIPS, ROWS_CHIP, MAXB * CB), jnp.bfloat16),
        in_specs=[smem] + [vmem] * 7,
        out_specs=vmem,
        scratch_shapes=[white],
        compiler_params=limit,
        name="twin_cross",
    )(slots, window, compress, twin, own_size, twin_size, far, own_cross)
    groups = [list(range(0, OWNERS, 2)), list(range(1, OWNERS, 2))]
    packed = lax.all_to_all(packed, "pairs", 0, 0, axis_index_groups=groups, tiled=True)

    def with_live(live):
        def finish(packed):
            parts = pl.pallas_call(
                combine_kernel,
                out_shape=jax.ShapeDtypeStruct((HOURS, ROWS_PART, live * CB), jnp.bfloat16),
                in_specs=[vmem] * 3,
                out_specs=vmem,
                compiler_params=limit,
                name=f"combine_{live}",
            )(high, low, packed)
            parts = lax.all_to_all(parts, "tm", 0, 0, tiled=True)
            return pl.pallas_call(
                stack_kernel,
                out_shape=jax.ShapeDtypeStruct((MAXB, CB, LAG_PART), jnp.float32),
                in_specs=[vmem] * 2,
                out_specs=pl.BlockSpec(memory_space=pl.ANY),
                scratch_shapes=[
                    pltpu.VMEM((MAXB, CB, LAG_PART), jnp.float32),
                    pltpu.SemaphoreType.DMA((MAXB,)),
                ],
                compiler_params=limit,
                name=f"stack_{live}",
            )(expand, parts)

        return finish

    count = lax.dynamic_index_in_dim(block_count, owner, 0, keepdims=False)
    return lax.switch(count - 1, [with_live(live) for live in range(1, MAXB + 1)], packed)


def solution(mesh):
    return jax.shard_map(
        on_device,
        mesh=mesh,
        in_specs=(P(None, "tm", "pairs", None), P(), P()),
        out_specs=P("pairs", None, "tm"),
        check_vma=False,
    )
```

```python
import functools
import math

import jax
import jax.numpy as jnp
import ml_dtypes
import numpy as np
from jax import lax
from jax.experimental import pallas as pl
from jax.experimental.pallas import tpu as pltpu
from jax.sharding import PartitionSpec as P

C = 4096
CB = 128
NF = 1024
FIRST_BIN = 16
FFT_LEN = 8192
LAGS = 2048
SMOOTH = 32
MAXB = 4
HOURS = 8
OWNERS = 32
amp_floor = 0.2

CHIPS = OWNERS // 2
BINS = NF // OWNERS
CHIP_BINS = 2 * BINS
LAG_PART = LAGS // HOURS
RANK_CHIP = 28
RANK_PART = 48
ROWS_CHIP = 2 * RANK_CHIP
ROWS_PART = 2 * RANK_PART
STEP = 2.0 * math.pi / FFT_LEN


def slepian(points, half_width, count):
    n = np.arange(points, dtype=np.float64)
    tri = np.diag(((points - 1) / 2.0 - n) ** 2 * math.cos(2.0 * math.pi * half_width))
    off = n[1:] * (points - n[1:]) / 2.0
    tri = tri + np.diag(off, 1) + np.diag(off, -1)
    vectors = np.linalg.eigh(tri)[1][:, ::-1][:, :count]
    return vectors * np.where(vectors[points // 2] < 0, -1.0, 1.0)


def split_rounded(table):
    high = table.astype(ml_dtypes.bfloat16)
    low = (table - high.astype(np.float64)).astype(ml_dtypes.bfloat16)
    return high, low


def real_form(table):
    return np.block([[table.real, -table.imag], [table.imag, table.real]])


@functools.cache
def tables():
    chip_basis = slepian(CHIP_BINS, LAGS / 2 / FFT_LEN, RANK_CHIP)
    part_basis = slepian(NF, LAG_PART / 2 / FFT_LEN, RANK_PART)
    bins = np.arange(NF) - (NF - 1) / 2.0
    lags = np.arange(LAG_PART) - LAG_PART // 2
    mid_bin = FIRST_BIN + (NF - 1) / 2.0
    compress = np.kron(np.eye(2), chip_basis.T)
    parts = []
    for part in range(HOURS // 2):
        mid_lag = LAG_PART * part - (LAGS - LAG_PART) // 2
        turned = np.exp(1j * STEP * (bins + mid_bin) * mid_lag)[:, None] * part_basis
        turned = turned.reshape(CHIPS, CHIP_BINS, RANK_PART)
        blocks = [(chip_basis.T @ turned[chip]).T for chip in range(CHIPS)]
        parts.append(np.concatenate(blocks, axis=1))
    combine = np.concatenate([half for part in parts for half in (part.real, part.imag)], axis=0)
    waves = np.exp(1j * STEP * np.outer(lags, bins)) @ part_basis
    waves = waves * np.exp(1j * STEP * mid_bin * lags)[:, None] / math.sqrt(NF)
    expand = real_form(waves)
    row = np.arange(BINS)[:, None] + SMOOTH
    column = np.arange(BINS + 2 * SMOOTH)[None, :]
    window = (np.abs(row - column) <= SMOOTH).astype(ml_dtypes.bfloat16)
    turned = [window[:, -SMOOTH:], window[:, SMOOTH:-SMOOTH], window[:, :SMOOTH]]
    window = np.stack([window, np.concatenate(turned, axis=1)])
    halves = np.split(compress, 2 * CHIP_BINS // BINS, axis=1)
    by_core = []
    for core in range(2):
        own, twin = core, 1 - core
        ordered = [halves[own], halves[2 + own], halves[twin], halves[2 + twin]]
        by_core.append(np.concatenate(split_rounded(np.concatenate(ordered, axis=1)), axis=1))
    compress = np.stack(by_core)
    padded = np.zeros((2 * CB, 2 * LAG_PART), ml_dtypes.bfloat16)
    for index, half in enumerate(split_rounded(expand)):
        padded[index * CB : index * CB + ROWS_PART] = half.T
    expand = padded
    return window, compress, split_rounded(combine), expand


def magnitude_of(real, imag):
    real, imag = real.astype(jnp.float32), imag.astype(jnp.float32)
    return jnp.sqrt(real * real + imag * imag).astype(jnp.bfloat16)


def whiten(core, window, source, first, centre, second, white):
    chunk = 512
    weights = window[core]
    for start in range(0, C, chunk):
        lanes = slice(start, start + chunk)
        sizes = jnp.concatenate([first[:, lanes], centre[:, lanes], second[:, lanes]], axis=0)
        sums = jnp.dot(weights, sizes, preferred_element_type=jnp.float32)
        inverse = 1.0 / (sums * (1.0 / (2 * SMOOTH + 1)) + 1e-05)
        for part in range(2):
            value = source[part, :, lanes].astype(jnp.float32) * inverse
            white[part, :, lanes] = value.astype(jnp.bfloat16)


def cross_of(blocks, base, white):
    crossed = []
    for slot in range(MAXB):
        left = pl.ds(pl.multiple_of(blocks[base + 2 * slot] * CB, CB), CB)
        right = pl.ds(pl.multiple_of(blocks[base + 2 * slot + 1] * CB, CB), CB)
        left_re = white[0, :, left].astype(jnp.float32)
        left_im = white[1, :, left].astype(jnp.float32)
        right_re = white[0, :, right].astype(jnp.float32)
        right_im = white[1, :, right].astype(jnp.float32)
        real = left_re * right_re + left_im * right_im
        imag = left_im * right_re - left_re * right_im
        crossed.append(jnp.concatenate([real, imag], axis=0).astype(jnp.bfloat16))
    return jnp.concatenate(crossed, axis=1)


def own_kernel(blocks, window, own, near, own_size, twin_size, out, white):
    core = blocks[CHIPS * 2 * MAXB]
    whiten(core, window, own, near, own_size, twin_size, white)
    for chip in range(CHIPS):
        out[chip] = cross_of(blocks, chip * 2 * MAXB, white)


def twin_kernel(
    blocks, window, compress, twin, own_size, twin_size, far, own_cross, out, white
):
    core = blocks[CHIPS * 2 * MAXB]
    whiten(core, window, twin, own_size, twin_size, far, white)
    weights = compress[core]
    for chip in range(CHIPS):
        twin_cross = cross_of(blocks, chip * 2 * MAXB, white)
        cross = jnp.concatenate([own_cross[chip], twin_cross] * 2, axis=0)
        packed = jnp.dot(weights, cross, preferred_element_type=jnp.float32)
        out[chip] = packed.astype(jnp.bfloat16)


def combine_kernel(high, low, packed, out):
    wide = out.shape[2]
    real = [packed[chip, :RANK_CHIP, :wide] for chip in range(CHIPS)]
    imag = [packed[chip, RANK_CHIP:, :wide] for chip in range(CHIPS)]
    value = jnp.concatenate([jnp.concatenate(real, axis=0), jnp.concatenate(imag, axis=0)], axis=1)
    total = jnp.dot(high[...], value, preferred_element_type=jnp.float32)
    total = total + jnp.dot(low[...], value, preferred_element_type=jnp.float32)
    for part in range(HOURS // 2):
        base = part * ROWS_PART
        real_rows = slice(base, base + RANK_PART)
        imag_rows = slice(base + RANK_PART, base + ROWS_PART)
        real_real, real_imag = total[real_rows, :wide], total[real_rows, wide:]
        imag_real, imag_imag = total[imag_rows, :wide], total[imag_rows, wide:]
        for where, sign in ((part, 1.0), (HOURS - 1 - part, -1.0)):
            both = [real_real - sign * imag_imag, real_imag + sign * imag_real]
            out[where] = jnp.concatenate(both, axis=0).astype(jnp.bfloat16)


def stack_kernel(live, expand, parts, out, result, sems):
    blank = jnp.zeros((CB - ROWS_PART, CB), jnp.bfloat16)
    copies = []
    for slot in range(MAXB):
        lanes = slice(slot * CB, (slot + 1) * CB)
        rows = []
        for hour in range(HOURS):
            part = jnp.concatenate([parts[hour, :, lanes], blank], axis=0).T
            rows.append(jnp.concatenate([part, part], axis=1))
        lagged = jnp.dot(
            jnp.concatenate(rows, axis=0), expand[...], preferred_element_type=jnp.float32
        )
        linear = mean_real = mean_imag = None
        for hour in range(HOURS):
            correlation = lagged[hour * CB : (hour + 1) * CB, :LAG_PART]
            quadrature = lagged[hour * CB : (hour + 1) * CB, LAG_PART:]
            power = correlation * correlation + quadrature * quadrature
            inverse = jnp.minimum(lax.rsqrt(power), 1.0 / amp_floor)
            unit_real = correlation * inverse
            unit_imag = quadrature * inverse
            if hour == 0:
                linear, mean_real, mean_imag = correlation, unit_real, unit_imag
            else:
                linear = linear + correlation
                mean_real = mean_real + unit_real
                mean_imag = mean_imag + unit_imag
        stacked = linear * (mean_real * mean_real + mean_imag * mean_imag) * (1.0 / HOURS**3)
        result[slot] = jnp.where(live[slot] > 0, stacked, jnp.zeros_like(stacked))
        copy = pltpu.make_async_copy(result.at[slot], out.at[slot], sems.at[slot])
        copy.start()
        copies.append(copy)
    for copy in copies:
        copy.wait()


def on_device(spectra, pair_blocks, block_count):
    owner = lax.axis_index("pairs")
    core = owner % 2
    window, compress, (high, low), expand = tables()
    spectra = spectra[:, 0]
    twins = [(i, i ^ 1) for i in range(OWNERS)]
    twin = lax.ppermute(spectra, "pairs", twins)
    own_size = magnitude_of(spectra[0], spectra[1])
    last = OWNERS - 1
    near_pairs = [(i, i + 1) for i in range(1, last, 2)] + [(i, i - 1) for i in range(2, last, 2)]
    near = lax.ppermute(own_size, "pairs", near_pairs)
    far = lax.ppermute(near, "pairs", twins)
    twin_size = magnitude_of(twin[0], twin[1])
    vmem = pl.BlockSpec(memory_space=pltpu.VMEM)
    smem = pl.BlockSpec(memory_space=pltpu.SMEM)
    limit = pltpu.CompilerParams(vmem_limit_bytes=32 * 2**20)
    slots = lax.dynamic_index_in_dim(
        pair_blocks.reshape(CHIPS, 2, 2 * MAXB), core, 1, keepdims=False
    )
    slots = jnp.concatenate([slots.reshape(-1), core[None]])
    count = lax.dynamic_index_in_dim(block_count, owner, 0, keepdims=False)
    slots, count = lax.optimization_barrier((slots, count))
    high, low = lax.optimization_barrier((jnp.asarray(high), jnp.asarray(low)))
    white = pltpu.VMEM((2, BINS, C), jnp.bfloat16)
    own_cross = pl.pallas_call(
        own_kernel,
        out_shape=jax.ShapeDtypeStruct((CHIPS, 2 * BINS, MAXB * CB), jnp.bfloat16),
        in_specs=[smem] + [vmem] * 5,
        out_specs=vmem,
        scratch_shapes=[white],
        compiler_params=limit,
        name="own_cross",
    )(slots, window, spectra, near, own_size, twin_size)
    packed = pl.pallas_call(
        twin_kernel,
        out_shape=jax.ShapeDtypeStruct((CHIPS, ROWS_CHIP, MAXB * CB), jnp.bfloat16),
        in_specs=[smem] + [vmem] * 7,
        out_specs=vmem,
        scratch_shapes=[white],
        compiler_params=limit,
        name="twin_cross",
    )(slots, window, compress, twin, own_size, twin_size, far, own_cross)
    groups = [list(range(0, OWNERS, 2)), list(range(1, OWNERS, 2))]
    packed = lax.all_to_all(packed, "pairs", 0, 0, axis_index_groups=groups, tiled=True)

    def with_live(live):
        def exchange(packed, high, low):
            parts = pl.pallas_call(
                combine_kernel,
                out_shape=jax.ShapeDtypeStruct((HOURS, ROWS_PART, live * CB), jnp.bfloat16),
                in_specs=[vmem] * 3,
                out_specs=vmem,
                compiler_params=limit,
                name=f"combine_{live}",
            )(high, low, packed)
            parts = lax.all_to_all(parts, "tm", 0, 0, tiled=True)
            return jnp.pad(parts, ((0, 0), (0, 0), (0, (MAXB - live) * CB)))

        return exchange

    branches = [with_live(live) for live in range(1, MAXB + 1)]
    parts = lax.switch(count - 1, branches, packed, high, low)
    live = (lax.broadcasted_iota(jnp.int32, (MAXB, 1, LAG_PART), 0) < count).astype(jnp.float32)
    return pl.pallas_call(
        stack_kernel,
        out_shape=jax.ShapeDtypeStruct((MAXB, CB, LAG_PART), jnp.float32),
        in_specs=[vmem] * 3,
        out_specs=pl.BlockSpec(memory_space=pl.ANY),
        scratch_shapes=[
            pltpu.VMEM((MAXB, CB, LAG_PART), jnp.float32),
            pltpu.SemaphoreType.DMA((MAXB,)),
        ],
        compiler_params=limit,
        name="stack",
    )(live, expand, parts)


def solution(mesh):
    return jax.shard_map(
        on_device,
        mesh=mesh,
        in_specs=(P(None, "tm", "pairs", None), P(), P()),
        out_specs=P("pairs", None, "tm"),
        check_vma=False,
    )
```

```python
import functools
import math

import jax
import jax.numpy as jnp
import ml_dtypes
import numpy as np
from jax import lax
from jax.experimental import pallas as pl
from jax.experimental.pallas import tpu as pltpu
from jax.sharding import PartitionSpec as P

C = 4096
CB = 128
NF = 1024
FIRST_BIN = 16
FFT_LEN = 8192
LAGS = 2048
SMOOTH = 32
MAXB = 4
HOURS = 8
OWNERS = 32
amp_floor = 0.2

CHIPS = OWNERS // 2
BINS = NF // OWNERS
CHIP_BINS = 2 * BINS
LAG_PART = LAGS // HOURS
RANK_CHIP = 28
RANK_PART = 48
ROWS_CHIP = 2 * RANK_CHIP
ROWS_PART = 2 * RANK_PART
STEP = 2.0 * math.pi / FFT_LEN


def slepian(points, half_width, count):
    n = np.arange(points, dtype=np.float64)
    tri = np.diag(((points - 1) / 2.0 - n) ** 2 * math.cos(2.0 * math.pi * half_width))
    off = n[1:] * (points - n[1:]) / 2.0
    tri = tri + np.diag(off, 1) + np.diag(off, -1)
    vectors = np.linalg.eigh(tri)[1][:, ::-1][:, :count]
    return vectors * np.where(vectors[points // 2] < 0, -1.0, 1.0)


def split_rounded(table):
    high = table.astype(ml_dtypes.bfloat16)
    low = (table - high.astype(np.float64)).astype(ml_dtypes.bfloat16)
    return high, low


def real_form(table):
    return np.block([[table.real, -table.imag], [table.imag, table.real]])


@functools.cache
def tables():
    chip_basis = slepian(CHIP_BINS, LAGS / 2 / FFT_LEN, RANK_CHIP)
    part_basis = slepian(NF, LAG_PART / 2 / FFT_LEN, RANK_PART)
    bins = np.arange(NF) - (NF - 1) / 2.0
    lags = np.arange(LAG_PART) - LAG_PART // 2
    mid_bin = FIRST_BIN + (NF - 1) / 2.0
    compress = np.kron(np.eye(2), chip_basis.T)
    parts = []
    for part in range(HOURS // 2):
        mid_lag = LAG_PART * part - (LAGS - LAG_PART) // 2
        turned = np.exp(1j * STEP * (bins + mid_bin) * mid_lag)[:, None] * part_basis
        turned = turned.reshape(CHIPS, CHIP_BINS, RANK_PART)
        blocks = [(chip_basis.T @ turned[chip]).T for chip in range(CHIPS)]
        parts.append(np.concatenate(blocks, axis=1))
    combine = np.concatenate([half for part in parts for half in (part.real, part.imag)], axis=0)
    waves = np.exp(1j * STEP * np.outer(lags, bins)) @ part_basis
    waves = waves * np.exp(1j * STEP * mid_bin * lags)[:, None] / math.sqrt(NF)
    expand = real_form(waves)
    row = np.arange(BINS)[:, None] + SMOOTH
    column = np.arange(BINS + 2 * SMOOTH)[None, :]
    window = (np.abs(row - column) <= SMOOTH).astype(ml_dtypes.bfloat16)
    turned = [window[:, -SMOOTH:], window[:, SMOOTH:-SMOOTH], window[:, :SMOOTH]]
    window = np.stack([window, np.concatenate(turned, axis=1)])
    halves = np.split(compress, 2 * CHIP_BINS // BINS, axis=1)
    by_core = []
    for core in range(2):
        own, twin = core, 1 - core
        ordered = [halves[own], halves[2 + own], halves[twin], halves[2 + twin]]
        by_core.append(np.concatenate(split_rounded(np.concatenate(ordered, axis=1)), axis=1))
    compress = np.stack(by_core)
    padded = np.zeros((2 * CB, 2 * LAG_PART), ml_dtypes.bfloat16)
    for index, half in enumerate(split_rounded(expand)):
        padded[index * CB : index * CB + ROWS_PART] = half.T
    expand = padded
    return window, compress, split_rounded(combine), expand


def magnitude_of(real, imag):
    real, imag = real.astype(jnp.float32), imag.astype(jnp.float32)
    return jnp.sqrt(real * real + imag * imag).astype(jnp.bfloat16)


def whiten(core, window, source, first, centre, second, white):
    chunk = 512
    weights = window[core]
    for start in range(0, C, chunk):
        lanes = slice(start, start + chunk)
        sizes = jnp.concatenate([first[:, lanes], centre[:, lanes], second[:, lanes]], axis=0)
        sums = jnp.dot(weights, sizes, preferred_element_type=jnp.float32)
        inverse = 1.0 / (sums * (1.0 / (2 * SMOOTH + 1)) + 1e-05)
        for part in range(2):
            value = source[part, :, lanes].astype(jnp.float32) * inverse
            white[part, :, lanes] = value.astype(jnp.bfloat16)


def cross_of(blocks, base, white):
    crossed = []
    for slot in range(MAXB):
        left = pl.ds(pl.multiple_of(blocks[base + 2 * slot] * CB, CB), CB)
        right = pl.ds(pl.multiple_of(blocks[base + 2 * slot + 1] * CB, CB), CB)
        left_re = white[0, :, left].astype(jnp.float32)
        left_im = white[1, :, left].astype(jnp.float32)
        right_re = white[0, :, right].astype(jnp.float32)
        right_im = white[1, :, right].astype(jnp.float32)
        real = left_re * right_re + left_im * right_im
        imag = left_im * right_re - left_re * right_im
        crossed.append(jnp.concatenate([real, imag], axis=0).astype(jnp.bfloat16))
    return jnp.concatenate(crossed, axis=1)


def own_kernel(blocks, window, own, near, own_size, twin_size, out, white):
    core = blocks[CHIPS * 2 * MAXB]
    whiten(core, window, own, near, own_size, twin_size, white)
    for chip in range(CHIPS):
        out[chip] = cross_of(blocks, chip * 2 * MAXB, white)


def twin_kernel(
    blocks, window, compress, twin, own_size, twin_size, far, own_cross, out, white
):
    core = blocks[CHIPS * 2 * MAXB]
    whiten(core, window, twin, own_size, twin_size, far, white)
    weights = compress[core]
    for chip in range(CHIPS):
        twin_cross = cross_of(blocks, chip * 2 * MAXB, white)
        cross = jnp.concatenate([own_cross[chip], twin_cross] * 2, axis=0)
        packed = jnp.dot(weights, cross, preferred_element_type=jnp.float32)
        out[chip] = packed.astype(jnp.bfloat16)


def combine_kernel(high, low, packed, out):
    wide = out.shape[2]
    real = [packed[chip, :RANK_CHIP, :wide] for chip in range(CHIPS)]
    imag = [packed[chip, RANK_CHIP:, :wide] for chip in range(CHIPS)]
    value = jnp.concatenate([jnp.concatenate(real, axis=0), jnp.concatenate(imag, axis=0)], axis=1)
    total = jnp.dot(high[...], value, preferred_element_type=jnp.float32)
    total = total + jnp.dot(low[...], value, preferred_element_type=jnp.float32)
    for part in range(HOURS // 2):
        base = part * ROWS_PART
        real_rows = slice(base, base + RANK_PART)
        imag_rows = slice(base + RANK_PART, base + ROWS_PART)
        real_real, real_imag = total[real_rows, :wide], total[real_rows, wide:]
        imag_real, imag_imag = total[imag_rows, :wide], total[imag_rows, wide:]
        for where, sign in ((part, 1.0), (HOURS - 1 - part, -1.0)):
            both = [real_real - sign * imag_imag, real_imag + sign * imag_real]
            out[where] = jnp.concatenate(both, axis=0).astype(jnp.bfloat16)


def stack_kernel(live, expand, parts, out, result, sems):
    blank = jnp.zeros((CB - ROWS_PART, CB), jnp.bfloat16)
    copies = []
    for slot in range(MAXB):
        lanes = slice(slot * CB, (slot + 1) * CB)
        rows = []
        for hour in range(HOURS):
            part = jnp.concatenate([parts[hour, :, lanes], blank], axis=0).T
            rows.append(jnp.concatenate([part, part], axis=1))
        lagged = jnp.dot(
            jnp.concatenate(rows, axis=0), expand[...], preferred_element_type=jnp.float32
        )
        linear = mean_real = mean_imag = None
        for hour in range(HOURS):
            correlation = lagged[hour * CB : (hour + 1) * CB, :LAG_PART]
            quadrature = lagged[hour * CB : (hour + 1) * CB, LAG_PART:]
            power = correlation * correlation + quadrature * quadrature
            inverse = jnp.minimum(lax.rsqrt(power), 1.0 / amp_floor)
            unit_real = correlation * inverse
            unit_imag = quadrature * inverse
            if hour == 0:
                linear, mean_real, mean_imag = correlation, unit_real, unit_imag
            else:
                linear = linear + correlation
                mean_real = mean_real + unit_real
                mean_imag = mean_imag + unit_imag
        stacked = linear * (mean_real * mean_real + mean_imag * mean_imag) * (1.0 / HOURS**3)
        result[slot] = jnp.where(live[slot] > 0, stacked, jnp.zeros_like(stacked))
        copy = pltpu.make_async_copy(result.at[slot], out.at[slot], sems.at[slot])
        copy.start()
        copies.append(copy)
    for copy in copies:
        copy.wait()


def on_device(spectra, pair_blocks, block_count):
    owner = lax.axis_index("pairs")
    core = owner % 2
    window, compress, (high, low), expand = tables()
    spectra = spectra[:, 0]
    twins = [(i, i ^ 1) for i in range(OWNERS)]
    twin = lax.ppermute(spectra, "pairs", twins)
    own_size = magnitude_of(spectra[0], spectra[1])
    last = OWNERS - 1
    near_pairs = [(i, i + 1) for i in range(1, last, 2)] + [(i, i - 1) for i in range(2, last, 2)]
    near = lax.ppermute(own_size, "pairs", near_pairs)
    twin_size = magnitude_of(twin[0], twin[1])
    near, twin_size = lax.optimization_barrier((near, twin_size))
    far = lax.ppermute(near, "pairs", twins)
    vmem = pl.BlockSpec(memory_space=pltpu.VMEM)
    smem = pl.BlockSpec(memory_space=pltpu.SMEM)
    limit = pltpu.CompilerParams(vmem_limit_bytes=32 * 2**20)
    slots = lax.dynamic_index_in_dim(
        pair_blocks.reshape(CHIPS, 2, 2 * MAXB), core, 1, keepdims=False
    )
    slots = jnp.concatenate([slots.reshape(-1), core[None]])
    count = lax.dynamic_index_in_dim(block_count, owner, 0, keepdims=False)
    live = (lax.broadcasted_iota(jnp.int32, (MAXB, 1, LAG_PART), 0) < count).astype(jnp.float32)
    slots, count, live = lax.optimization_barrier((slots, count, live))
    high, low = lax.optimization_barrier((jnp.asarray(high), jnp.asarray(low)))
    white = pltpu.VMEM((2, BINS, C), jnp.bfloat16)
    own_cross = pl.pallas_call(
        own_kernel,
        out_shape=jax.ShapeDtypeStruct((CHIPS, 2 * BINS, MAXB * CB), jnp.bfloat16),
        in_specs=[smem] + [vmem] * 5,
        out_specs=vmem,
        scratch_shapes=[white],
        compiler_params=limit,
        name="own_cross",
    )(slots, window, spectra, near, own_size, twin_size)
    packed = pl.pallas_call(
        twin_kernel,
        out_shape=jax.ShapeDtypeStruct((CHIPS, ROWS_CHIP, MAXB * CB), jnp.bfloat16),
        in_specs=[smem] + [vmem] * 7,
        out_specs=vmem,
        scratch_shapes=[white],
        compiler_params=limit,
        name="twin_cross",
    )(slots, window, compress, twin, own_size, twin_size, far, own_cross)
    groups = [list(range(0, OWNERS, 2)), list(range(1, OWNERS, 2))]
    packed = lax.all_to_all(packed, "pairs", 0, 0, axis_index_groups=groups, tiled=True)

    def with_live(live):
        def exchange(packed, high, low):
            parts = pl.pallas_call(
                combine_kernel,
                out_shape=jax.ShapeDtypeStruct((HOURS, ROWS_PART, live * CB), jnp.bfloat16),
                in_specs=[vmem] * 3,
                out_specs=vmem,
                compiler_params=limit,
                name=f"combine_{live}",
            )(high, low, packed)
            parts = lax.all_to_all(parts, "tm", 0, 0, tiled=True)
            return jnp.pad(parts, ((0, 0), (0, 0), (0, (MAXB - live) * CB)))

        return exchange

    branches = [with_live(live) for live in range(1, MAXB + 1)]
    parts = lax.switch(count - 1, branches, packed, high, low)
    return pl.pallas_call(
        stack_kernel,
        out_shape=jax.ShapeDtypeStruct((MAXB, CB, LAG_PART), jnp.float32),
        in_specs=[vmem] * 3,
        out_specs=pl.BlockSpec(memory_space=pl.ANY),
        scratch_shapes=[
            pltpu.VMEM((MAXB, CB, LAG_PART), jnp.float32),
            pltpu.SemaphoreType.DMA((MAXB,)),
        ],
        compiler_params=limit,
        name="stack",
    )(live, expand, parts)


def solution(mesh):
    return jax.shard_map(
        on_device,
        mesh=mesh,
        in_specs=(P(None, "tm", "pairs", None), P(), P()),
        out_specs=P("pairs", None, "tm"),
        check_vma=False,
    )
```

```python
import functools
import math

import jax
import jax.numpy as jnp
import ml_dtypes
import numpy as np
from jax import lax
from jax.experimental import pallas as pl
from jax.experimental.pallas import tpu as pltpu
from jax.sharding import PartitionSpec as P

C = 4096
CB = 128
NF = 1024
FIRST_BIN = 16
FFT_LEN = 8192
LAGS = 2048
SMOOTH = 32
MAXB = 4
HOURS = 8
OWNERS = 32
amp_floor = 0.2

CHIPS = OWNERS // 2
BINS = NF // OWNERS
CHIP_BINS = 2 * BINS
LAG_PART = LAGS // HOURS
RANK_CHIP = 28
RANK_PART = 48
ROWS_CHIP = 2 * RANK_CHIP
ROWS_PART = 2 * RANK_PART
STEP = 2.0 * math.pi / FFT_LEN


def slepian(points, half_width, count):
    n = np.arange(points, dtype=np.float64)
    tri = np.diag(((points - 1) / 2.0 - n) ** 2 * math.cos(2.0 * math.pi * half_width))
    off = n[1:] * (points - n[1:]) / 2.0
    tri = tri + np.diag(off, 1) + np.diag(off, -1)
    vectors = np.linalg.eigh(tri)[1][:, ::-1][:, :count]
    return vectors * np.where(vectors[points // 2] < 0, -1.0, 1.0)


def split_rounded(table):
    high = table.astype(ml_dtypes.bfloat16)
    low = (table - high.astype(np.float64)).astype(ml_dtypes.bfloat16)
    return high, low


def real_form(table):
    return np.block([[table.real, -table.imag], [table.imag, table.real]])


@functools.cache
def tables():
    chip_basis = slepian(CHIP_BINS, LAGS / 2 / FFT_LEN, RANK_CHIP)
    part_basis = slepian(NF, LAG_PART / 2 / FFT_LEN, RANK_PART)
    bins = np.arange(NF) - (NF - 1) / 2.0
    lags = np.arange(LAG_PART) - LAG_PART // 2
    mid_bin = FIRST_BIN + (NF - 1) / 2.0
    compress = np.kron(np.eye(2), chip_basis.T)
    parts = []
    for part in range(HOURS // 2):
        mid_lag = LAG_PART * part - (LAGS - LAG_PART) // 2
        turned = np.exp(1j * STEP * (bins + mid_bin) * mid_lag)[:, None] * part_basis
        turned = turned.reshape(CHIPS, CHIP_BINS, RANK_PART)
        blocks = [(chip_basis.T @ turned[chip]).T for chip in range(CHIPS)]
        parts.append(np.concatenate(blocks, axis=1))
    combine = np.concatenate([half for part in parts for half in (part.real, part.imag)], axis=0)
    waves = np.exp(1j * STEP * np.outer(lags, bins)) @ part_basis
    waves = waves * np.exp(1j * STEP * mid_bin * lags)[:, None] / math.sqrt(NF)
    expand = real_form(waves)
    row = np.arange(BINS)[:, None] + SMOOTH
    column = np.arange(BINS + 2 * SMOOTH)[None, :]
    window = (np.abs(row - column) <= SMOOTH).astype(ml_dtypes.bfloat16)
    turned = [window[:, -SMOOTH:], window[:, SMOOTH:-SMOOTH], window[:, :SMOOTH]]
    window = np.stack([window, np.concatenate(turned, axis=1)])
    halves = np.split(compress, 2 * CHIP_BINS // BINS, axis=1)
    by_core = []
    for core in range(2):
        own, twin = core, 1 - core
        ordered = [halves[own], halves[2 + own], halves[twin], halves[2 + twin]]
        by_core.append(np.concatenate(split_rounded(np.concatenate(ordered, axis=1)), axis=1))
    compress = np.stack(by_core)
    padded = np.zeros((2 * CB, 2 * LAG_PART), ml_dtypes.bfloat16)
    for index, half in enumerate(split_rounded(expand)):
        padded[index * CB : index * CB + ROWS_PART] = half.T
    expand = padded
    return window, compress, split_rounded(combine), expand


def magnitude_of(real, imag):
    real, imag = real.astype(jnp.float32), imag.astype(jnp.float32)
    return jnp.sqrt(real * real + imag * imag).astype(jnp.bfloat16)


def whiten(core, window, source, first, centre, second, white):
    chunk = 512
    weights = window[core]
    for start in range(0, C, chunk):
        lanes = slice(start, start + chunk)
        sizes = jnp.concatenate([first[:, lanes], centre[:, lanes], second[:, lanes]], axis=0)
        sums = jnp.dot(weights, sizes, preferred_element_type=jnp.float32)
        inverse = 1.0 / (sums * (1.0 / (2 * SMOOTH + 1)) + 1e-05)
        for part in range(2):
            value = source[part, :, lanes].astype(jnp.float32) * inverse
            white[part, :, lanes] = value.astype(jnp.bfloat16)


def cross_of(blocks, base, white):
    crossed = []
    for slot in range(MAXB):
        left = pl.ds(pl.multiple_of(blocks[base + 2 * slot] * CB, CB), CB)
        right = pl.ds(pl.multiple_of(blocks[base + 2 * slot + 1] * CB, CB), CB)
        left_re = white[0, :, left].astype(jnp.float32)
        left_im = white[1, :, left].astype(jnp.float32)
        right_re = white[0, :, right].astype(jnp.float32)
        right_im = white[1, :, right].astype(jnp.float32)
        real = left_re * right_re + left_im * right_im
        imag = left_im * right_re - left_re * right_im
        crossed.append(jnp.concatenate([real, imag], axis=0).astype(jnp.bfloat16))
    return jnp.concatenate(crossed, axis=1)


def own_kernel(blocks, branch, window, own, near, own_size, twin_size, out, white):
    core = blocks[CHIPS * 2 * MAXB]
    whiten(core, window, own, near, own_size, twin_size, white)
    for chip in range(CHIPS):
        out[chip] = cross_of(blocks, chip * 2 * MAXB, white)


def twin_kernel(
    blocks, window, compress, twin, own_size, twin_size, far, own_cross, out, white
):
    core = blocks[CHIPS * 2 * MAXB]
    whiten(core, window, twin, own_size, twin_size, far, white)
    weights = compress[core]
    for chip in range(CHIPS):
        twin_cross = cross_of(blocks, chip * 2 * MAXB, white)
        cross = jnp.concatenate([own_cross[chip], twin_cross] * 2, axis=0)
        packed = jnp.dot(weights, cross, preferred_element_type=jnp.float32)
        out[chip] = packed.astype(jnp.bfloat16)


def combine_kernel(high, low, packed, out):
    wide = out.shape[2]
    real = [packed[chip, :RANK_CHIP, :wide] for chip in range(CHIPS)]
    imag = [packed[chip, RANK_CHIP:, :wide] for chip in range(CHIPS)]
    value = jnp.concatenate([jnp.concatenate(real, axis=0), jnp.concatenate(imag, axis=0)], axis=1)
    total = jnp.dot(high[...], value, preferred_element_type=jnp.float32)
    total = total + jnp.dot(low[...], value, preferred_element_type=jnp.float32)
    for part in range(HOURS // 2):
        base = part * ROWS_PART
        real_rows = slice(base, base + RANK_PART)
        imag_rows = slice(base + RANK_PART, base + ROWS_PART)
        real_real, real_imag = total[real_rows, :wide], total[real_rows, wide:]
        imag_real, imag_imag = total[imag_rows, :wide], total[imag_rows, wide:]
        for where, sign in ((part, 1.0), (HOURS - 1 - part, -1.0)):
            both = [real_real - sign * imag_imag, real_imag + sign * imag_real]
            out[where] = jnp.concatenate(both, axis=0).astype(jnp.bfloat16)


def stack_kernel(live, expand, parts, out, result, sems):
    blank = jnp.zeros((CB - ROWS_PART, CB), jnp.bfloat16)
    copies = []
    for slot in range(MAXB):
        lanes = slice(slot * CB, (slot + 1) * CB)
        rows = []
        for hour in range(HOURS):
            part = jnp.concatenate([parts[hour, :, lanes], blank], axis=0).T
            rows.append(jnp.concatenate([part, part], axis=1))
        lagged = jnp.dot(
            jnp.concatenate(rows, axis=0), expand[...], preferred_element_type=jnp.float32
        )
        linear = mean_real = mean_imag = None
        for hour in range(HOURS):
            correlation = lagged[hour * CB : (hour + 1) * CB, :LAG_PART]
            quadrature = lagged[hour * CB : (hour + 1) * CB, LAG_PART:]
            power = correlation * correlation + quadrature * quadrature
            inverse = jnp.minimum(lax.rsqrt(power), 1.0 / amp_floor)
            unit_real = correlation * inverse
            unit_imag = quadrature * inverse
            if hour == 0:
                linear, mean_real, mean_imag = correlation, unit_real, unit_imag
            else:
                linear = linear + correlation
                mean_real = mean_real + unit_real
                mean_imag = mean_imag + unit_imag
        stacked = linear * (mean_real * mean_real + mean_imag * mean_imag) * (1.0 / HOURS**3)
        result[slot] = jnp.where(live[slot] > 0, stacked, jnp.zeros_like(stacked))
        copy = pltpu.make_async_copy(result.at[slot], out.at[slot], sems.at[slot])
        copy.start()
        copies.append(copy)
    for copy in copies:
        copy.wait()


def on_device(spectra, pair_blocks, block_count):
    owner = lax.axis_index("pairs")
    core = owner % 2
    window, compress, (high, low), expand = tables()
    spectra = spectra[:, 0]
    twins = [(i, i ^ 1) for i in range(OWNERS)]
    twin = lax.ppermute(spectra, "pairs", twins)
    own_size = magnitude_of(spectra[0], spectra[1])
    last = OWNERS - 1
    near_pairs = [(i, i + 1) for i in range(1, last, 2)] + [(i, i - 1) for i in range(2, last, 2)]
    near = lax.ppermute(own_size, "pairs", near_pairs)
    twin_size = magnitude_of(twin[0], twin[1])
    slots = lax.dynamic_index_in_dim(
        pair_blocks.reshape(CHIPS, 2, 2 * MAXB), core, 1, keepdims=False
    )
    slots = jnp.concatenate([slots.reshape(-1), core[None]])
    count = lax.dynamic_index_in_dim(block_count, owner, 0, keepdims=False)
    live = (lax.broadcasted_iota(jnp.int32, (MAXB, 1, LAG_PART), 0) < count).astype(jnp.float32)
    near, twin_size, slots, count, live = lax.optimization_barrier(
        (near, twin_size, slots, count, live)
    )
    far = lax.ppermute(near, "pairs", twins)
    branch = lax.clamp(jnp.int32(0), count - 1, jnp.int32(MAXB - 1))
    vmem = pl.BlockSpec(memory_space=pltpu.VMEM)
    smem = pl.BlockSpec(memory_space=pltpu.SMEM)
    limit = pltpu.CompilerParams(vmem_limit_bytes=32 * 2**20)
    high, low = lax.optimization_barrier((jnp.asarray(high), jnp.asarray(low)))
    white = pltpu.VMEM((2, BINS, C), jnp.bfloat16)
    own_cross = pl.pallas_call(
        own_kernel,
        out_shape=jax.ShapeDtypeStruct((CHIPS, 2 * BINS, MAXB * CB), jnp.bfloat16),
        in_specs=[smem] * 2 + [vmem] * 5,
        out_specs=vmem,
        scratch_shapes=[white],
        compiler_params=limit,
        name="own_cross",
    )(slots, branch[None], window, spectra, near, own_size, twin_size)
    packed = pl.pallas_call(
        twin_kernel,
        out_shape=jax.ShapeDtypeStruct((CHIPS, ROWS_CHIP, MAXB * CB), jnp.bfloat16),
        in_specs=[smem] + [vmem] * 7,
        out_specs=vmem,
        scratch_shapes=[white],
        compiler_params=limit,
        name="twin_cross",
    )(slots, window, compress, twin, own_size, twin_size, far, own_cross)
    groups = [list(range(0, OWNERS, 2)), list(range(1, OWNERS, 2))]
    packed = lax.all_to_all(packed, "pairs", 0, 0, axis_index_groups=groups, tiled=True)

    def with_live(live):
        def exchange(packed, high, low):
            parts = pl.pallas_call(
                combine_kernel,
                out_shape=jax.ShapeDtypeStruct((HOURS, ROWS_PART, live * CB), jnp.bfloat16),
                in_specs=[vmem] * 3,
                out_specs=vmem,
                compiler_params=limit,
                name=f"combine_{live}",
            )(high, low, packed)
            parts = lax.all_to_all(parts, "tm", 0, 0, tiled=True)
            return jnp.pad(parts, ((0, 0), (0, 0), (0, (MAXB - live) * CB)))

        return exchange

    branches = [with_live(live) for live in range(1, MAXB + 1)]
    parts = lax.switch(count - 1, branches, packed, high, low)
    return pl.pallas_call(
        stack_kernel,
        out_shape=jax.ShapeDtypeStruct((MAXB, CB, LAG_PART), jnp.float32),
        in_specs=[vmem] * 3,
        out_specs=pl.BlockSpec(memory_space=pl.ANY),
        scratch_shapes=[
            pltpu.VMEM((MAXB, CB, LAG_PART), jnp.float32),
            pltpu.SemaphoreType.DMA((MAXB,)),
        ],
        compiler_params=limit,
        name="stack",
    )(live, expand, parts)


def solution(mesh):
    return jax.shard_map(
        on_device,
        mesh=mesh,
        in_specs=(P(None, "tm", "pairs", None), P(), P()),
        out_specs=P("pairs", None, "tm"),
        check_vma=False,
    )
```

```python
import functools
import math

import jax
import jax.numpy as jnp
import ml_dtypes
import numpy as np
from jax import lax
from jax.experimental import pallas as pl
from jax.experimental.pallas import tpu as pltpu
from jax.sharding import PartitionSpec as P

C = 4096
CB = 128
NF = 1024
FIRST_BIN = 16
FFT_LEN = 8192
LAGS = 2048
SMOOTH = 32
MAXB = 4
HOURS = 8
OWNERS = 32
amp_floor = 0.2

CHIPS = OWNERS // 2
BINS = NF // OWNERS
CHIP_BINS = 2 * BINS
LAG_PART = LAGS // HOURS
RANK_CHIP = 28
RANK_PART = 48
ROWS_CHIP = 2 * RANK_CHIP
ROWS_PART = 2 * RANK_PART
STEP = 2.0 * math.pi / FFT_LEN


def slepian(points, half_width, count):
    n = np.arange(points, dtype=np.float64)
    tri = np.diag(((points - 1) / 2.0 - n) ** 2 * math.cos(2.0 * math.pi * half_width))
    off = n[1:] * (points - n[1:]) / 2.0
    tri = tri + np.diag(off, 1) + np.diag(off, -1)
    vectors = np.linalg.eigh(tri)[1][:, ::-1][:, :count]
    return vectors * np.where(vectors[points // 2] < 0, -1.0, 1.0)


def split_rounded(table):
    high = table.astype(ml_dtypes.bfloat16)
    low = (table - high.astype(np.float64)).astype(ml_dtypes.bfloat16)
    return high, low


def real_form(table):
    return np.block([[table.real, -table.imag], [table.imag, table.real]])


@functools.cache
def tables():
    chip_basis = slepian(CHIP_BINS, LAGS / 2 / FFT_LEN, RANK_CHIP)
    part_basis = slepian(NF, LAG_PART / 2 / FFT_LEN, RANK_PART)
    bins = np.arange(NF) - (NF - 1) / 2.0
    lags = np.arange(LAG_PART) - LAG_PART // 2
    mid_bin = FIRST_BIN + (NF - 1) / 2.0
    compress = np.kron(np.eye(2), chip_basis.T)
    parts = []
    for part in range(HOURS // 2):
        mid_lag = LAG_PART * part - (LAGS - LAG_PART) // 2
        turned = np.exp(1j * STEP * (bins + mid_bin) * mid_lag)[:, None] * part_basis
        turned = turned.reshape(CHIPS, CHIP_BINS, RANK_PART)
        blocks = [(chip_basis.T @ turned[chip]).T for chip in range(CHIPS)]
        parts.append(np.concatenate(blocks, axis=1))
    combine = np.concatenate([half for part in parts for half in (part.real, part.imag)], axis=0)
    waves = np.exp(1j * STEP * np.outer(lags, bins)) @ part_basis
    waves = waves * np.exp(1j * STEP * mid_bin * lags)[:, None] / math.sqrt(NF)
    expand = real_form(waves)
    row = np.arange(BINS)[:, None] + SMOOTH
    column = np.arange(BINS + 2 * SMOOTH)[None, :]
    window = (np.abs(row - column) <= SMOOTH).astype(ml_dtypes.bfloat16)
    turned = [window[:, -SMOOTH:], window[:, SMOOTH:-SMOOTH], window[:, :SMOOTH]]
    window = np.stack([window, np.concatenate(turned, axis=1)])
    halves = np.split(compress, 2 * CHIP_BINS // BINS, axis=1)
    by_core = []
    for core in range(2):
        own, twin = core, 1 - core
        ordered = [halves[own], halves[2 + own], halves[twin], halves[2 + twin]]
        by_core.append(np.concatenate(split_rounded(np.concatenate(ordered, axis=1)), axis=1))
    compress = np.stack(by_core)
    padded = np.zeros((2 * CB, 2 * LAG_PART), ml_dtypes.bfloat16)
    for index, half in enumerate(split_rounded(expand)):
        padded[index * CB : index * CB + ROWS_PART] = half.T
    expand = padded
    return window, compress, split_rounded(combine), expand


def magnitude_of(real, imag):
    real, imag = real.astype(jnp.float32), imag.astype(jnp.float32)
    return jnp.sqrt(real * real + imag * imag).astype(jnp.bfloat16)


def whiten(core, window, source, first, centre, second, white):
    chunk = 512
    weights = window[core]
    for start in range(0, C, chunk):
        lanes = slice(start, start + chunk)
        sizes = jnp.concatenate([first[:, lanes], centre[:, lanes], second[:, lanes]], axis=0)
        sums = jnp.dot(weights, sizes, preferred_element_type=jnp.float32)
        inverse = 1.0 / (sums * (1.0 / (2 * SMOOTH + 1)) + 1e-05)
        for part in range(2):
            value = source[part, :, lanes].astype(jnp.float32) * inverse
            white[part, :, lanes] = value.astype(jnp.bfloat16)


def cross_of(blocks, base, white):
    crossed = []
    for slot in range(MAXB):
        left = pl.ds(pl.multiple_of(blocks[base + 2 * slot] * CB, CB), CB)
        right = pl.ds(pl.multiple_of(blocks[base + 2 * slot + 1] * CB, CB), CB)
        left_re = white[0, :, left].astype(jnp.float32)
        left_im = white[1, :, left].astype(jnp.float32)
        right_re = white[0, :, right].astype(jnp.float32)
        right_im = white[1, :, right].astype(jnp.float32)
        real = left_re * right_re + left_im * right_im
        imag = left_im * right_re - left_re * right_im
        crossed.append(jnp.concatenate([real, imag], axis=0).astype(jnp.bfloat16))
    return jnp.concatenate(crossed, axis=1)


def own_kernel(blocks, window, own, near, own_size, twin_size, out, white):
    core = blocks[CHIPS * 2 * MAXB]
    whiten(core, window, own, near, own_size, twin_size, white)
    for chip in range(CHIPS):
        out[chip] = cross_of(blocks, chip * 2 * MAXB, white)


def twin_kernel(
    blocks, window, compress, twin, own_size, twin_size, far, own_cross, out, white, result, sems
):
    core = blocks[CHIPS * 2 * MAXB]
    whiten(core, window, twin, own_size, twin_size, far, white)
    weights = compress[core]
    copies = []
    for chip in range(CHIPS):
        twin_cross = cross_of(blocks, chip * 2 * MAXB, white)
        cross = jnp.concatenate([own_cross[chip], twin_cross] * 2, axis=0)
        packed = jnp.dot(weights, cross, preferred_element_type=jnp.float32)
        result[chip] = packed.astype(jnp.bfloat16)
        copy = pltpu.make_async_copy(result.at[chip], out.at[chip], sems.at[chip])
        copy.start()
        copies.append(copy)
    for copy in copies:
        copy.wait()


def combine_kernel(high, low, packed, out):
    wide = out.shape[2]
    real = [packed[chip, :RANK_CHIP, :wide] for chip in range(CHIPS)]
    imag = [packed[chip, RANK_CHIP:, :wide] for chip in range(CHIPS)]
    value = jnp.concatenate([jnp.concatenate(real, axis=0), jnp.concatenate(imag, axis=0)], axis=1)
    total = jnp.dot(high[...], value, preferred_element_type=jnp.float32)
    total = total + jnp.dot(low[...], value, preferred_element_type=jnp.float32)
    for part in range(HOURS // 2):
        base = part * ROWS_PART
        real_rows = slice(base, base + RANK_PART)
        imag_rows = slice(base + RANK_PART, base + ROWS_PART)
        real_real, real_imag = total[real_rows, :wide], total[real_rows, wide:]
        imag_real, imag_imag = total[imag_rows, :wide], total[imag_rows, wide:]
        for where, sign in ((part, 1.0), (HOURS - 1 - part, -1.0)):
            both = [real_real - sign * imag_imag, real_imag + sign * imag_real]
            out[where] = jnp.concatenate(both, axis=0).astype(jnp.bfloat16)


def stack_kernel(live, expand, parts, out, result, sems):
    blank = jnp.zeros((CB - ROWS_PART, CB), jnp.bfloat16)
    copies = []
    for slot in range(MAXB):
        lanes = slice(slot * CB, (slot + 1) * CB)
        rows = []
        for hour in range(HOURS):
            part = jnp.concatenate([parts[hour, :, lanes], blank], axis=0).T
            rows.append(jnp.concatenate([part, part], axis=1))
        lagged = jnp.dot(
            jnp.concatenate(rows, axis=0), expand[...], preferred_element_type=jnp.float32
        )
        linear = mean_real = mean_imag = None
        for hour in range(HOURS):
            correlation = lagged[hour * CB : (hour + 1) * CB, :LAG_PART]
            quadrature = lagged[hour * CB : (hour + 1) * CB, LAG_PART:]
            power = correlation * correlation + quadrature * quadrature
            inverse = jnp.minimum(lax.rsqrt(power), 1.0 / amp_floor)
            unit_real = correlation * inverse
            unit_imag = quadrature * inverse
            if hour == 0:
                linear, mean_real, mean_imag = correlation, unit_real, unit_imag
            else:
                linear = linear + correlation
                mean_real = mean_real + unit_real
                mean_imag = mean_imag + unit_imag
        stacked = linear * (mean_real * mean_real + mean_imag * mean_imag) * (1.0 / HOURS**3)
        result[slot] = jnp.where(live[slot] > 0, stacked, jnp.zeros_like(stacked))
        copy = pltpu.make_async_copy(result.at[slot], out.at[slot], sems.at[slot])
        copy.start()
        copies.append(copy)
    for copy in copies:
        copy.wait()


def on_device(spectra, pair_blocks, block_count):
    owner = lax.axis_index("pairs")
    core = owner % 2
    window, compress, (high, low), expand = tables()
    spectra = spectra[:, 0]
    twins = [(i, i ^ 1) for i in range(OWNERS)]
    twin = lax.ppermute(spectra, "pairs", twins)
    own_size = magnitude_of(spectra[0], spectra[1])
    last = OWNERS - 1
    near_pairs = [(i, i + 1) for i in range(1, last, 2)] + [(i, i - 1) for i in range(2, last, 2)]
    near = lax.ppermute(own_size, "pairs", near_pairs)
    twin_size = magnitude_of(twin[0], twin[1])
    slots = lax.dynamic_index_in_dim(
        pair_blocks.reshape(CHIPS, 2, 2 * MAXB), core, 1, keepdims=False
    )
    slots = jnp.concatenate([slots.reshape(-1), core[None]])
    count = lax.dynamic_index_in_dim(block_count, owner, 0, keepdims=False)
    live = (lax.broadcasted_iota(jnp.int32, (MAXB, 1, LAG_PART), 0) < count).astype(jnp.float32)
    near, twin_size, slots, count, live = lax.optimization_barrier(
        (near, twin_size, slots, count, live)
    )
    far = lax.ppermute(near, "pairs", twins)
    vmem = pl.BlockSpec(memory_space=pltpu.VMEM)
    smem = pl.BlockSpec(memory_space=pltpu.SMEM)
    limit = pltpu.CompilerParams(vmem_limit_bytes=32 * 2**20)
    high, low = lax.optimization_barrier((jnp.asarray(high), jnp.asarray(low)))
    white = pltpu.VMEM((2, BINS, C), jnp.bfloat16)
    own_cross = pl.pallas_call(
        own_kernel,
        out_shape=jax.ShapeDtypeStruct((CHIPS, 2 * BINS, MAXB * CB), jnp.bfloat16),
        in_specs=[smem] + [vmem] * 5,
        out_specs=vmem,
        scratch_shapes=[white],
        compiler_params=limit,
        name="own_cross",
    )(slots, window, spectra, near, own_size, twin_size)
    packed = pl.pallas_call(
        twin_kernel,
        out_shape=jax.ShapeDtypeStruct((CHIPS, ROWS_CHIP, MAXB * CB), jnp.bfloat16),
        in_specs=[smem] + [vmem] * 7,
        out_specs=pl.BlockSpec(memory_space=pl.ANY),
        scratch_shapes=[
            white,
            pltpu.VMEM((CHIPS, ROWS_CHIP, MAXB * CB), jnp.bfloat16),
            pltpu.SemaphoreType.DMA((CHIPS,)),
        ],
        compiler_params=limit,
        name="twin_cross",
    )(slots, window, compress, twin, own_size, twin_size, far, own_cross)
    groups = [list(range(0, OWNERS, 2)), list(range(1, OWNERS, 2))]
    packed = lax.all_to_all(packed, "pairs", 0, 0, axis_index_groups=groups, tiled=True)

    def with_live(live):
        def exchange(packed, high, low):
            parts = pl.pallas_call(
                combine_kernel,
                out_shape=jax.ShapeDtypeStruct((HOURS, ROWS_PART, live * CB), jnp.bfloat16),
                in_specs=[vmem] * 3,
                out_specs=vmem,
                compiler_params=limit,
                name=f"combine_{live}",
            )(high, low, packed)
            parts = lax.all_to_all(parts, "tm", 0, 0, tiled=True)
            return jnp.pad(parts, ((0, 0), (0, 0), (0, (MAXB - live) * CB)))

        return exchange

    branches = [with_live(live) for live in range(1, MAXB + 1)]
    parts = lax.switch(count - 1, branches, packed, high, low)
    return pl.pallas_call(
        stack_kernel,
        out_shape=jax.ShapeDtypeStruct((MAXB, CB, LAG_PART), jnp.float32),
        in_specs=[vmem] * 3,
        out_specs=pl.BlockSpec(memory_space=pl.ANY),
        scratch_shapes=[
            pltpu.VMEM((MAXB, CB, LAG_PART), jnp.float32),
            pltpu.SemaphoreType.DMA((MAXB,)),
        ],
        compiler_params=limit,
        name="stack",
    )(live, expand, parts)


def solution(mesh):
    return jax.shard_map(
        on_device,
        mesh=mesh,
        in_specs=(P(None, "tm", "pairs", None), P(), P()),
        out_specs=P("pairs", None, "tm"),
        check_vma=False,
    )
```

```python
import functools
import math

import jax
import jax.numpy as jnp
import ml_dtypes
import numpy as np
from jax import lax
from jax.experimental import pallas as pl
from jax.experimental.pallas import tpu as pltpu
from jax.sharding import PartitionSpec as P

C = 4096
CB = 128
NF = 1024
FIRST_BIN = 16
FFT_LEN = 8192
LAGS = 2048
SMOOTH = 32
MAXB = 4
HOURS = 8
OWNERS = 32
amp_floor = 0.2

CHIPS = OWNERS // 2
BINS = NF // OWNERS
CHIP_BINS = 2 * BINS
LAG_PART = LAGS // HOURS
RANK_CHIP = 28
RANK_PART = 48
ROWS_CHIP = 2 * RANK_CHIP
ROWS_PART = 2 * RANK_PART
STEP = 2.0 * math.pi / FFT_LEN


def slepian(points, half_width, count):
    n = np.arange(points, dtype=np.float64)
    tri = np.diag(((points - 1) / 2.0 - n) ** 2 * math.cos(2.0 * math.pi * half_width))
    off = n[1:] * (points - n[1:]) / 2.0
    tri = tri + np.diag(off, 1) + np.diag(off, -1)
    vectors = np.linalg.eigh(tri)[1][:, ::-1][:, :count]
    return vectors * np.where(vectors[points // 2] < 0, -1.0, 1.0)


def split_rounded(table):
    high = table.astype(ml_dtypes.bfloat16)
    low = (table - high.astype(np.float64)).astype(ml_dtypes.bfloat16)
    return high, low


def real_form(table):
    return np.block([[table.real, -table.imag], [table.imag, table.real]])


@functools.cache
def tables():
    chip_basis = slepian(CHIP_BINS, LAGS / 2 / FFT_LEN, RANK_CHIP)
    part_basis = slepian(NF, LAG_PART / 2 / FFT_LEN, RANK_PART)
    bins = np.arange(NF) - (NF - 1) / 2.0
    lags = np.arange(LAG_PART) - LAG_PART // 2
    mid_bin = FIRST_BIN + (NF - 1) / 2.0
    compress = np.kron(np.eye(2), chip_basis.T)
    parts = []
    for part in range(HOURS // 2):
        mid_lag = LAG_PART * part - (LAGS - LAG_PART) // 2
        turned = np.exp(1j * STEP * (bins + mid_bin) * mid_lag)[:, None] * part_basis
        turned = turned.reshape(CHIPS, CHIP_BINS, RANK_PART)
        blocks = [(chip_basis.T @ turned[chip]).T for chip in range(CHIPS)]
        parts.append(np.concatenate(blocks, axis=1))
    combine = np.concatenate([half for part in parts for half in (part.real, part.imag)], axis=0)
    waves = np.exp(1j * STEP * np.outer(lags, bins)) @ part_basis
    waves = waves * np.exp(1j * STEP * mid_bin * lags)[:, None] / math.sqrt(NF)
    expand = real_form(waves)
    row = np.arange(BINS)[:, None] + SMOOTH
    column = np.arange(BINS + 2 * SMOOTH)[None, :]
    window = (np.abs(row - column) <= SMOOTH).astype(ml_dtypes.bfloat16)
    turned = [window[:, -SMOOTH:], window[:, SMOOTH:-SMOOTH], window[:, :SMOOTH]]
    window = np.stack([window, np.concatenate(turned, axis=1)])
    halves = np.split(compress, 2 * CHIP_BINS // BINS, axis=1)
    by_core = []
    for core in range(2):
        own, twin = core, 1 - core
        ordered = [halves[own], halves[2 + own], halves[twin], halves[2 + twin]]
        by_core.append(np.concatenate(split_rounded(np.concatenate(ordered, axis=1)), axis=1))
    compress = np.stack(by_core)
    padded = np.zeros((2 * CB, 2 * LAG_PART), ml_dtypes.bfloat16)
    for index, half in enumerate(split_rounded(expand)):
        padded[index * CB : index * CB + ROWS_PART] = half.T
    expand = padded
    return window, compress, split_rounded(combine), expand


def magnitude_of(real, imag):
    real, imag = real.astype(jnp.float32), imag.astype(jnp.float32)
    return jnp.sqrt(real * real + imag * imag).astype(jnp.bfloat16)


def whiten(core, window, source, first, centre, second, white):
    chunk = 512
    weights = window[core]
    for start in range(0, C, chunk):
        lanes = slice(start, start + chunk)
        sizes = jnp.concatenate([first[:, lanes], centre[:, lanes], second[:, lanes]], axis=0)
        sums = jnp.dot(weights, sizes, preferred_element_type=jnp.float32)
        inverse = 1.0 / (sums * (1.0 / (2 * SMOOTH + 1)) + 1e-05)
        for part in range(2):
            value = source[part, :, lanes].astype(jnp.float32) * inverse
            white[part, :, lanes] = value.astype(jnp.bfloat16)


def cross_of(blocks, base, white):
    crossed = []
    for slot in range(MAXB):
        left = pl.ds(pl.multiple_of(blocks[base + 2 * slot] * CB, CB), CB)
        right = pl.ds(pl.multiple_of(blocks[base + 2 * slot + 1] * CB, CB), CB)
        left_re = white[0, :, left].astype(jnp.float32)
        left_im = white[1, :, left].astype(jnp.float32)
        right_re = white[0, :, right].astype(jnp.float32)
        right_im = white[1, :, right].astype(jnp.float32)
        real = left_re * right_re + left_im * right_im
        imag = left_im * right_re - left_re * right_im
        crossed.append(jnp.concatenate([real, imag], axis=0).astype(jnp.bfloat16))
    return jnp.concatenate(crossed, axis=1)


def own_kernel(blocks, most, count, window, own, near, own_size, twin_size, out, white):
    core = blocks[CHIPS * 2 * MAXB]
    whiten(core, window, own, near, own_size, twin_size, white)
    for chip in range(CHIPS):
        out[chip] = cross_of(blocks, chip * 2 * MAXB, white)


def twin_kernel(
    blocks, window, compress, twin, own_size, twin_size, far, own_cross, out, white
):
    core = blocks[CHIPS * 2 * MAXB]
    whiten(core, window, twin, own_size, twin_size, far, white)
    weights = compress[core]
    for chip in range(CHIPS):
        twin_cross = cross_of(blocks, chip * 2 * MAXB, white)
        cross = jnp.concatenate([own_cross[chip], twin_cross] * 2, axis=0)
        packed = jnp.dot(weights, cross, preferred_element_type=jnp.float32)
        out[chip] = packed.astype(jnp.bfloat16)


def combine_kernel(high, low, packed, out):
    wide = out.shape[2]
    real = [packed[chip, :RANK_CHIP, :wide] for chip in range(CHIPS)]
    imag = [packed[chip, RANK_CHIP:, :wide] for chip in range(CHIPS)]
    value = jnp.concatenate([jnp.concatenate(real, axis=0), jnp.concatenate(imag, axis=0)], axis=1)
    total = jnp.dot(high[...], value, preferred_element_type=jnp.float32)
    total = total + jnp.dot(low[...], value, preferred_element_type=jnp.float32)
    for part in range(HOURS // 2):
        base = part * ROWS_PART
        real_rows = slice(base, base + RANK_PART)
        imag_rows = slice(base + RANK_PART, base + ROWS_PART)
        real_real, real_imag = total[real_rows, :wide], total[real_rows, wide:]
        imag_real, imag_imag = total[imag_rows, :wide], total[imag_rows, wide:]
        for where, sign in ((part, 1.0), (HOURS - 1 - part, -1.0)):
            both = [real_real - sign * imag_imag, real_imag + sign * imag_real]
            out[where] = jnp.concatenate(both, axis=0).astype(jnp.bfloat16)


def stack_kernel(live, expand, parts, out, result, sems):
    blank = jnp.zeros((CB - ROWS_PART, CB), jnp.bfloat16)
    copies = []
    for slot in range(MAXB):
        lanes = slice(slot * CB, (slot + 1) * CB)
        rows = []
        for hour in range(HOURS):
            part = jnp.concatenate([parts[hour, :, lanes], blank], axis=0).T
            rows.append(jnp.concatenate([part, part], axis=1))
        lagged = jnp.dot(
            jnp.concatenate(rows, axis=0), expand[...], preferred_element_type=jnp.float32
        )
        linear = mean_real = mean_imag = None
        for hour in range(HOURS):
            correlation = lagged[hour * CB : (hour + 1) * CB, :LAG_PART]
            quadrature = lagged[hour * CB : (hour + 1) * CB, LAG_PART:]
            power = correlation * correlation + quadrature * quadrature
            inverse = jnp.minimum(lax.rsqrt(power), 1.0 / amp_floor)
            unit_real = correlation * inverse
            unit_imag = quadrature * inverse
            if hour == 0:
                linear, mean_real, mean_imag = correlation, unit_real, unit_imag
            else:
                linear = linear + correlation
                mean_real = mean_real + unit_real
                mean_imag = mean_imag + unit_imag
        stacked = linear * (mean_real * mean_real + mean_imag * mean_imag) * (1.0 / HOURS**3)
        result[slot] = jnp.where(live[slot] > 0, stacked, jnp.zeros_like(stacked))
        copy = pltpu.make_async_copy(result.at[slot], out.at[slot], sems.at[slot])
        copy.start()
        copies.append(copy)
    for copy in copies:
        copy.wait()


def on_device(spectra, pair_blocks, block_count):
    owner = lax.axis_index("pairs")
    core = owner % 2
    window, compress, (high, low), expand = tables()
    spectra = spectra[:, 0]
    twins = [(i, i ^ 1) for i in range(OWNERS)]
    twin = lax.ppermute(spectra, "pairs", twins)
    own_size = magnitude_of(spectra[0], spectra[1])
    last = OWNERS - 1
    near_pairs = [(i, i + 1) for i in range(1, last, 2)] + [(i, i - 1) for i in range(2, last, 2)]
    near = lax.ppermute(own_size, "pairs", near_pairs)
    twin_size = magnitude_of(twin[0], twin[1])
    slots = lax.dynamic_index_in_dim(
        pair_blocks.reshape(CHIPS, 2, 2 * MAXB), core, 1, keepdims=False
    )
    slots = jnp.concatenate([slots.reshape(-1), core[None]])
    count = lax.dynamic_index_in_dim(block_count, owner, 0, keepdims=False)
    live = (lax.broadcasted_iota(jnp.int32, (MAXB, 1, LAG_PART), 0) < count).astype(jnp.float32)
    most = jnp.max(jnp.where(lax.iota(jnp.int32, OWNERS) % 2 == core, block_count, 0))
    first, last_live = jnp.int32(0), jnp.int32(MAXB - 1)
    branches = [lax.clamp(first, value - 1, last_live) for value in (most, count)]
    near, twin_size, slots, live, *branches = lax.optimization_barrier(
        (near, twin_size, slots, live, *branches)
    )
    far = lax.ppermute(near, "pairs", twins)
    vmem = pl.BlockSpec(memory_space=pltpu.VMEM)
    smem = pl.BlockSpec(memory_space=pltpu.SMEM)
    limit = pltpu.CompilerParams(vmem_limit_bytes=32 * 2**20)
    high, low = lax.optimization_barrier((jnp.asarray(high), jnp.asarray(low)))
    white = pltpu.VMEM((2, BINS, C), jnp.bfloat16)
    own_cross = pl.pallas_call(
        own_kernel,
        out_shape=jax.ShapeDtypeStruct((CHIPS, 2 * BINS, MAXB * CB), jnp.bfloat16),
        in_specs=[smem] * 3 + [vmem] * 5,
        out_specs=vmem,
        scratch_shapes=[white],
        compiler_params=limit,
        name="own_cross",
    )(slots, *(branch[None] for branch in branches), window, spectra, near, own_size, twin_size)
    packed = pl.pallas_call(
        twin_kernel,
        out_shape=jax.ShapeDtypeStruct((CHIPS, ROWS_CHIP, MAXB * CB), jnp.bfloat16),
        in_specs=[smem] + [vmem] * 7,
        out_specs=vmem,
        scratch_shapes=[white],
        compiler_params=limit,
        name="twin_cross",
    )(slots, window, compress, twin, own_size, twin_size, far, own_cross)
    groups = [list(range(0, OWNERS, 2)), list(range(1, OWNERS, 2))]

    def widen(parts, slots):
        return jnp.pad(parts, ((0, 0), (0, 0), (0, (MAXB - slots) * CB)))

    def between_chips(slots):
        def exchange(packed):
            packed = lax.all_to_all(
                packed[:, :, : slots * CB], "pairs", 0, 0, axis_index_groups=groups, tiled=True
            )
            return widen(packed, slots)

        return exchange

    packed = lax.switch(most - 1, [between_chips(slots) for slots in range(1, MAXB + 1)], packed)

    def with_live(live):
        def exchange(packed, high, low):
            parts = pl.pallas_call(
                combine_kernel,
                out_shape=jax.ShapeDtypeStruct((HOURS, ROWS_PART, live * CB), jnp.bfloat16),
                in_specs=[vmem] * 3,
                out_specs=vmem,
                compiler_params=limit,
                name=f"combine_{live}",
            )(high, low, packed)
            parts = lax.all_to_all(parts, "tm", 0, 0, tiled=True)
            return widen(parts, live)

        return exchange

    parts = lax.switch(
        count - 1, [with_live(live) for live in range(1, MAXB + 1)], packed, high, low
    )
    return pl.pallas_call(
        stack_kernel,
        out_shape=jax.ShapeDtypeStruct((MAXB, CB, LAG_PART), jnp.float32),
        in_specs=[vmem] * 3,
        out_specs=pl.BlockSpec(memory_space=pl.ANY),
        scratch_shapes=[
            pltpu.VMEM((MAXB, CB, LAG_PART), jnp.float32),
            pltpu.SemaphoreType.DMA((MAXB,)),
        ],
        compiler_params=limit,
        name="stack",
    )(live, expand, parts)


def solution(mesh):
    return jax.shard_map(
        on_device,
        mesh=mesh,
        in_specs=(P(None, "tm", "pairs", None), P(), P()),
        out_specs=P("pairs", None, "tm"),
        check_vma=False,
    )
```

```python
import functools
import math

import jax
import jax.numpy as jnp
import ml_dtypes
import numpy as np
from jax import lax
from jax.experimental import pallas as pl
from jax.experimental.pallas import tpu as pltpu
from jax.sharding import PartitionSpec as P

C = 4096
CB = 128
NF = 1024
FIRST_BIN = 16
FFT_LEN = 8192
LAGS = 2048
SMOOTH = 32
MAXB = 4
HOURS = 8
OWNERS = 32
amp_floor = 0.2

CHIPS = OWNERS // 2
BINS = NF // OWNERS
CHIP_BINS = 2 * BINS
LAG_PART = LAGS // HOURS
RANK_CHIP = 28
RANK_PART = 48
ROWS_CHIP = 2 * RANK_CHIP
ROWS_PART = 2 * RANK_PART
STEP = 2.0 * math.pi / FFT_LEN


def slepian(points, half_width, count):
    n = np.arange(points, dtype=np.float64)
    tri = np.diag(((points - 1) / 2.0 - n) ** 2 * math.cos(2.0 * math.pi * half_width))
    off = n[1:] * (points - n[1:]) / 2.0
    tri = tri + np.diag(off, 1) + np.diag(off, -1)
    vectors = np.linalg.eigh(tri)[1][:, ::-1][:, :count]
    return vectors * np.where(vectors[points // 2] < 0, -1.0, 1.0)


def split_rounded(table):
    high = table.astype(ml_dtypes.bfloat16)
    low = (table - high.astype(np.float64)).astype(ml_dtypes.bfloat16)
    return high, low


def real_form(table):
    return np.block([[table.real, -table.imag], [table.imag, table.real]])


@functools.cache
def tables():
    chip_basis = slepian(CHIP_BINS, LAGS / 2 / FFT_LEN, RANK_CHIP)
    part_basis = slepian(NF, LAG_PART / 2 / FFT_LEN, RANK_PART)
    bins = np.arange(NF) - (NF - 1) / 2.0
    lags = np.arange(LAG_PART) - LAG_PART // 2
    mid_bin = FIRST_BIN + (NF - 1) / 2.0
    compress = np.kron(np.eye(2), chip_basis.T)
    parts = []
    for part in range(HOURS // 2):
        mid_lag = LAG_PART * part - (LAGS - LAG_PART) // 2
        turned = np.exp(1j * STEP * (bins + mid_bin) * mid_lag)[:, None] * part_basis
        turned = turned.reshape(CHIPS, CHIP_BINS, RANK_PART)
        blocks = [(chip_basis.T @ turned[chip]).T for chip in range(CHIPS)]
        parts.append(np.concatenate(blocks, axis=1))
    combine = np.concatenate([half for part in parts for half in (part.real, part.imag)], axis=0)
    waves = np.exp(1j * STEP * np.outer(lags, bins)) @ part_basis
    waves = waves * np.exp(1j * STEP * mid_bin * lags)[:, None] / math.sqrt(NF)
    expand = real_form(waves)
    row = np.arange(BINS)[:, None] + SMOOTH
    column = np.arange(BINS + 2 * SMOOTH)[None, :]
    window = (np.abs(row - column) <= SMOOTH).astype(ml_dtypes.bfloat16)
    turned = [window[:, -SMOOTH:], window[:, SMOOTH:-SMOOTH], window[:, :SMOOTH]]
    window = np.stack([window, np.concatenate(turned, axis=1)])
    halves = np.split(compress, 2 * CHIP_BINS // BINS, axis=1)
    by_core = []
    for core in range(2):
        own, twin = core, 1 - core
        ordered = [halves[own], halves[2 + own], halves[twin], halves[2 + twin]]
        by_core.append(np.concatenate(split_rounded(np.concatenate(ordered, axis=1)), axis=0))
    compress = np.stack(by_core)
    padded = np.zeros((2 * CB, 2 * LAG_PART), ml_dtypes.bfloat16)
    for index, half in enumerate(split_rounded(expand)):
        padded[index * CB : index * CB + ROWS_PART] = half.T
    expand = padded
    return window, compress, np.concatenate(split_rounded(combine), axis=0), expand


def magnitude_of(real, imag):
    real, imag = real.astype(jnp.float32), imag.astype(jnp.float32)
    return jnp.sqrt(real * real + imag * imag).astype(jnp.bfloat16)


def size_kernel(source, out):
    out[...] = magnitude_of(source[0], source[1])


def whiten(core, window, source, first, centre, second, white):
    chunk = 512
    weights = window[core]
    for start in range(0, C, chunk):
        lanes = slice(start, start + chunk)
        sizes = jnp.concatenate([first[:, lanes], centre[:, lanes], second[:, lanes]], axis=0)
        sums = jnp.dot(weights, sizes, preferred_element_type=jnp.float32)
        inverse = 1.0 / (sums * (1.0 / (2 * SMOOTH + 1)) + 1e-05)
        for part in range(2):
            value = source[part, :, lanes].astype(jnp.float32) * inverse
            white[part, :, lanes] = value.astype(jnp.bfloat16)


def cross_of(blocks, base, white):
    crossed = []
    for slot in range(MAXB):
        left = pl.ds(pl.multiple_of(blocks[base + 2 * slot] * CB, CB), CB)
        right = pl.ds(pl.multiple_of(blocks[base + 2 * slot + 1] * CB, CB), CB)
        left_re = white[0, :, left].astype(jnp.float32)
        left_im = white[1, :, left].astype(jnp.float32)
        right_re = white[0, :, right].astype(jnp.float32)
        right_im = white[1, :, right].astype(jnp.float32)
        real = left_re * right_re + left_im * right_im
        imag = left_im * right_re - left_re * right_im
        crossed.append(jnp.concatenate([real, imag], axis=0).astype(jnp.bfloat16))
    return jnp.concatenate(crossed, axis=1)


def own_kernel(blocks, most, count, window, own, near, own_size, twin_size, out, white):
    core = blocks[CHIPS * 2 * MAXB]
    whiten(core, window, own, near, own_size, twin_size, white)
    for chip in range(CHIPS):
        out[chip] = cross_of(blocks, chip * 2 * MAXB, white)


def twin_kernel(
    blocks, window, compress, twin, own_size, twin_size, far, own_cross, out, white
):
    core = blocks[CHIPS * 2 * MAXB]
    whiten(core, window, twin, own_size, twin_size, far, white)
    weights = compress[core]
    for chip in range(CHIPS):
        twin_cross = cross_of(blocks, chip * 2 * MAXB, white)
        cross = jnp.concatenate([own_cross[chip], twin_cross], axis=0)
        packed = jnp.dot(weights, cross, preferred_element_type=jnp.float32)
        out[chip] = (packed[:ROWS_CHIP] + packed[ROWS_CHIP:]).astype(jnp.bfloat16)


def combine_kernel(table, packed, out):
    wide = out.shape[2]
    real = [packed[chip, :RANK_CHIP, :wide] for chip in range(CHIPS)]
    imag = [packed[chip, RANK_CHIP:, :wide] for chip in range(CHIPS)]
    value = jnp.concatenate([jnp.concatenate(real, axis=0), jnp.concatenate(imag, axis=0)], axis=1)
    total = jnp.dot(table[...], value, preferred_element_type=jnp.float32)
    half = table.shape[0] // 2
    total = total[:half] + total[half:]
    for part in range(HOURS // 2):
        base = part * ROWS_PART
        real_rows = slice(base, base + RANK_PART)
        imag_rows = slice(base + RANK_PART, base + ROWS_PART)
        real_real, real_imag = total[real_rows, :wide], total[real_rows, wide:]
        imag_real, imag_imag = total[imag_rows, :wide], total[imag_rows, wide:]
        for where, sign in ((part, 1.0), (HOURS - 1 - part, -1.0)):
            both = [real_real - sign * imag_imag, real_imag + sign * imag_real]
            out[where] = jnp.concatenate(both, axis=0).astype(jnp.bfloat16)


def stack_kernel(live, expand, parts, out, result, sems):
    blank = jnp.zeros((CB - ROWS_PART, CB), jnp.bfloat16)
    copies = []
    for slot in range(MAXB):
        lanes = slice(slot * CB, (slot + 1) * CB)
        rows = []
        for hour in range(HOURS):
            part = jnp.concatenate([parts[hour, :, lanes], blank], axis=0).T
            rows.append(jnp.concatenate([part, part], axis=1))
        lagged = jnp.dot(
            jnp.concatenate(rows, axis=0), expand[...], preferred_element_type=jnp.float32
        )
        linear = mean_real = mean_imag = None
        for hour in range(HOURS):
            correlation = lagged[hour * CB : (hour + 1) * CB, :LAG_PART]
            quadrature = lagged[hour * CB : (hour + 1) * CB, LAG_PART:]
            power = correlation * correlation + quadrature * quadrature
            inverse = jnp.minimum(lax.rsqrt(power), 1.0 / amp_floor)
            unit_real = correlation * inverse
            unit_imag = quadrature * inverse
            if hour == 0:
                linear, mean_real, mean_imag = correlation, unit_real, unit_imag
            else:
                linear = linear + correlation
                mean_real = mean_real + unit_real
                mean_imag = mean_imag + unit_imag
        stacked = linear * (mean_real * mean_real + mean_imag * mean_imag) * (1.0 / HOURS**3)
        result[slot] = jnp.where(live[slot] > 0, stacked, jnp.zeros_like(stacked))
        copy = pltpu.make_async_copy(result.at[slot], out.at[slot], sems.at[slot])
        copy.start()
        copies.append(copy)
    for copy in copies:
        copy.wait()


def on_device(spectra, pair_blocks, block_count):
    owner = lax.axis_index("pairs")
    core = owner % 2
    window, compress, combine, expand = tables()
    vmem = pl.BlockSpec(memory_space=pltpu.VMEM)
    smem = pl.BlockSpec(memory_space=pltpu.SMEM)
    limit = pltpu.CompilerParams(vmem_limit_bytes=32 * 2**20)
    spectra = spectra[:, 0]
    twins = [(i, i ^ 1) for i in range(OWNERS)]
    twin = lax.ppermute(spectra, "pairs", twins)
    own_size = pl.pallas_call(
        size_kernel,
        out_shape=jax.ShapeDtypeStruct((BINS, C), jnp.bfloat16),
        in_specs=[vmem],
        out_specs=vmem,
        compiler_params=limit,
        name="own_size",
    )(spectra)
    last = OWNERS - 1
    near_pairs = [(i, i + 1) for i in range(1, last, 2)] + [(i, i - 1) for i in range(2, last, 2)]
    near = lax.ppermute(own_size, "pairs", near_pairs)
    twin_size = magnitude_of(twin[0], twin[1])
    slots = lax.dynamic_index_in_dim(
        pair_blocks.reshape(CHIPS, 2, 2 * MAXB), core, 1, keepdims=False
    )
    slots = jnp.concatenate([slots.reshape(-1), core[None]])
    count = lax.dynamic_index_in_dim(block_count, owner, 0, keepdims=False)
    live = (lax.broadcasted_iota(jnp.int32, (MAXB, 1, LAG_PART), 0) < count).astype(jnp.float32)
    most = jnp.max(jnp.where(lax.iota(jnp.int32, OWNERS) % 2 == core, block_count, 0))
    first, last_live = jnp.int32(0), jnp.int32(MAXB - 1)
    branches = [lax.clamp(first, value - 1, last_live) for value in (most, count)]
    near, twin_size, slots, live, *branches = lax.optimization_barrier(
        (near, twin_size, slots, live, *branches)
    )
    far = lax.ppermute(near, "pairs", twins)
    combine = lax.optimization_barrier(jnp.asarray(combine))
    white = pltpu.VMEM((2, BINS, C), jnp.bfloat16)
    own_cross = pl.pallas_call(
        own_kernel,
        out_shape=jax.ShapeDtypeStruct((CHIPS, 2 * BINS, MAXB * CB), jnp.bfloat16),
        in_specs=[smem] * 3 + [vmem] * 5,
        out_specs=vmem,
        scratch_shapes=[white],
        compiler_params=limit,
        name="own_cross",
    )(slots, *(branch[None] for branch in branches), window, spectra, near, own_size, twin_size)
    packed = pl.pallas_call(
        twin_kernel,
        out_shape=jax.ShapeDtypeStruct((CHIPS, ROWS_CHIP, MAXB * CB), jnp.bfloat16),
        in_specs=[smem] + [vmem] * 7,
        out_specs=vmem,
        scratch_shapes=[white],
        compiler_params=limit,
        name="twin_cross",
    )(slots, window, compress, twin, own_size, twin_size, far, own_cross)
    groups = [list(range(0, OWNERS, 2)), list(range(1, OWNERS, 2))]

    def widen(parts, slots):
        return jnp.pad(parts, ((0, 0), (0, 0), (0, (MAXB - slots) * CB)))

    def between_chips(slots):
        def exchange(packed):
            packed = lax.all_to_all(
                packed[:, :, : slots * CB], "pairs", 0, 0, axis_index_groups=groups, tiled=True
            )
            return widen(packed, slots)

        return exchange

    packed = lax.switch(most - 1, [between_chips(slots) for slots in range(1, MAXB + 1)], packed)

    def with_live(live):
        def exchange(packed, combine):
            parts = pl.pallas_call(
                combine_kernel,
                out_shape=jax.ShapeDtypeStruct((HOURS, ROWS_PART, live * CB), jnp.bfloat16),
                in_specs=[vmem] * 2,
                out_specs=vmem,
                compiler_params=limit,
                name=f"combine_{live}",
            )(combine, packed)
            parts = lax.all_to_all(parts, "tm", 0, 0, tiled=True)
            return widen(parts, live)

        return exchange

    parts = lax.switch(
        count - 1, [with_live(live) for live in range(1, MAXB + 1)], packed, combine
    )
    return pl.pallas_call(
        stack_kernel,
        out_shape=jax.ShapeDtypeStruct((MAXB, CB, LAG_PART), jnp.float32),
        in_specs=[vmem] * 3,
        out_specs=pl.BlockSpec(memory_space=pl.ANY),
        scratch_shapes=[
            pltpu.VMEM((MAXB, CB, LAG_PART), jnp.float32),
            pltpu.SemaphoreType.DMA((MAXB,)),
        ],
        compiler_params=limit,
        name="stack",
    )(live, expand, parts)


def solution(mesh):
    return jax.shard_map(
        on_device,
        mesh=mesh,
        in_specs=(P(None, "tm", "pairs", None), P(), P()),
        out_specs=P("pairs", None, "tm"),
        check_vma=False,
    )
```

```python
import functools
import math

import jax
import jax.numpy as jnp
import ml_dtypes
import numpy as np
from jax import lax
from jax.experimental import pallas as pl
from jax.experimental.pallas import tpu as pltpu
from jax.sharding import PartitionSpec as P

C = 4096
CB = 128
NF = 1024
FIRST_BIN = 16
FFT_LEN = 8192
LAGS = 2048
SMOOTH = 32
MAXB = 4
HOURS = 8
OWNERS = 32
amp_floor = 0.2

CHIPS = OWNERS // 2
BINS = NF // OWNERS
CHIP_BINS = 2 * BINS
LAG_PART = LAGS // HOURS
RANK_CHIP = 28
RANK_PART = 48
ROWS_CHIP = 2 * RANK_CHIP
ROWS_PART = 2 * RANK_PART
STEP = 2.0 * math.pi / FFT_LEN


def slepian(points, half_width, count):
    n = np.arange(points, dtype=np.float64)
    tri = np.diag(((points - 1) / 2.0 - n) ** 2 * math.cos(2.0 * math.pi * half_width))
    off = n[1:] * (points - n[1:]) / 2.0
    tri = tri + np.diag(off, 1) + np.diag(off, -1)
    vectors = np.linalg.eigh(tri)[1][:, ::-1][:, :count]
    return vectors * np.where(vectors[points // 2] < 0, -1.0, 1.0)


def split_rounded(table):
    high = table.astype(ml_dtypes.bfloat16)
    low = (table - high.astype(np.float64)).astype(ml_dtypes.bfloat16)
    return high, low


def real_form(table):
    return np.block([[table.real, -table.imag], [table.imag, table.real]])


@functools.cache
def tables():
    chip_basis = slepian(CHIP_BINS, LAGS / 2 / FFT_LEN, RANK_CHIP)
    part_basis = slepian(NF, LAG_PART / 2 / FFT_LEN, RANK_PART)
    bins = np.arange(NF) - (NF - 1) / 2.0
    lags = np.arange(LAG_PART) - LAG_PART // 2
    mid_bin = FIRST_BIN + (NF - 1) / 2.0
    compress = np.kron(np.eye(2), chip_basis.T)
    parts = []
    for part in range(HOURS // 2):
        mid_lag = LAG_PART * part - (LAGS - LAG_PART) // 2
        turned = np.exp(1j * STEP * (bins + mid_bin) * mid_lag)[:, None] * part_basis
        turned = turned.reshape(CHIPS, CHIP_BINS, RANK_PART)
        blocks = [(chip_basis.T @ turned[chip]).T for chip in range(CHIPS)]
        parts.append(np.concatenate(blocks, axis=1))
    combine = np.concatenate([half for part in parts for half in (part.real, part.imag)], axis=0)
    waves = np.exp(1j * STEP * np.outer(lags, bins)) @ part_basis
    waves = waves * np.exp(1j * STEP * mid_bin * lags)[:, None] / math.sqrt(NF)
    expand = real_form(waves)
    row = np.arange(BINS)[:, None] + SMOOTH
    column = np.arange(BINS + 2 * SMOOTH)[None, :]
    window = (np.abs(row - column) <= SMOOTH).astype(ml_dtypes.bfloat16)
    turned = [window[:, -SMOOTH:], window[:, SMOOTH:-SMOOTH], window[:, :SMOOTH]]
    window = np.stack([window, np.concatenate(turned, axis=1)])
    halves = np.split(compress, 2 * CHIP_BINS // BINS, axis=1)
    by_core = []
    for core in range(2):
        own, twin = core, 1 - core
        ordered = [halves[own], halves[2 + own], halves[twin], halves[2 + twin]]
        by_core.append(np.concatenate(split_rounded(np.concatenate(ordered, axis=1)), axis=0))
    compress = np.stack(by_core)
    padded = np.zeros((2 * CB, 2 * LAG_PART), ml_dtypes.bfloat16)
    for index, half in enumerate(split_rounded(expand)):
        padded[index * CB : index * CB + ROWS_PART] = half.T
    expand = padded
    return window, compress, combine.astype(ml_dtypes.bfloat16), expand


def magnitude_of(real, imag):
    real, imag = real.astype(jnp.float32), imag.astype(jnp.float32)
    return jnp.sqrt(real * real + imag * imag).astype(jnp.bfloat16)


def whiten(core, window, source, first, centre, second, white):
    chunk = 512
    weights = window[core]
    for start in range(0, C, chunk):
        lanes = slice(start, start + chunk)
        sizes = jnp.concatenate([first[:, lanes], centre[:, lanes], second[:, lanes]], axis=0)
        sums = jnp.dot(weights, sizes, preferred_element_type=jnp.float32)
        inverse = 1.0 / (sums * (1.0 / (2 * SMOOTH + 1)) + 1e-05)
        for part in range(2):
            value = source[part, :, lanes].astype(jnp.float32) * inverse
            white[part, :, lanes] = value.astype(jnp.bfloat16)


def cross_of(blocks, base, white):
    crossed = []
    for slot in range(MAXB):
        left = pl.ds(pl.multiple_of(blocks[base + 2 * slot] * CB, CB), CB)
        right = pl.ds(pl.multiple_of(blocks[base + 2 * slot + 1] * CB, CB), CB)
        left_re = white[0, :, left].astype(jnp.float32)
        left_im = white[1, :, left].astype(jnp.float32)
        right_re = white[0, :, right].astype(jnp.float32)
        right_im = white[1, :, right].astype(jnp.float32)
        real = left_re * right_re + left_im * right_im
        imag = left_im * right_re - left_re * right_im
        crossed.append(jnp.concatenate([real, imag], axis=0).astype(jnp.bfloat16))
    return jnp.concatenate(crossed, axis=1)


def own_kernel(blocks, most, count, window, own, near, own_size, twin_size, out, white):
    core = blocks[CHIPS * 2 * MAXB]
    whiten(core, window, own, near, own_size, twin_size, white)
    for chip in range(CHIPS):
        out[chip] = cross_of(blocks, chip * 2 * MAXB, white)


def twin_kernel(
    blocks, window, compress, twin, own_size, twin_size, far, own_cross, out, white
):
    core = blocks[CHIPS * 2 * MAXB]
    whiten(core, window, twin, own_size, twin_size, far, white)
    weights = compress[core]
    for chip in range(CHIPS):
        twin_cross = cross_of(blocks, chip * 2 * MAXB, white)
        cross = jnp.concatenate([own_cross[chip], twin_cross], axis=0)
        packed = jnp.dot(weights, cross, preferred_element_type=jnp.float32)
        out[chip] = (packed[:ROWS_CHIP] + packed[ROWS_CHIP:]).astype(jnp.bfloat16)


def combine_kernel(table, packed, out):
    wide = out.shape[2]
    real = [packed[chip, :RANK_CHIP, :wide] for chip in range(CHIPS)]
    imag = [packed[chip, RANK_CHIP:, :wide] for chip in range(CHIPS)]
    value = jnp.concatenate([jnp.concatenate(real, axis=0), jnp.concatenate(imag, axis=0)], axis=1)
    total = jnp.dot(table[...], value, preferred_element_type=jnp.float32)
    for part in range(HOURS // 2):
        base = part * ROWS_PART
        real_rows = slice(base, base + RANK_PART)
        imag_rows = slice(base + RANK_PART, base + ROWS_PART)
        real_real, real_imag = total[real_rows, :wide], total[real_rows, wide:]
        imag_real, imag_imag = total[imag_rows, :wide], total[imag_rows, wide:]
        for where, sign in ((part, 1.0), (HOURS - 1 - part, -1.0)):
            both = [real_real - sign * imag_imag, real_imag + sign * imag_real]
            out[where] = jnp.concatenate(both, axis=0).astype(jnp.bfloat16)


def stack_kernel(live, expand, parts, out, result, sems):
    blank = jnp.zeros((CB - ROWS_PART, CB), jnp.bfloat16)
    copies = []
    for slot in range(MAXB):
        lanes = slice(slot * CB, (slot + 1) * CB)
        rows = []
        for hour in range(HOURS):
            part = jnp.concatenate([parts[hour, :, lanes], blank], axis=0).T
            rows.append(jnp.concatenate([part, part], axis=1))
        lagged = jnp.dot(
            jnp.concatenate(rows, axis=0), expand[...], preferred_element_type=jnp.float32
        )
        linear = mean_real = mean_imag = None
        for hour in range(HOURS):
            correlation = lagged[hour * CB : (hour + 1) * CB, :LAG_PART]
            quadrature = lagged[hour * CB : (hour + 1) * CB, LAG_PART:]
            power = correlation * correlation + quadrature * quadrature
            inverse = jnp.minimum(lax.rsqrt(power), 1.0 / amp_floor)
            unit_real = correlation * inverse
            unit_imag = quadrature * inverse
            if hour == 0:
                linear, mean_real, mean_imag = correlation, unit_real, unit_imag
            else:
                linear = linear + correlation
                mean_real = mean_real + unit_real
                mean_imag = mean_imag + unit_imag
        stacked = linear * (mean_real * mean_real + mean_imag * mean_imag) * (1.0 / HOURS**3)
        result[slot] = jnp.where(live[slot] > 0, stacked, jnp.zeros_like(stacked))
        copy = pltpu.make_async_copy(result.at[slot], out.at[slot], sems.at[slot])
        copy.start()
        copies.append(copy)
    for copy in copies:
        copy.wait()


def on_device(spectra, pair_blocks, block_count):
    owner = lax.axis_index("pairs")
    core = owner % 2
    window, compress, combine, expand = tables()
    spectra = spectra[:, 0]
    twins = [(i, i ^ 1) for i in range(OWNERS)]
    twin = lax.ppermute(spectra, "pairs", twins)
    own_size = magnitude_of(spectra[0], spectra[1])
    last = OWNERS - 1
    near_pairs = [(i, i + 1) for i in range(1, last, 2)] + [(i, i - 1) for i in range(2, last, 2)]
    near = lax.ppermute(own_size, "pairs", near_pairs)
    twin_size = magnitude_of(twin[0], twin[1])
    slots = lax.dynamic_index_in_dim(
        pair_blocks.reshape(CHIPS, 2, 2 * MAXB), core, 1, keepdims=False
    )
    slots = jnp.concatenate([slots.reshape(-1), core[None]])
    count = lax.dynamic_index_in_dim(block_count, owner, 0, keepdims=False)
    live = (lax.broadcasted_iota(jnp.int32, (MAXB, 1, 1), 0) < count).astype(jnp.float32)
    most = jnp.max(jnp.where(lax.iota(jnp.int32, OWNERS) % 2 == core, block_count, 0))
    first, last_live = jnp.int32(0), jnp.int32(MAXB - 1)
    branches = [lax.clamp(first, value - 1, last_live) for value in (most, count)]
    near, twin_size, slots, live, *branches = lax.optimization_barrier(
        (near, twin_size, slots, live, *branches)
    )
    far = lax.ppermute(near, "pairs", twins)
    vmem = pl.BlockSpec(memory_space=pltpu.VMEM)
    smem = pl.BlockSpec(memory_space=pltpu.SMEM)
    limit = pltpu.CompilerParams(vmem_limit_bytes=32 * 2**20)
    combine = lax.optimization_barrier(jnp.asarray(combine))
    white = pltpu.VMEM((2, BINS, C), jnp.bfloat16)
    own_cross = pl.pallas_call(
        own_kernel,
        out_shape=jax.ShapeDtypeStruct((CHIPS, 2 * BINS, MAXB * CB), jnp.bfloat16),
        in_specs=[smem] * 3 + [vmem] * 5,
        out_specs=vmem,
        scratch_shapes=[white],
        compiler_params=limit,
        name="own_cross",
    )(slots, *(branch[None] for branch in branches), window, spectra, near, own_size, twin_size)
    packed = pl.pallas_call(
        twin_kernel,
        out_shape=jax.ShapeDtypeStruct((CHIPS, ROWS_CHIP, MAXB * CB), jnp.bfloat16),
        in_specs=[smem] + [vmem] * 7,
        out_specs=vmem,
        scratch_shapes=[white],
        compiler_params=limit,
        name="twin_cross",
    )(slots, window, compress, twin, own_size, twin_size, far, own_cross)
    groups = [list(range(0, OWNERS, 2)), list(range(1, OWNERS, 2))]

    def widen(parts, slots):
        return jnp.pad(parts, ((0, 0), (0, 0), (0, (MAXB - slots) * CB)))

    def between_chips(slots):
        def exchange(packed):
            packed = lax.all_to_all(
                packed[:, :, : slots * CB], "pairs", 0, 0, axis_index_groups=groups, tiled=True
            )
            return widen(packed, slots)

        return exchange

    packed = lax.switch(most - 1, [between_chips(slots) for slots in range(1, MAXB + 1)], packed)

    def with_live(live):
        def exchange(packed, combine):
            parts = pl.pallas_call(
                combine_kernel,
                out_shape=jax.ShapeDtypeStruct((HOURS, ROWS_PART, live * CB), jnp.bfloat16),
                in_specs=[vmem] * 2,
                out_specs=vmem,
                compiler_params=limit,
                name=f"combine_{live}",
            )(combine, packed)
            parts = lax.all_to_all(parts, "tm", 0, 0, tiled=True)
            return widen(parts, live)

        return exchange

    parts = lax.switch(
        count - 1, [with_live(live) for live in range(1, MAXB + 1)], packed, combine
    )
    return pl.pallas_call(
        stack_kernel,
        out_shape=jax.ShapeDtypeStruct((MAXB, CB, LAG_PART), jnp.float32),
        in_specs=[vmem] * 3,
        out_specs=pl.BlockSpec(memory_space=pl.ANY),
        scratch_shapes=[
            pltpu.VMEM((MAXB, CB, LAG_PART), jnp.float32),
            pltpu.SemaphoreType.DMA((MAXB,)),
        ],
        compiler_params=limit,
        name="stack",
    )(live, expand, parts)


def solution(mesh):
    return jax.shard_map(
        on_device,
        mesh=mesh,
        in_specs=(P(None, "tm", "pairs", None), P(), P()),
        out_specs=P("pairs", None, "tm"),
        check_vma=False,
    )
```

```python
import functools
import math

import jax
import jax.numpy as jnp
import ml_dtypes
import numpy as np
from jax import lax
from jax.experimental import pallas as pl
from jax.experimental.pallas import tpu as pltpu
from jax.sharding import PartitionSpec as P

C = 4096
CB = 128
NF = 1024
FIRST_BIN = 16
FFT_LEN = 8192
LAGS = 2048
SMOOTH = 32
MAXB = 4
HOURS = 8
OWNERS = 32
amp_floor = 0.2

CHIPS = OWNERS // 2
BINS = NF // OWNERS
CHIP_BINS = 2 * BINS
LAG_PART = LAGS // HOURS
RANK_CHIP = 28
RANK_PART = 48
ROWS_CHIP = 2 * RANK_CHIP
ROWS_PART = 2 * RANK_PART
STEP = 2.0 * math.pi / FFT_LEN


def slepian(points, half_width, count):
    n = np.arange(points, dtype=np.float64)
    tri = np.diag(((points - 1) / 2.0 - n) ** 2 * math.cos(2.0 * math.pi * half_width))
    off = n[1:] * (points - n[1:]) / 2.0
    tri = tri + np.diag(off, 1) + np.diag(off, -1)
    vectors = np.linalg.eigh(tri)[1][:, ::-1][:, :count]
    return vectors * np.where(vectors[points // 2] < 0, -1.0, 1.0)


def split_rounded(table):
    high = table.astype(ml_dtypes.bfloat16)
    low = (table - high.astype(np.float64)).astype(ml_dtypes.bfloat16)
    return high, low


def real_form(table):
    return np.block([[table.real, -table.imag], [table.imag, table.real]])


@functools.cache
def tables():
    chip_basis = slepian(CHIP_BINS, (LAGS / 2 + 4) / FFT_LEN, RANK_CHIP)
    part_basis = slepian(NF, (LAG_PART / 2 + 0.5) / FFT_LEN, RANK_PART)
    bins = np.arange(NF) - (NF - 1) / 2.0
    lags = np.arange(LAG_PART) - LAG_PART // 2
    mid_bin = FIRST_BIN + (NF - 1) / 2.0
    compress = np.kron(np.eye(2), chip_basis.T)
    parts = []
    for part in range(HOURS // 2):
        mid_lag = LAG_PART * part - (LAGS - LAG_PART) // 2
        turned = np.exp(1j * STEP * (bins + mid_bin) * mid_lag)[:, None] * part_basis
        turned = turned.reshape(CHIPS, CHIP_BINS, RANK_PART)
        blocks = [(chip_basis.T @ turned[chip]).T for chip in range(CHIPS)]
        parts.append(np.concatenate(blocks, axis=1))
    combine = np.concatenate([half for part in parts for half in (part.real, part.imag)], axis=0)
    waves = np.exp(1j * STEP * np.outer(lags, bins)) @ part_basis
    waves = waves * np.exp(1j * STEP * mid_bin * lags)[:, None] / math.sqrt(NF)
    expand = real_form(waves)
    row = np.arange(BINS)[:, None] + SMOOTH
    column = np.arange(BINS + 2 * SMOOTH)[None, :]
    window = (np.abs(row - column) <= SMOOTH).astype(ml_dtypes.bfloat16)
    turned = [window[:, -SMOOTH:], window[:, SMOOTH:-SMOOTH], window[:, :SMOOTH]]
    window = np.stack([window, np.concatenate(turned, axis=1)])
    halves = np.split(compress, 2 * CHIP_BINS // BINS, axis=1)
    by_core = []
    for core in range(2):
        own, twin = core, 1 - core
        ordered = [halves[own], halves[2 + own], halves[twin], halves[2 + twin]]
        by_core.append(np.concatenate(split_rounded(np.concatenate(ordered, axis=1)), axis=0))
    compress = np.stack(by_core)
    padded = np.zeros((2 * CB, 2 * LAG_PART), ml_dtypes.bfloat16)
    for index, half in enumerate(split_rounded(expand)):
        padded[index * CB : index * CB + ROWS_PART] = half.T
    expand = padded
    return window, compress, combine.astype(ml_dtypes.bfloat16), expand


def magnitude_of(real, imag):
    real, imag = real.astype(jnp.float32), imag.astype(jnp.float32)
    return jnp.sqrt(real * real + imag * imag).astype(jnp.bfloat16)


def whiten(core, window, source, first, centre, second, white):
    chunk = 512
    weights = window[core]
    for start in range(0, C, chunk):
        lanes = slice(start, start + chunk)
        sizes = jnp.concatenate([first[:, lanes], centre[:, lanes], second[:, lanes]], axis=0)
        sums = jnp.dot(weights, sizes, preferred_element_type=jnp.float32)
        inverse = 1.0 / (sums * (1.0 / (2 * SMOOTH + 1)) + 1e-05)
        for part in range(2):
            value = source[part, :, lanes].astype(jnp.float32) * inverse
            white[part, :, lanes] = value.astype(jnp.bfloat16)


def cross_of(blocks, base, white):
    crossed = []
    for slot in range(MAXB):
        left = pl.ds(pl.multiple_of(blocks[base + 2 * slot] * CB, CB), CB)
        right = pl.ds(pl.multiple_of(blocks[base + 2 * slot + 1] * CB, CB), CB)
        left_re = white[0, :, left].astype(jnp.float32)
        left_im = white[1, :, left].astype(jnp.float32)
        right_re = white[0, :, right].astype(jnp.float32)
        right_im = white[1, :, right].astype(jnp.float32)
        real = left_re * right_re + left_im * right_im
        imag = left_im * right_re - left_re * right_im
        crossed.append(jnp.concatenate([real, imag], axis=0).astype(jnp.bfloat16))
    return jnp.concatenate(crossed, axis=1)


def own_kernel(blocks, most, count, window, own, near, own_size, twin_size, out, white):
    core = blocks[CHIPS * 2 * MAXB]
    whiten(core, window, own, near, own_size, twin_size, white)
    for chip in range(CHIPS):
        out[chip] = cross_of(blocks, chip * 2 * MAXB, white)


def twin_kernel(
    blocks, window, compress, twin, own_size, twin_size, far, own_cross, out, white
):
    core = blocks[CHIPS * 2 * MAXB]
    whiten(core, window, twin, own_size, twin_size, far, white)
    weights = compress[core]
    for chip in range(CHIPS):
        twin_cross = cross_of(blocks, chip * 2 * MAXB, white)
        cross = jnp.concatenate([own_cross[chip], twin_cross], axis=0)
        packed = jnp.dot(weights, cross, preferred_element_type=jnp.float32)
        out[chip] = (packed[:ROWS_CHIP] + packed[ROWS_CHIP:]).astype(jnp.bfloat16)


def combine_kernel(table, packed, out):
    wide = out.shape[2]
    real = [packed[chip, :RANK_CHIP, :wide] for chip in range(CHIPS)]
    imag = [packed[chip, RANK_CHIP:, :wide] for chip in range(CHIPS)]
    value = jnp.concatenate([jnp.concatenate(real, axis=0), jnp.concatenate(imag, axis=0)], axis=1)
    total = jnp.dot(table[...], value, preferred_element_type=jnp.float32)
    for part in range(HOURS // 2):
        base = part * ROWS_PART
        real_rows = slice(base, base + RANK_PART)
        imag_rows = slice(base + RANK_PART, base + ROWS_PART)
        real_real, real_imag = total[real_rows, :wide], total[real_rows, wide:]
        imag_real, imag_imag = total[imag_rows, :wide], total[imag_rows, wide:]
        for where, sign in ((part, 1.0), (HOURS - 1 - part, -1.0)):
            both = [real_real - sign * imag_imag, real_imag + sign * imag_real]
            out[where] = jnp.concatenate(both, axis=0).astype(jnp.bfloat16)


def stack_kernel(live, expand, parts, out, result, sems):
    blank = jnp.zeros((CB - ROWS_PART, CB), jnp.bfloat16)
    copies = []
    for slot in range(MAXB):
        lanes = slice(slot * CB, (slot + 1) * CB)
        rows = []
        for hour in range(HOURS):
            part = jnp.concatenate([parts[hour, :, lanes], blank], axis=0).T
            rows.append(jnp.concatenate([part, part], axis=1))
        lagged = jnp.dot(
            jnp.concatenate(rows, axis=0), expand[...], preferred_element_type=jnp.float32
        )
        linear = mean_real = mean_imag = None
        for hour in range(HOURS):
            correlation = lagged[hour * CB : (hour + 1) * CB, :LAG_PART]
            quadrature = lagged[hour * CB : (hour + 1) * CB, LAG_PART:]
            power = correlation * correlation + quadrature * quadrature
            inverse = jnp.minimum(lax.rsqrt(power), 1.0 / amp_floor)
            unit_real = correlation * inverse
            unit_imag = quadrature * inverse
            if hour == 0:
                linear, mean_real, mean_imag = correlation, unit_real, unit_imag
            else:
                linear = linear + correlation
                mean_real = mean_real + unit_real
                mean_imag = mean_imag + unit_imag
        stacked = linear * (mean_real * mean_real + mean_imag * mean_imag) * (1.0 / HOURS**3)
        result[slot] = jnp.where(live[slot] > 0, stacked, jnp.zeros_like(stacked))
        copy = pltpu.make_async_copy(result.at[slot], out.at[slot], sems.at[slot])
        copy.start()
        copies.append(copy)
    for copy in copies:
        copy.wait()


def on_device(spectra, pair_blocks, block_count):
    owner = lax.axis_index("pairs")
    core = owner % 2
    window, compress, combine, expand = tables()
    spectra = spectra[:, 0]
    twins = [(i, i ^ 1) for i in range(OWNERS)]
    twin = lax.ppermute(spectra, "pairs", twins)
    own_size = magnitude_of(spectra[0], spectra[1])
    last = OWNERS - 1
    near_pairs = [(i, i + 1) for i in range(1, last, 2)] + [(i, i - 1) for i in range(2, last, 2)]
    near = lax.ppermute(own_size, "pairs", near_pairs)
    twin_size = magnitude_of(twin[0], twin[1])
    slots = lax.dynamic_index_in_dim(
        pair_blocks.reshape(CHIPS, 2, 2 * MAXB), core, 1, keepdims=False
    )
    slots = jnp.concatenate([slots.reshape(-1), core[None]])
    count = lax.dynamic_index_in_dim(block_count, owner, 0, keepdims=False)
    live = (lax.broadcasted_iota(jnp.int32, (MAXB, 1, 1), 0) < count).astype(jnp.float32)
    most = jnp.max(jnp.where(lax.iota(jnp.int32, OWNERS) % 2 == core, block_count, 0))
    first, last_live = jnp.int32(0), jnp.int32(MAXB - 1)
    branches = [lax.clamp(first, value - 1, last_live) for value in (most, count)]
    near, twin_size, slots, live, *branches = lax.optimization_barrier(
        (near, twin_size, slots, live, *branches)
    )
    far = lax.ppermute(near, "pairs", twins)
    vmem = pl.BlockSpec(memory_space=pltpu.VMEM)
    smem = pl.BlockSpec(memory_space=pltpu.SMEM)
    limit = pltpu.CompilerParams(vmem_limit_bytes=32 * 2**20)
    combine = lax.optimization_barrier(jnp.asarray(combine))
    white = pltpu.VMEM((2, BINS, C), jnp.bfloat16)
    own_cross = pl.pallas_call(
        own_kernel,
        out_shape=jax.ShapeDtypeStruct((CHIPS, 2 * BINS, MAXB * CB), jnp.bfloat16),
        in_specs=[smem] * 3 + [vmem] * 5,
        out_specs=vmem,
        scratch_shapes=[white],
        compiler_params=limit,
        name="own_cross",
    )(slots, *(branch[None] for branch in branches), window, spectra, near, own_size, twin_size)
    packed = pl.pallas_call(
        twin_kernel,
        out_shape=jax.ShapeDtypeStruct((CHIPS, ROWS_CHIP, MAXB * CB), jnp.bfloat16),
        in_specs=[smem] + [vmem] * 7,
        out_specs=vmem,
        scratch_shapes=[white],
        compiler_params=limit,
        name="twin_cross",
    )(slots, window, compress, twin, own_size, twin_size, far, own_cross)
    groups = [list(range(0, OWNERS, 2)), list(range(1, OWNERS, 2))]

    def widen(parts, slots):
        return jnp.pad(parts, ((0, 0), (0, 0), (0, (MAXB - slots) * CB)))

    def between_chips(slots):
        def exchange(packed):
            packed = lax.all_to_all(
                packed[:, :, : slots * CB], "pairs", 0, 0, axis_index_groups=groups, tiled=True
            )
            return widen(packed, slots)

        return exchange

    packed = lax.switch(most - 1, [between_chips(slots) for slots in range(1, MAXB + 1)], packed)

    def with_live(live):
        def exchange(packed, combine):
            parts = pl.pallas_call(
                combine_kernel,
                out_shape=jax.ShapeDtypeStruct((HOURS, ROWS_PART, live * CB), jnp.bfloat16),
                in_specs=[vmem] * 2,
                out_specs=vmem,
                compiler_params=limit,
                name=f"combine_{live}",
            )(combine, packed)
            parts = lax.all_to_all(parts, "tm", 0, 0, tiled=True)
            return widen(parts, live)

        return exchange

    parts = lax.switch(
        count - 1, [with_live(live) for live in range(1, MAXB + 1)], packed, combine
    )
    return pl.pallas_call(
        stack_kernel,
        out_shape=jax.ShapeDtypeStruct((MAXB, CB, LAG_PART), jnp.float32),
        in_specs=[vmem] * 3,
        out_specs=pl.BlockSpec(memory_space=pl.ANY),
        scratch_shapes=[
            pltpu.VMEM((MAXB, CB, LAG_PART), jnp.float32),
            pltpu.SemaphoreType.DMA((MAXB,)),
        ],
        compiler_params=limit,
        name="stack",
    )(live, expand, parts)


def solution(mesh):
    return jax.shard_map(
        on_device,
        mesh=mesh,
        in_specs=(P(None, "tm", "pairs", None), P(), P()),
        out_specs=P("pairs", None, "tm"),
        check_vma=False,
    )
```

```python
import functools
import math

import jax
import jax.numpy as jnp
import ml_dtypes
import numpy as np
from jax import lax
from jax.experimental import pallas as pl
from jax.experimental.pallas import tpu as pltpu
from jax.sharding import PartitionSpec as P

C = 4096
CB = 128
NF = 1024
FIRST_BIN = 16
FFT_LEN = 8192
LAGS = 2048
SMOOTH = 32
MAXB = 4
HOURS = 8
OWNERS = 32
amp_floor = 0.2

CHIPS = OWNERS // 2
BINS = NF // OWNERS
CHIP_BINS = 2 * BINS
LAG_PART = LAGS // HOURS
RANK_CHIP = 28
RANK_PART = 48
ROWS_CHIP = 2 * RANK_CHIP
ROWS_PART = 2 * RANK_PART
STEP = 2.0 * math.pi / FFT_LEN


def slepian(points, half_width, count):
    n = np.arange(points, dtype=np.float64)
    tri = np.diag(((points - 1) / 2.0 - n) ** 2 * math.cos(2.0 * math.pi * half_width))
    off = n[1:] * (points - n[1:]) / 2.0
    tri = tri + np.diag(off, 1) + np.diag(off, -1)
    vectors = np.linalg.eigh(tri)[1][:, ::-1][:, :count]
    return vectors * np.where(vectors[points // 2] < 0, -1.0, 1.0)


def split_rounded(table):
    high = table.astype(ml_dtypes.bfloat16)
    low = (table - high.astype(np.float64)).astype(ml_dtypes.bfloat16)
    return high, low


def real_form(table):
    return np.block([[table.real, -table.imag], [table.imag, table.real]])


@functools.cache
def tables():
    chip_basis = slepian(CHIP_BINS, (LAGS / 2 + 4) / FFT_LEN, RANK_CHIP)
    part_basis = slepian(NF, (LAG_PART / 2 + 0.5) / FFT_LEN, RANK_PART)
    bins = np.arange(NF) - (NF - 1) / 2.0
    lags = np.arange(LAG_PART) - LAG_PART // 2
    mid_bin = FIRST_BIN + (NF - 1) / 2.0
    compress = np.kron(np.eye(2), chip_basis.T)
    parts = []
    for part in range(HOURS // 2):
        mid_lag = LAG_PART * part - (LAGS - LAG_PART) // 2
        turned = np.exp(1j * STEP * (bins + mid_bin) * mid_lag)[:, None] * part_basis
        turned = turned.reshape(CHIPS, CHIP_BINS, RANK_PART)
        blocks = [(chip_basis.T @ turned[chip]).T for chip in range(CHIPS)]
        parts.append(np.concatenate(blocks, axis=1))
    combine = np.concatenate([half for part in parts for half in (part.real, part.imag)], axis=0)
    waves = np.exp(1j * STEP * np.outer(lags, bins)) @ part_basis
    waves = waves * np.exp(1j * STEP * mid_bin * lags)[:, None] / math.sqrt(NF)
    expand = real_form(waves)
    row = np.arange(BINS)[:, None] + SMOOTH
    column = np.arange(BINS + 2 * SMOOTH)[None, :]
    window = (np.abs(row - column) <= SMOOTH).astype(ml_dtypes.bfloat16)
    turned = [window[:, -SMOOTH:], window[:, SMOOTH:-SMOOTH], window[:, :SMOOTH]]
    window = np.stack([window, np.concatenate(turned, axis=1)])
    halves = np.split(compress, 2 * CHIP_BINS // BINS, axis=1)
    by_core = []
    for core in range(2):
        own, twin = core, 1 - core
        ordered = [halves[own], halves[2 + own], halves[twin], halves[2 + twin]]
        by_core.append(np.concatenate(split_rounded(np.concatenate(ordered, axis=1)), axis=0))
    compress = np.stack(by_core)
    padded = np.zeros((2 * CB, 2 * LAG_PART), ml_dtypes.bfloat16)
    for index, half in enumerate(split_rounded(expand)):
        padded[index * CB : index * CB + ROWS_PART] = half.T
    expand = padded
    return window, compress, np.concatenate(split_rounded(combine), axis=0), expand


def magnitude_of(real, imag):
    real, imag = real.astype(jnp.float32), imag.astype(jnp.float32)
    return jnp.sqrt(real * real + imag * imag).astype(jnp.bfloat16)


def whiten(core, window, source, first, centre, second, white):
    chunk = 512
    weights = window[core]
    for start in range(0, C, chunk):
        lanes = slice(start, start + chunk)
        sizes = jnp.concatenate([first[:, lanes], centre[:, lanes], second[:, lanes]], axis=0)
        sums = jnp.dot(weights, sizes, preferred_element_type=jnp.float32)
        inverse = 1.0 / (sums * (1.0 / (2 * SMOOTH + 1)) + 1e-05)
        for part in range(2):
            value = source[part, :, lanes].astype(jnp.float32) * inverse
            white[part, :, lanes] = value.astype(jnp.bfloat16)


def cross_of(blocks, base, white):
    crossed = []
    for slot in range(MAXB):
        left = pl.ds(pl.multiple_of(blocks[base + 2 * slot] * CB, CB), CB)
        right = pl.ds(pl.multiple_of(blocks[base + 2 * slot + 1] * CB, CB), CB)
        left_re = white[0, :, left].astype(jnp.float32)
        left_im = white[1, :, left].astype(jnp.float32)
        right_re = white[0, :, right].astype(jnp.float32)
        right_im = white[1, :, right].astype(jnp.float32)
        real = left_re * right_re + left_im * right_im
        imag = left_im * right_re - left_re * right_im
        crossed.append(jnp.concatenate([real, imag], axis=0).astype(jnp.bfloat16))
    return jnp.concatenate(crossed, axis=1)


def own_kernel(blocks, most, count, window, own, near, own_size, twin_size, out, white):
    core = blocks[CHIPS * 2 * MAXB]
    whiten(core, window, own, near, own_size, twin_size, white)
    for chip in range(CHIPS):
        out[chip] = cross_of(blocks, chip * 2 * MAXB, white)


def twin_kernel(
    blocks, window, compress, twin, own_size, twin_size, far, own_cross, out, white
):
    core = blocks[CHIPS * 2 * MAXB]
    whiten(core, window, twin, own_size, twin_size, far, white)
    weights = compress[core]
    for chip in range(CHIPS):
        twin_cross = cross_of(blocks, chip * 2 * MAXB, white)
        cross = jnp.concatenate([own_cross[chip], twin_cross], axis=0)
        packed = jnp.dot(weights, cross, preferred_element_type=jnp.float32)
        out[chip] = (packed[:ROWS_CHIP] + packed[ROWS_CHIP:]).astype(jnp.bfloat16)


def combine_kernel(table, packed, out):
    wide = out.shape[2]
    real = [packed[chip, :RANK_CHIP, :wide] for chip in range(CHIPS)]
    imag = [packed[chip, RANK_CHIP:, :wide] for chip in range(CHIPS)]
    value = jnp.concatenate([jnp.concatenate(real, axis=0), jnp.concatenate(imag, axis=0)], axis=1)
    total = jnp.dot(table[...], value, preferred_element_type=jnp.float32)
    half = table.shape[0] // 2
    total = total[:half] + total[half:]
    for part in range(HOURS // 2):
        base = part * ROWS_PART
        real_rows = slice(base, base + RANK_PART)
        imag_rows = slice(base + RANK_PART, base + ROWS_PART)
        real_real, real_imag = total[real_rows, :wide], total[real_rows, wide:]
        imag_real, imag_imag = total[imag_rows, :wide], total[imag_rows, wide:]
        for where, sign in ((part, 1.0), (HOURS - 1 - part, -1.0)):
            both = [real_real - sign * imag_imag, real_imag + sign * imag_real]
            out[where] = jnp.concatenate(both, axis=0).astype(jnp.bfloat16)


def stack_kernel(live, expand, parts, out, result, sems):
    blank = jnp.zeros((CB - ROWS_PART, CB), jnp.bfloat16)
    copies = []
    for slot in range(MAXB):
        lanes = slice(slot * CB, (slot + 1) * CB)
        rows = []
        for hour in range(HOURS):
            part = jnp.concatenate([parts[hour, :, lanes], blank], axis=0).T
            rows.append(jnp.concatenate([part, part], axis=1))
        lagged = jnp.dot(
            jnp.concatenate(rows, axis=0), expand[...], preferred_element_type=jnp.float32
        )
        linear = mean_real = mean_imag = None
        for hour in range(HOURS):
            correlation = lagged[hour * CB : (hour + 1) * CB, :LAG_PART]
            quadrature = lagged[hour * CB : (hour + 1) * CB, LAG_PART:]
            power = correlation * correlation + quadrature * quadrature
            inverse = jnp.minimum(lax.rsqrt(power), 1.0 / amp_floor)
            unit_real = correlation * inverse
            unit_imag = quadrature * inverse
            if hour == 0:
                linear, mean_real, mean_imag = correlation, unit_real, unit_imag
            else:
                linear = linear + correlation
                mean_real = mean_real + unit_real
                mean_imag = mean_imag + unit_imag
        stacked = linear * (mean_real * mean_real + mean_imag * mean_imag) * (1.0 / HOURS**3)
        result[slot] = jnp.where(live[slot] > 0, stacked, jnp.zeros_like(stacked))
        copy = pltpu.make_async_copy(result.at[slot], out.at[slot], sems.at[slot])
        copy.start()
        copies.append(copy)
    for copy in copies:
        copy.wait()


def on_device(spectra, pair_blocks, block_count):
    owner = lax.axis_index("pairs")
    core = owner % 2
    window, compress, combine, expand = tables()
    spectra = spectra[:, 0]
    twins = [(i, i ^ 1) for i in range(OWNERS)]
    twin = lax.ppermute(spectra, "pairs", twins)
    own_size = magnitude_of(spectra[0], spectra[1])
    last = OWNERS - 1
    near_pairs = [(i, i + 1) for i in range(1, last, 2)] + [(i, i - 1) for i in range(2, last, 2)]
    near = lax.ppermute(own_size, "pairs", near_pairs)
    twin_size = magnitude_of(twin[0], twin[1])
    slots = lax.dynamic_index_in_dim(
        pair_blocks.reshape(CHIPS, 2, 2 * MAXB), core, 1, keepdims=False
    )
    slots = jnp.concatenate([slots.reshape(-1), core[None]])
    count = lax.dynamic_index_in_dim(block_count, owner, 0, keepdims=False)
    live = (lax.broadcasted_iota(jnp.int32, (MAXB, 1, 1), 0) < count).astype(jnp.float32)
    most = jnp.max(jnp.where(lax.iota(jnp.int32, OWNERS) % 2 == core, block_count, 0))
    first, last_live = jnp.int32(0), jnp.int32(MAXB - 1)
    branches = [lax.clamp(first, value - 1, last_live) for value in (most, count)]
    near, twin_size, slots, live, *branches = lax.optimization_barrier(
        (near, twin_size, slots, live, *branches)
    )
    far = lax.ppermute(near, "pairs", twins)
    vmem = pl.BlockSpec(memory_space=pltpu.VMEM)
    smem = pl.BlockSpec(memory_space=pltpu.SMEM)
    limit = pltpu.CompilerParams(vmem_limit_bytes=32 * 2**20)
    combine = lax.optimization_barrier(jnp.asarray(combine))
    white = pltpu.VMEM((2, BINS, C), jnp.bfloat16)
    own_cross = pl.pallas_call(
        own_kernel,
        out_shape=jax.ShapeDtypeStruct((CHIPS, 2 * BINS, MAXB * CB), jnp.bfloat16),
        in_specs=[smem] * 3 + [vmem] * 5,
        out_specs=vmem,
        scratch_shapes=[white],
        compiler_params=limit,
        name="own_cross",
    )(slots, *(branch[None] for branch in branches), window, spectra, near, own_size, twin_size)
    packed = pl.pallas_call(
        twin_kernel,
        out_shape=jax.ShapeDtypeStruct((CHIPS, ROWS_CHIP, MAXB * CB), jnp.bfloat16),
        in_specs=[smem] + [vmem] * 7,
        out_specs=vmem,
        scratch_shapes=[white],
        compiler_params=limit,
        name="twin_cross",
    )(slots, window, compress, twin, own_size, twin_size, far, own_cross)
    groups = [list(range(0, OWNERS, 2)), list(range(1, OWNERS, 2))]

    def widen(parts, slots):
        return jnp.pad(parts, ((0, 0), (0, 0), (0, (MAXB - slots) * CB)))

    def between_chips(slots):
        def exchange(packed):
            packed = lax.all_to_all(
                packed[:, :, : slots * CB], "pairs", 0, 0, axis_index_groups=groups, tiled=True
            )
            return widen(packed, slots)

        return exchange

    packed = lax.switch(most - 1, [between_chips(slots) for slots in range(1, MAXB + 1)], packed)

    def with_live(live):
        def exchange(packed, combine):
            parts = pl.pallas_call(
                combine_kernel,
                out_shape=jax.ShapeDtypeStruct((HOURS, ROWS_PART, live * CB), jnp.bfloat16),
                in_specs=[vmem] * 2,
                out_specs=vmem,
                compiler_params=limit,
                name=f"combine_{live}",
            )(combine, packed)
            parts = lax.all_to_all(parts, "tm", 0, 0, tiled=True)
            return widen(parts, live)

        return exchange

    parts = lax.switch(
        count - 1, [with_live(live) for live in range(1, MAXB + 1)], packed, combine
    )
    return pl.pallas_call(
        stack_kernel,
        out_shape=jax.ShapeDtypeStruct((MAXB, CB, LAG_PART), jnp.float32),
        in_specs=[vmem] * 3,
        out_specs=pl.BlockSpec(memory_space=pl.ANY),
        scratch_shapes=[
            pltpu.VMEM((MAXB, CB, LAG_PART), jnp.float32),
            pltpu.SemaphoreType.DMA((MAXB,)),
        ],
        compiler_params=limit,
        name="stack",
    )(live, expand, parts)


def solution(mesh):
    return jax.shard_map(
        on_device,
        mesh=mesh,
        in_specs=(P(None, "tm", "pairs", None), P(), P()),
        out_specs=P("pairs", None, "tm"),
        check_vma=False,
    )
```

```python
import functools
import math

import jax
import jax.numpy as jnp
import ml_dtypes
import numpy as np
from jax import lax
from jax.experimental import pallas as pl
from jax.experimental.pallas import tpu as pltpu
from jax.sharding import PartitionSpec as P

C = 4096
CB = 128
NF = 1024
FIRST_BIN = 16
FFT_LEN = 8192
LAGS = 2048
SMOOTH = 32
MAXB = 4
HOURS = 8
OWNERS = 32
amp_floor = 0.2

CHIPS = OWNERS // 2
BINS = NF // OWNERS
CHIP_BINS = 2 * BINS
LAG_PART = LAGS // HOURS
RANK_CHIP = 28
RANK_PART = 48
ROWS_CHIP = 2 * RANK_CHIP
ROWS_PART = 2 * RANK_PART
STEP = 2.0 * math.pi / FFT_LEN


def slepian(points, half_width, count):
    n = np.arange(points, dtype=np.float64)
    tri = np.diag(((points - 1) / 2.0 - n) ** 2 * math.cos(2.0 * math.pi * half_width))
    off = n[1:] * (points - n[1:]) / 2.0
    tri = tri + np.diag(off, 1) + np.diag(off, -1)
    vectors = np.linalg.eigh(tri)[1][:, ::-1][:, :count]
    return vectors * np.where(vectors[points // 2] < 0, -1.0, 1.0)


def split_rounded(table):
    high = table.astype(ml_dtypes.bfloat16)
    low = (table - high.astype(np.float64)).astype(ml_dtypes.bfloat16)
    return high, low


def real_form(table):
    return np.block([[table.real, -table.imag], [table.imag, table.real]])


@functools.cache
def tables():
    chip_basis = slepian(CHIP_BINS, (LAGS / 2 + 4) / FFT_LEN, RANK_CHIP)
    part_basis = slepian(NF, (LAG_PART / 2 + 0.5) / FFT_LEN, RANK_PART)
    bins = np.arange(NF) - (NF - 1) / 2.0
    lags = np.arange(LAG_PART) - LAG_PART // 2
    mid_bin = FIRST_BIN + (NF - 1) / 2.0
    compress = np.kron(np.eye(2), chip_basis.T)
    parts = []
    for part in range(HOURS // 2):
        mid_lag = LAG_PART * part - (LAGS - LAG_PART) // 2
        turned = np.exp(1j * STEP * (bins + mid_bin) * mid_lag)[:, None] * part_basis
        turned = turned.reshape(CHIPS, CHIP_BINS, RANK_PART)
        blocks = [(chip_basis.T @ turned[chip]).T for chip in range(CHIPS)]
        parts.append(np.concatenate(blocks, axis=1))
    combine = np.concatenate([half for part in parts for half in (part.real, part.imag)], axis=0)
    waves = np.exp(1j * STEP * np.outer(lags, bins)) @ part_basis
    waves = waves * np.exp(1j * STEP * mid_bin * lags)[:, None] / math.sqrt(NF)
    expand = real_form(waves)
    halves = np.split(compress, 2 * CHIP_BINS // BINS, axis=1)
    by_core = []
    for core in range(2):
        own, twin = core, 1 - core
        ordered = [halves[own], halves[2 + own], halves[twin], halves[2 + twin]]
        by_core.append(np.concatenate(split_rounded(np.concatenate(ordered, axis=1)), axis=0))
    compress = np.stack(by_core)
    padded = np.zeros((2 * CB, 2 * LAG_PART), ml_dtypes.bfloat16)
    for index, half in enumerate(split_rounded(expand)):
        padded[index * CB : index * CB + ROWS_PART] = half.T
    expand = padded
    return compress, np.concatenate(split_rounded(combine), axis=0), expand


def magnitude_of(real, imag):
    real, imag = real.astype(jnp.float32), imag.astype(jnp.float32)
    return jnp.sqrt(real * real + imag * imag).astype(jnp.bfloat16)


def window_weights(core):
    shape = (BINS, 3 * BINS)
    row = lax.broadcasted_iota(jnp.int32, shape, 0)
    column = lax.broadcasted_iota(jnp.int32, shape, 1)
    place = column % BINS
    below = jnp.where(core == 0, BINS - 1 - column, column - 2 * BINS) >= 0
    ahead = jnp.where(below, place - row, row - place)
    centre = (column >= BINS) & (column < 2 * BINS)
    return jnp.where(centre | (ahead >= 0), 1.0, 0.0).astype(jnp.bfloat16)


def whiten(core, source, first, centre, second, white):
    chunk = 512
    weights = window_weights(core)
    for start in range(0, C, chunk):
        lanes = slice(start, start + chunk)
        sizes = jnp.concatenate([first[:, lanes], centre[:, lanes], second[:, lanes]], axis=0)
        sums = jnp.dot(weights, sizes, preferred_element_type=jnp.float32)
        inverse = 1.0 / (sums * (1.0 / (2 * SMOOTH + 1)) + 1e-05)
        for part in range(2):
            value = source[part, :, lanes].astype(jnp.float32) * inverse
            white[part, :, lanes] = value.astype(jnp.bfloat16)


def cross_of(blocks, base, white):
    crossed = []
    for slot in range(MAXB):
        left = pl.ds(pl.multiple_of(blocks[base + 2 * slot] * CB, CB), CB)
        right = pl.ds(pl.multiple_of(blocks[base + 2 * slot + 1] * CB, CB), CB)
        left_re = white[0, :, left].astype(jnp.float32)
        left_im = white[1, :, left].astype(jnp.float32)
        right_re = white[0, :, right].astype(jnp.float32)
        right_im = white[1, :, right].astype(jnp.float32)
        real = left_re * right_re + left_im * right_im
        imag = left_im * right_re - left_re * right_im
        crossed.append(jnp.concatenate([real, imag], axis=0).astype(jnp.bfloat16))
    return jnp.concatenate(crossed, axis=1)


def own_kernel(blocks, most, count, own, near, own_size, twin_size, out, white):
    core = blocks[CHIPS * 2 * MAXB]
    whiten(core, own, near, own_size, twin_size, white)
    for chip in range(CHIPS):
        out[chip] = cross_of(blocks, chip * 2 * MAXB, white)


def twin_kernel(
    blocks, compress, twin, own_size, twin_size, far, own_cross, out, white
):
    core = blocks[CHIPS * 2 * MAXB]
    whiten(core, twin, own_size, twin_size, far, white)
    weights = compress[core]
    for chip in range(CHIPS):
        twin_cross = cross_of(blocks, chip * 2 * MAXB, white)
        cross = jnp.concatenate([own_cross[chip], twin_cross], axis=0)
        packed = jnp.dot(weights, cross, preferred_element_type=jnp.float32)
        out[chip] = (packed[:ROWS_CHIP] + packed[ROWS_CHIP:]).astype(jnp.bfloat16)


def combine_kernel(table, packed, out):
    wide = out.shape[2]
    real = [packed[chip, :RANK_CHIP, :wide] for chip in range(CHIPS)]
    imag = [packed[chip, RANK_CHIP:, :wide] for chip in range(CHIPS)]
    value = jnp.concatenate([jnp.concatenate(real, axis=0), jnp.concatenate(imag, axis=0)], axis=1)
    total = jnp.dot(table[...], value, preferred_element_type=jnp.float32)
    half = table.shape[0] // 2
    total = total[:half] + total[half:]
    for part in range(HOURS // 2):
        base = part * ROWS_PART
        real_rows = slice(base, base + RANK_PART)
        imag_rows = slice(base + RANK_PART, base + ROWS_PART)
        real_real, real_imag = total[real_rows, :wide], total[real_rows, wide:]
        imag_real, imag_imag = total[imag_rows, :wide], total[imag_rows, wide:]
        for where, sign in ((part, 1.0), (HOURS - 1 - part, -1.0)):
            both = [real_real - sign * imag_imag, real_imag + sign * imag_real]
            out[where] = jnp.concatenate(both, axis=0).astype(jnp.bfloat16)


def stack_kernel(live, expand, parts, out, result, sems):
    blank = jnp.zeros((CB - ROWS_PART, CB), jnp.bfloat16)
    copies = []
    for slot in range(MAXB):
        lanes = slice(slot * CB, (slot + 1) * CB)
        rows = []
        for hour in range(HOURS):
            part = jnp.concatenate([parts[hour, :, lanes], blank], axis=0).T
            rows.append(jnp.concatenate([part, part], axis=1))
        lagged = jnp.dot(
            jnp.concatenate(rows, axis=0), expand[...], preferred_element_type=jnp.float32
        )
        linear = mean_real = mean_imag = None
        for hour in range(HOURS):
            correlation = lagged[hour * CB : (hour + 1) * CB, :LAG_PART]
            quadrature = lagged[hour * CB : (hour + 1) * CB, LAG_PART:]
            power = correlation * correlation + quadrature * quadrature
            inverse = jnp.minimum(lax.rsqrt(power), 1.0 / amp_floor)
            unit_real = correlation * inverse
            unit_imag = quadrature * inverse
            if hour == 0:
                linear, mean_real, mean_imag = correlation, unit_real, unit_imag
            else:
                linear = linear + correlation
                mean_real = mean_real + unit_real
                mean_imag = mean_imag + unit_imag
        stacked = linear * (mean_real * mean_real + mean_imag * mean_imag) * (1.0 / HOURS**3)
        result[slot] = jnp.where(live[slot] > 0, stacked, jnp.zeros_like(stacked))
        copy = pltpu.make_async_copy(result.at[slot], out.at[slot], sems.at[slot])
        copy.start()
        copies.append(copy)
    for copy in copies:
        copy.wait()


def on_device(spectra, pair_blocks, block_count):
    owner = lax.axis_index("pairs")
    core = owner % 2
    compress, combine, expand = tables()
    spectra = spectra[:, 0]
    twins = [(i, i ^ 1) for i in range(OWNERS)]
    twin = lax.ppermute(spectra, "pairs", twins)
    own_size = magnitude_of(spectra[0], spectra[1])
    last = OWNERS - 1
    near_pairs = [(i, i + 1) for i in range(1, last, 2)] + [(i, i - 1) for i in range(2, last, 2)]
    near = lax.ppermute(own_size, "pairs", near_pairs)
    twin_size = magnitude_of(twin[0], twin[1])
    slots = lax.dynamic_index_in_dim(
        pair_blocks.reshape(CHIPS, 2, 2 * MAXB), core, 1, keepdims=False
    )
    slots = jnp.concatenate([slots.reshape(-1), core[None]])
    count = lax.dynamic_index_in_dim(block_count, owner, 0, keepdims=False)
    live = (lax.broadcasted_iota(jnp.int32, (MAXB, 1, 1), 0) < count).astype(jnp.float32)
    most = jnp.max(jnp.where(lax.iota(jnp.int32, OWNERS) % 2 == core, block_count, 0))
    first, last_live = jnp.int32(0), jnp.int32(MAXB - 1)
    branches = [lax.clamp(first, value - 1, last_live) for value in (most, count)]
    near, twin_size, slots, live, *branches = lax.optimization_barrier(
        (near, twin_size, slots, live, *branches)
    )
    far = lax.ppermute(near, "pairs", twins)
    vmem = pl.BlockSpec(memory_space=pltpu.VMEM)
    smem = pl.BlockSpec(memory_space=pltpu.SMEM)
    limit = pltpu.CompilerParams(vmem_limit_bytes=32 * 2**20)
    combine = lax.optimization_barrier(jnp.asarray(combine))
    white = pltpu.VMEM((2, BINS, C), jnp.bfloat16)
    own_cross = pl.pallas_call(
        own_kernel,
        out_shape=jax.ShapeDtypeStruct((CHIPS, 2 * BINS, MAXB * CB), jnp.bfloat16),
        in_specs=[smem] * 3 + [vmem] * 4,
        out_specs=vmem,
        scratch_shapes=[white],
        compiler_params=limit,
        name="own_cross",
    )(slots, *(branch[None] for branch in branches), spectra, near, own_size, twin_size)
    packed = pl.pallas_call(
        twin_kernel,
        out_shape=jax.ShapeDtypeStruct((CHIPS, ROWS_CHIP, MAXB * CB), jnp.bfloat16),
        in_specs=[smem] + [vmem] * 6,
        out_specs=vmem,
        scratch_shapes=[white],
        compiler_params=limit,
        name="twin_cross",
    )(slots, compress, twin, own_size, twin_size, far, own_cross)
    groups = [list(range(0, OWNERS, 2)), list(range(1, OWNERS, 2))]

    def widen(parts, slots):
        return jnp.pad(parts, ((0, 0), (0, 0), (0, (MAXB - slots) * CB)))

    def between_chips(slots):
        def exchange(packed):
            packed = lax.all_to_all(
                packed[:, :, : slots * CB], "pairs", 0, 0, axis_index_groups=groups, tiled=True
            )
            return widen(packed, slots)

        return exchange

    packed = lax.switch(most - 1, [between_chips(slots) for slots in range(1, MAXB + 1)], packed)

    def with_live(live):
        def exchange(packed, combine):
            parts = pl.pallas_call(
                combine_kernel,
                out_shape=jax.ShapeDtypeStruct((HOURS, ROWS_PART, live * CB), jnp.bfloat16),
                in_specs=[vmem] * 2,
                out_specs=vmem,
                compiler_params=limit,
                name=f"combine_{live}",
            )(combine, packed)
            parts = lax.all_to_all(parts, "tm", 0, 0, tiled=True)
            return widen(parts, live)

        return exchange

    parts = lax.switch(
        count - 1, [with_live(live) for live in range(1, MAXB + 1)], packed, combine
    )
    return pl.pallas_call(
        stack_kernel,
        out_shape=jax.ShapeDtypeStruct((MAXB, CB, LAG_PART), jnp.float32),
        in_specs=[vmem] * 3,
        out_specs=pl.BlockSpec(memory_space=pl.ANY),
        scratch_shapes=[
            pltpu.VMEM((MAXB, CB, LAG_PART), jnp.float32),
            pltpu.SemaphoreType.DMA((MAXB,)),
        ],
        compiler_params=limit,
        name="stack",
    )(live, expand, parts)


def solution(mesh):
    return jax.shard_map(
        on_device,
        mesh=mesh,
        in_specs=(P(None, "tm", "pairs", None), P(), P()),
        out_specs=P("pairs", None, "tm"),
        check_vma=False,
    )
```

```python
import functools
import math

import jax
import jax.numpy as jnp
import ml_dtypes
import numpy as np
from jax import lax
from jax.experimental import pallas as pl
from jax.experimental.pallas import tpu as pltpu
from jax.sharding import PartitionSpec as P

C = 4096
CB = 128
NF = 1024
FIRST_BIN = 16
FFT_LEN = 8192
LAGS = 2048
SMOOTH = 32
MAXB = 4
HOURS = 8
OWNERS = 32
amp_floor = 0.2

CHIPS = OWNERS // 2
BINS = NF // OWNERS
CHIP_BINS = 2 * BINS
LAG_PART = LAGS // HOURS
RANK_CHIP = 28
RANK_PART = 48
ROWS_CHIP = 2 * RANK_CHIP
ROWS_PART = 2 * RANK_PART
STEP = 2.0 * math.pi / FFT_LEN


def slepian(points, half_width, count):
    n = np.arange(points, dtype=np.float64)
    tri = np.diag(((points - 1) / 2.0 - n) ** 2 * math.cos(2.0 * math.pi * half_width))
    off = n[1:] * (points - n[1:]) / 2.0
    tri = tri + np.diag(off, 1) + np.diag(off, -1)
    vectors = np.linalg.eigh(tri)[1][:, ::-1][:, :count]
    return vectors * np.where(vectors[points // 2] < 0, -1.0, 1.0)


def split_rounded(table):
    high = table.astype(ml_dtypes.bfloat16)
    low = (table - high.astype(np.float64)).astype(ml_dtypes.bfloat16)
    return high, low


def real_form(table):
    return np.block([[table.real, -table.imag], [table.imag, table.real]])


@functools.cache
def tables():
    chip_basis = slepian(CHIP_BINS, (LAGS / 2 + 4) / FFT_LEN, RANK_CHIP)
    part_basis = slepian(NF, (LAG_PART / 2 + 0.5) / FFT_LEN, RANK_PART)
    bins = np.arange(NF) - (NF - 1) / 2.0
    lags = np.arange(LAG_PART) - LAG_PART // 2
    mid_bin = FIRST_BIN + (NF - 1) / 2.0
    compress = np.kron(np.eye(2), chip_basis.T)
    parts = []
    for part in range(HOURS // 2):
        mid_lag = LAG_PART * part - (LAGS - LAG_PART) // 2
        turned = np.exp(1j * STEP * (bins + mid_bin) * mid_lag)[:, None] * part_basis
        turned = turned.reshape(CHIPS, CHIP_BINS, RANK_PART)
        blocks = [(chip_basis.T @ turned[chip]).T for chip in range(CHIPS)]
        parts.append(np.concatenate(blocks, axis=1))
    combine = np.concatenate([half for part in parts for half in (part.real, part.imag)], axis=0)
    waves = np.exp(1j * STEP * np.outer(lags, bins)) @ part_basis
    waves = waves * np.exp(1j * STEP * mid_bin * lags)[:, None] / math.sqrt(NF)
    expand = real_form(waves)
    row = np.arange(BINS)[:, None] + SMOOTH
    column = np.arange(BINS + 2 * SMOOTH)[None, :]
    window = (np.abs(row - column) <= SMOOTH).astype(ml_dtypes.bfloat16)
    turned = [window[:, -SMOOTH:], window[:, SMOOTH:-SMOOTH], window[:, :SMOOTH]]
    window = np.stack([window, np.concatenate(turned, axis=1)])
    halves = np.split(compress, 2 * CHIP_BINS // BINS, axis=1)
    by_core = []
    for core in range(2):
        own, twin = core, 1 - core
        ordered = [halves[own], halves[2 + own], halves[twin], halves[2 + twin]]
        by_core.append(np.concatenate(split_rounded(np.concatenate(ordered, axis=1)), axis=0))
    compress = np.stack(by_core)
    padded = np.zeros((2 * CB, 2 * LAG_PART), ml_dtypes.bfloat16)
    for index, half in enumerate(split_rounded(expand)):
        padded[index * CB : index * CB + ROWS_PART] = half.T
    expand = padded
    return window, compress, np.concatenate(split_rounded(combine), axis=0), expand


def magnitude_of(real, imag):
    real, imag = real.astype(jnp.float32), imag.astype(jnp.float32)
    return jnp.sqrt(real * real + imag * imag).astype(jnp.bfloat16)


def whiten(core, window, source, first, centre, second, white):
    chunk = 2048
    weights = window[core]
    for start in range(0, C, chunk):
        lanes = slice(start, start + chunk)
        sizes = jnp.concatenate([first[:, lanes], centre[:, lanes], second[:, lanes]], axis=0)
        sums = jnp.dot(weights, sizes, preferred_element_type=jnp.float32)
        inverse = 1.0 / (sums * (1.0 / (2 * SMOOTH + 1)) + 1e-05)
        for part in range(2):
            value = source[part, :, lanes].astype(jnp.float32) * inverse
            white[part, :, lanes] = value.astype(jnp.bfloat16)


def cross_of(blocks, base, white):
    crossed = []
    for slot in range(MAXB):
        left = pl.ds(pl.multiple_of(blocks[base + 2 * slot] * CB, CB), CB)
        right = pl.ds(pl.multiple_of(blocks[base + 2 * slot + 1] * CB, CB), CB)
        left_re = white[0, :, left].astype(jnp.float32)
        left_im = white[1, :, left].astype(jnp.float32)
        right_re = white[0, :, right].astype(jnp.float32)
        right_im = white[1, :, right].astype(jnp.float32)
        real = left_re * right_re + left_im * right_im
        imag = left_im * right_re - left_re * right_im
        crossed.append(jnp.concatenate([real, imag], axis=0).astype(jnp.bfloat16))
    return jnp.concatenate(crossed, axis=1)


def own_kernel(blocks, most, count, window, own, near, own_size, twin_size, out, white):
    core = blocks[CHIPS * 2 * MAXB]
    whiten(core, window, own, near, own_size, twin_size, white)
    for chip in range(CHIPS):
        out[chip] = cross_of(blocks, chip * 2 * MAXB, white)


def twin_kernel(
    blocks, window, compress, twin, own_size, twin_size, far, own_cross, out, white
):
    core = blocks[CHIPS * 2 * MAXB]
    whiten(core, window, twin, own_size, twin_size, far, white)
    weights = compress[core]
    for chip in range(CHIPS):
        twin_cross = cross_of(blocks, chip * 2 * MAXB, white)
        cross = jnp.concatenate([own_cross[chip], twin_cross], axis=0)
        packed = jnp.dot(weights, cross, preferred_element_type=jnp.float32)
        out[chip] = (packed[:ROWS_CHIP] + packed[ROWS_CHIP:]).astype(jnp.bfloat16)


def combine_kernel(table, packed, out):
    wide = out.shape[2]
    real = [packed[chip, :RANK_CHIP, :wide] for chip in range(CHIPS)]
    imag = [packed[chip, RANK_CHIP:, :wide] for chip in range(CHIPS)]
    value = jnp.concatenate([jnp.concatenate(real, axis=0), jnp.concatenate(imag, axis=0)], axis=1)
    total = jnp.dot(table[...], value, preferred_element_type=jnp.float32)
    half = table.shape[0] // 2
    total = total[:half] + total[half:]
    for part in range(HOURS // 2):
        base = part * ROWS_PART
        real_rows = slice(base, base + RANK_PART)
        imag_rows = slice(base + RANK_PART, base + ROWS_PART)
        real_real, real_imag = total[real_rows, :wide], total[real_rows, wide:]
        imag_real, imag_imag = total[imag_rows, :wide], total[imag_rows, wide:]
        for where, sign in ((part, 1.0), (HOURS - 1 - part, -1.0)):
            both = [real_real - sign * imag_imag, real_imag + sign * imag_real]
            out[where] = jnp.concatenate(both, axis=0).astype(jnp.bfloat16)


def stack_kernel(live, expand, parts, out, result, sems):
    blank = jnp.zeros((CB - ROWS_PART, CB), jnp.bfloat16)
    copies = []
    for slot in range(MAXB):
        lanes = slice(slot * CB, (slot + 1) * CB)
        rows = []
        for hour in range(HOURS):
            part = jnp.concatenate([parts[hour, :, lanes], blank], axis=0).T
            rows.append(jnp.concatenate([part, part], axis=1))
        lagged = jnp.dot(
            jnp.concatenate(rows, axis=0), expand[...], preferred_element_type=jnp.float32
        )
        linear = mean_real = mean_imag = None
        for hour in range(HOURS):
            correlation = lagged[hour * CB : (hour + 1) * CB, :LAG_PART]
            quadrature = lagged[hour * CB : (hour + 1) * CB, LAG_PART:]
            power = correlation * correlation + quadrature * quadrature
            inverse = jnp.minimum(lax.rsqrt(power), 1.0 / amp_floor)
            unit_real = correlation * inverse
            unit_imag = quadrature * inverse
            if hour == 0:
                linear, mean_real, mean_imag = correlation, unit_real, unit_imag
            else:
                linear = linear + correlation
                mean_real = mean_real + unit_real
                mean_imag = mean_imag + unit_imag
        stacked = linear * (mean_real * mean_real + mean_imag * mean_imag) * (1.0 / HOURS**3)
        result[slot] = jnp.where(live[slot] > 0, stacked, jnp.zeros_like(stacked))
        copy = pltpu.make_async_copy(result.at[slot], out.at[slot], sems.at[slot])
        copy.start()
        copies.append(copy)
    for copy in copies:
        copy.wait()


def on_device(spectra, pair_blocks, block_count):
    owner = lax.axis_index("pairs")
    core = owner % 2
    window, compress, combine, expand = tables()
    spectra = spectra[:, 0]
    twins = [(i, i ^ 1) for i in range(OWNERS)]
    twin = lax.ppermute(spectra, "pairs", twins)
    own_size = magnitude_of(spectra[0], spectra[1])
    last = OWNERS - 1
    near_pairs = [(i, i + 1) for i in range(1, last, 2)] + [(i, i - 1) for i in range(2, last, 2)]
    near = lax.ppermute(own_size, "pairs", near_pairs)
    twin_size = magnitude_of(twin[0], twin[1])
    slots = lax.dynamic_index_in_dim(
        pair_blocks.reshape(CHIPS, 2, 2 * MAXB), core, 1, keepdims=False
    )
    slots = jnp.concatenate([slots.reshape(-1), core[None]])
    count = lax.dynamic_index_in_dim(block_count, owner, 0, keepdims=False)
    live = (lax.broadcasted_iota(jnp.int32, (MAXB, 1, 1), 0) < count).astype(jnp.float32)
    most = jnp.max(jnp.where(lax.iota(jnp.int32, OWNERS) % 2 == core, block_count, 0))
    first, last_live = jnp.int32(0), jnp.int32(MAXB - 1)
    branches = [lax.clamp(first, value - 1, last_live) for value in (most, count)]
    near, twin_size, slots, live, *branches = lax.optimization_barrier(
        (near, twin_size, slots, live, *branches)
    )
    far = lax.ppermute(near, "pairs", twins)
    vmem = pl.BlockSpec(memory_space=pltpu.VMEM)
    smem = pl.BlockSpec(memory_space=pltpu.SMEM)
    limit = pltpu.CompilerParams(vmem_limit_bytes=32 * 2**20)
    combine = lax.optimization_barrier(jnp.asarray(combine))
    white = pltpu.VMEM((2, BINS, C), jnp.bfloat16)
    own_cross = pl.pallas_call(
        own_kernel,
        out_shape=jax.ShapeDtypeStruct((CHIPS, 2 * BINS, MAXB * CB), jnp.bfloat16),
        in_specs=[smem] * 3 + [vmem] * 5,
        out_specs=vmem,
        scratch_shapes=[white],
        compiler_params=limit,
        name="own_cross",
    )(slots, *(branch[None] for branch in branches), window, spectra, near, own_size, twin_size)
    packed = pl.pallas_call(
        twin_kernel,
        out_shape=jax.ShapeDtypeStruct((CHIPS, ROWS_CHIP, MAXB * CB), jnp.bfloat16),
        in_specs=[smem] + [vmem] * 7,
        out_specs=vmem,
        scratch_shapes=[white],
        compiler_params=limit,
        name="twin_cross",
    )(slots, window, compress, twin, own_size, twin_size, far, own_cross)
    groups = [list(range(0, OWNERS, 2)), list(range(1, OWNERS, 2))]

    def widen(parts, slots):
        return jnp.pad(parts, ((0, 0), (0, 0), (0, (MAXB - slots) * CB)))

    def between_chips(slots):
        def exchange(packed):
            packed = lax.all_to_all(
                packed[:, :, : slots * CB], "pairs", 0, 0, axis_index_groups=groups, tiled=True
            )
            return widen(packed, slots)

        return exchange

    packed = lax.switch(most - 1, [between_chips(slots) for slots in range(1, MAXB + 1)], packed)

    def with_live(live):
        def exchange(packed, combine):
            parts = pl.pallas_call(
                combine_kernel,
                out_shape=jax.ShapeDtypeStruct((HOURS, ROWS_PART, live * CB), jnp.bfloat16),
                in_specs=[vmem] * 2,
                out_specs=vmem,
                compiler_params=limit,
                name=f"combine_{live}",
            )(combine, packed)
            parts = lax.all_to_all(parts, "tm", 0, 0, tiled=True)
            return widen(parts, live)

        return exchange

    parts = lax.switch(
        count - 1, [with_live(live) for live in range(1, MAXB + 1)], packed, combine
    )
    return pl.pallas_call(
        stack_kernel,
        out_shape=jax.ShapeDtypeStruct((MAXB, CB, LAG_PART), jnp.float32),
        in_specs=[vmem] * 3,
        out_specs=pl.BlockSpec(memory_space=pl.ANY),
        scratch_shapes=[
            pltpu.VMEM((MAXB, CB, LAG_PART), jnp.float32),
            pltpu.SemaphoreType.DMA((MAXB,)),
        ],
        compiler_params=limit,
        name="stack",
    )(live, expand, parts)


def solution(mesh):
    return jax.shard_map(
        on_device,
        mesh=mesh,
        in_specs=(P(None, "tm", "pairs", None), P(), P()),
        out_specs=P("pairs", None, "tm"),
        check_vma=False,
    )
```
